32 devices in a mesh: blk: 8 (over z, x), lon: 4 (over y, core).
Axes of the slice: x: 2, y: 2, z: 4, core: 2. Of those that a mesh axis runs over, the one named last changes fastest.
Arguments:
- nodes: float32 [64, 256, 512], P(None, 'blk', 'lon'), may hold values from -6 to 6
- edges: float32 [64, 6, 256, 512], P(None, None, 'blk', 'lon'), may hold values from -6 to 6
- latent_mean: float32 [64, 256, 512], P(None, 'blk', 'lon'), may hold values from -3 to 3
- latent_logstd: float32 [64, 256, 512], P(None, 'blk', 'lon'), may hold values from -1 to 0
- latent_noise: float32 [64, 256, 512], P(None, 'blk', 'lon'), may hold values from -6 to 6
- kl_weight: float32 [1], replicated, may hold values from 0.5 to 2
- band_counts: int32 [8], replicated, may hold values from 32 to 128, as said below
- neighbors: int32 [6, 256, 512], P(None, 'blk', 'lon'), may hold values from 0 to 4419, as said below
- edge_mask: int32 [6, 256, 512], P(None, 'blk', 'lon'), may hold values 0 or 1
- w_edge_in: float32 [64, 192], replicated, may hold values from -0.4375 to 0.4375
- b_edge_in: float32 [64], replicated, may hold values from -3 to 3
- w_edge_out: float32 [64, 64], replicated, may hold values from -0.75 to 0.75
- b_edge_out: float32 [64], replicated, may hold values from -3 to 3
- edge_gain: float32 [64], replicated, may hold values from 0.5 to 1.5
- edge_shift: float32 [64], replicated, may hold values from -3 to 3
- w_node_in: float32 [64, 128], replicated, may hold values from -0.5 to 0.5
- b_node_in: float32 [64], replicated, may hold values from -3 to 3
- w_node_out: float32 [64, 64], replicated, may hold values from -0.75 to 0.75
- b_node_out: float32 [64], replicated, may hold values from -3 to 3
- node_gain: float32 [64], replicated, may hold values from 0.5 to 1.5
- node_shift: float32 [64], replicated, may hold values from -3 to 3
- cotangent: float32 [64, 256, 512], P(None, 'blk', 'lon'), may hold values from -6 to 6
Outputs:
- new_states: float32 [64, 256, 512], P(None, 'blk', 'lon')
- kl_value: float32 [1], replicated
- grad_nodes: float32 [64, 256, 512], P(None, 'blk', 'lon')
- grad_edges: float32 [64, 6, 256, 512], P(None, None, 'blk', 'lon')
- grad_mean: float32 [64, 256, 512], P(None, 'blk', 'lon')
- grad_logstd: float32 [64, 256, 512], P(None, 'blk', 'lon')
- grad_w_edge_in: float32 [64, 192], replicated
- grad_b_edge_in: float32 [64], replicated
- grad_w_edge_out: float32 [64, 64], replicated
- grad_b_edge_out: float32 [64], replicated
- grad_edge_gain: float32 [64], replicated
- grad_edge_shift: float32 [64], replicated
- grad_w_node_in: float32 [64, 128], replicated
- grad_b_node_in: float32 [64], replicated
- grad_w_node_out: float32 [64, 64], replicated
- grad_b_node_out: float32 [64], replicated
- grad_node_gain: float32 [64], replicated
- grad_node_shift: float32 [64], replicated
The draws below stay inside these ranges and needn't reach their ends.
Inputs may be any that keep to these rules, and one draw needn't show every extreme that they name: `band_counts`: band 8 // 2 holds 128 valid nodes a row and band 0 holds 32; the end bands hold fewer than the middle ones. `neighbors`: the entry for receiver at local row r and column c is er * 130 + ec, naming one of the eight cells around (r + 1, c + 1) in the device's block extended by one cell on every side.
All inputs are finite; a program needn't handle non-finite values. No bound on the sum of `edge_mask` on one device may be relied on, other than what follows from the above.
Results may differ from the reference program's by a relative error of at most 0.0003.
Values sent between devices are 32-bit elements; how exact they have to be, the bound alone decides.
A program may use at most 192 MiB of HBM per device.

```python
import math
import jax
import jax.numpy as jnp
from jax import lax

D = 64
NBR = 6
ROWS_DEV = 32
COLS_DEV = 128
BANDS = 8
NROWS = 256
NCOLS = 512


def draw_band_counts(key, part):
    key = jax.random.fold_in(key, 11)
    middle = BANDS // 2
    half_span = max(BANDS // 2, 1)
    band_ids = jnp.arange(BANDS, dtype=jnp.int32)
    distance = jnp.abs(band_ids - middle)
    shrink = distance * COLS_DEV * 3 // (4 * half_span)
    jitter = jax.random.randint(key, (BANDS,), 0, COLS_DEV // 8 + 1)
    values = jnp.maximum(COLS_DEV // 4, COLS_DEV - shrink - jitter)
    return jnp.where(band_ids == middle, COLS_DEV, values).astype(jnp.int32)


def draw_neighbors(key, part):
    key = jax.random.fold_in(key, 7)
    pick = jax.random.randint(key, (NBR, NROWS, NCOLS), 0, 8)
    local_row = (jnp.arange(NROWS, dtype=jnp.int32) % ROWS_DEV)[None, :, None]
    local_col = (jnp.arange(NCOLS, dtype=jnp.int32) % COLS_DEV)[None, None, :]
    slot_ids = jnp.arange(NBR, dtype=jnp.int32)[:, None, None]
    first_corner = (slot_ids == 0) & (local_row == 0) & (local_col == 0)
    last_corner = (slot_ids == 0) & (local_row == ROWS_DEV - 1) & (local_col == COLS_DEV - 1)
    pick = jnp.where(first_corner, 0, jnp.where(last_corner, 7, pick))
    cell = pick + (pick >= 4).astype(jnp.int32)
    row_step = cell // 3 - 1
    col_step = cell % 3 - 1
    flat = (local_row + 1 + row_step) * (COLS_DEV + 2) + local_col + 1 + col_step
    return flat.astype(jnp.int32)


def with_ends(values, key, least, top_value):
    longest = values.shape.index(max(values.shape))
    spots = []
    for shift in (0, 1):
        where = [jax.random.randint(jax.random.fold_in(key, axis), (), 0, length) for axis, length in enumerate(values.shape)]
        where[longest] = (where[longest] + shift) % values.shape[longest]
        spots.append(tuple(where))
    return values.at[spots[0]].set(least).at[spots[1]].set(top_value)


def shard_levels(rng, dims, shards, low, top_value):
    level, own = 1.0, jax.random.fold_in(rng, 6)
    for axis_at, blocks in shards:
        heights = jnp.exp(jax.random.uniform(jax.random.fold_in(own, axis_at), (blocks,), jnp.float32, low / len(shards), top_value / len(shards)))
        level = level * jnp.repeat(heights, dims[axis_at] // blocks).reshape([-1 if axis == axis_at else 1 for axis in range(len(dims))])
    return level


def scatter_about(own_key, extent, scale, limit, cuts=(), kind=jnp.bfloat16):
    result = jax.random.normal(own_key, extent, jnp.float32) * scale
    if len(cuts) > 0:
        result = shard_levels(own_key, extent, cuts, -0.22, 0.18) * result
    return jnp.clip(result, min=-limit, max=limit).astype(kind)


def setup_inputs(seed: int = 0) -> dict:
    key_list = jax.random.split(jax.random.key(seed), 23)
    nodes = scatter_about(key_list[0], (D, NROWS, NCOLS), 1.0, 6.0, ((1, 8), (2, 4)), jnp.float32)
    edges = scatter_about(key_list[1], (D, NBR, NROWS, NCOLS), 1.0, 6.0, ((2, 8), (3, 4)), jnp.float32)
    latent_mean = scatter_about(key_list[2], (D, NROWS, NCOLS), 0.5, 3.0, ((1, 8), (2, 4)), jnp.float32)
    latent_logstd = jnp.clip(-1.0 + 1.0 * jax.random.uniform(key_list[3], (D, NROWS, NCOLS), jnp.float32) ** shard_levels(key_list[3], (D, NROWS, NCOLS), ((1, 8), (2, 4)), -0.2, 0.2), -1.0, 0.0)
    latent_noise = scatter_about(key_list[4], (D, NROWS, NCOLS), 1.0, 6.0, ((1, 8), (2, 4)), jnp.float32)
    kl_weight = jnp.clip(jnp.exp(jax.random.uniform(key_list[5], (1,), jnp.float32, math.log(0.5), math.log(2.0))), 0.5, 2.0)
    band_counts = draw_band_counts(jax.random.fold_in(key_list[22], 71), 0)
    neighbors = draw_neighbors(jax.random.fold_in(key_list[22], 71), 0)
    edge_mask = with_ends((jax.random.randint(key_list[8], (NBR, NROWS, NCOLS), 0, 4) < 3).astype(jnp.int32), jax.random.fold_in(key_list[8], 1), 0, 1)
    w_edge_in = scatter_about(key_list[9], (D, 3 * D), (3 * D) ** -0.5, 0.4375, (), jnp.float32)
    b_edge_in = scatter_about(key_list[10], (D,), 0.5, 3.0, (), jnp.float32)
    w_edge_out = scatter_about(key_list[11], (D, D), D ** -0.5, 0.75, (), jnp.float32)
    b_edge_out = scatter_about(key_list[12], (D,), 0.5, 3.0, (), jnp.float32)
    edge_gain = jnp.clip(1.0 + 0.1 * jax.random.normal(key_list[13], (D,), jnp.float32), 0.5, 1.5)
    edge_shift = scatter_about(key_list[14], (D,), 0.5, 3.0, (), jnp.float32)
    w_node_in = scatter_about(key_list[15], (D, 2 * D), (2 * D) ** -0.5, 0.5, (), jnp.float32)
    b_node_in = scatter_about(key_list[16], (D,), 0.5, 3.0, (), jnp.float32)
    w_node_out = scatter_about(key_list[17], (D, D), D ** -0.5, 0.75, (), jnp.float32)
    b_node_out = scatter_about(key_list[18], (D,), 0.5, 3.0, (), jnp.float32)
    node_gain = jnp.clip(1.0 + 0.1 * jax.random.normal(key_list[19], (D,), jnp.float32), 0.5, 1.5)
    node_shift = scatter_about(key_list[20], (D,), 0.5, 3.0, (), jnp.float32)
    cotangent = scatter_about(key_list[21], (D, NROWS, NCOLS), 1.0, 6.0, ((1, 8), (2, 4)), jnp.float32)
    return dict(nodes=nodes, edges=edges, latent_mean=latent_mean, latent_logstd=latent_logstd, latent_noise=latent_noise, kl_weight=kl_weight, band_counts=band_counts, neighbors=neighbors, edge_mask=edge_mask, w_edge_in=w_edge_in, b_edge_in=b_edge_in, w_edge_out=w_edge_out, b_edge_out=b_edge_out, edge_gain=edge_gain, edge_shift=edge_shift, w_node_in=w_node_in, b_node_in=b_node_in, w_node_out=w_node_out, b_node_out=b_node_out, node_gain=node_gain, node_shift=node_shift, cotangent=cotangent)


@jax.custom_vjp
def low(v):
    return lax.optimization_barrier(v.astype(jnp.bfloat16)).astype(jnp.float32)

@jax.custom_vjp
def low_back(v):
    return v

def low_keep(v):
    return (low(v), None)

def low_pass(kept, grad):
    return (grad,)

def back_keep(v):
    return (v, None)

def back_low(kept, grad):
    return (low(grad),)
low.defvjp(low_keep, low_pass)
low_back.defvjp(back_keep, back_low)

def matmul(left, right):
    return jnp.dot(left, right, precision=lax.Precision.HIGHEST, preferred_element_type=jnp.float32)

def layer_norm(pre, gain, shift):
    centred = pre - lax.optimization_barrier(jnp.mean(pre, axis=0, keepdims=True))
    variance = lax.optimization_barrier(jnp.mean(centred * centred, axis=0, keepdims=True))
    return centred * lax.rsqrt(variance + 1e-05) * gain[:, None] + shift[:, None]

def reference(nodes, edges, latent_mean, latent_logstd, latent_noise, kl_weight, band_counts, neighbors, edge_mask, w_edge_in, b_edge_in, w_edge_out, b_edge_out, edge_gain, edge_shift, w_node_in, b_node_in, w_node_out, b_node_out, node_gain, node_shift, cotangent):
    width = D
    row_ids = jnp.arange(NROWS, dtype=jnp.int32)
    col_ids = jnp.arange(NCOLS, dtype=jnp.int32)
    band_of = row_ids // ROWS_DEV
    row_count = band_counts[band_of]
    node_valid = (col_ids[None, :] % COLS_DEV < row_count[:, None]).astype(jnp.float32)
    ext_row = neighbors // (COLS_DEV + 2)
    ext_col = neighbors % (COLS_DEV + 2)
    src_row = (band_of[None, :, None] * ROWS_DEV + ext_row - 1) % NROWS
    src_col = (col_ids[None, None, :] // COLS_DEV * COLS_DEV + ext_col - 1) % NCOLS
    source = (src_row * NCOLS + src_col).astype(jnp.int32)
    edge_valid = edge_mask.astype(jnp.float32) * node_valid[None] * node_valid.reshape(-1)[source]

    def bands_first(array, axis_rows):
        shape = array.shape
        split = shape[:axis_rows] + (BANDS, ROWS_DEV) + shape[axis_rows + 1:]
        return jnp.moveaxis(array.reshape(split), axis_rows, 0)
    source_bands = bands_first(source, 1)
    valid_bands = bands_first(edge_valid, 1)

    def forward(nodes_f, edges_f, mean_f, logstd_f, wei, bei, weo, beo, egain, eshift, wni, bni, wno, bno, ngain, nshift):
        spread = jnp.exp(logstd_f)
        state = nodes_f + mean_f + spread * latent_noise
        state_flat = state.reshape(width, -1)
        state_bands = bands_first(state, 1)
        edge_stack = bands_first(edges_f, 2)

        def band_fn(item):
            edge_part, src_part, valid_part, recv_part = item
            senders = jnp.take(state_flat, src_part.reshape(-1), axis=1)
            receivers = jnp.broadcast_to(recv_part[:, None], edge_part.shape).reshape(width, -1)
            stacked = jnp.concatenate([edge_part.reshape(width, -1), senders, receivers], axis=0)
            hidden = jax.nn.silu(matmul(wei, stacked) + bei[:, None])
            message = layer_norm(matmul(weo, hidden) + beo[:, None], egain, eshift)
            return lax.optimization_barrier(jnp.sum(message.reshape(edge_part.shape) * valid_part[None], axis=1))
        incoming_bands = lax.map(jax.checkpoint(band_fn), (edge_stack, source_bands, valid_bands, state_bands))
        incoming = jnp.moveaxis(incoming_bands, 0, 1).reshape(width, NROWS, NCOLS)
        node_input = jnp.concatenate([state, incoming], axis=0).reshape(2 * width, -1)
        node_hidden = jax.nn.silu(matmul(wni, node_input) + bni[:, None])
        update = layer_norm(matmul(wno, node_hidden) + bno[:, None], ngain, nshift)
        new_states = state + update.reshape(state.shape)
        divergence = 0.5 * jnp.sum(node_valid[None] * (mean_f * mean_f + spread * spread - 1.0 - 2.0 * logstd_f))
        return (new_states, divergence)
    outputs, pullback = jax.vjp(forward, nodes, edges, latent_mean, latent_logstd, w_edge_in, b_edge_in, w_edge_out, b_edge_out, edge_gain, edge_shift, w_node_in, b_node_in, w_node_out, b_node_out, node_gain, node_shift)
    new_states, divergence = outputs
    grads = pullback((cotangent, kl_weight[0]))
    kl_value = (divergence / (width * jnp.sum(node_valid))).reshape(1)
    return (new_states, kl_value, grads[0], grads[1], grads[2], grads[3], grads[4], grads[5], grads[6], grads[7], grads[8], grads[9], grads[10], grads[11], grads[12], grads[13], grads[14], grads[15])
```

```python
import functools

import jax
import jax.numpy as jnp
from jax import lax
from jax.experimental import pallas as pl
from jax.experimental.pallas import tpu as pltpu
from jax.sharding import PartitionSpec as P

F32 = jnp.float32
BF16 = jnp.bfloat16
MESH = pl.DeviceIdType.MESH
D = 64
LANES = 128
NBR = 6
EPS = 1e-05
HBM = pl.BlockSpec(memory_space=pltpu.HBM)
VMEM = pl.BlockSpec(memory_space=pltpu.VMEM)
SMEM = pl.BlockSpec(memory_space=pltpu.SMEM)

WINDOWS = ((-1, -1), (-1, 0), (-1, 1), (0, -1), (0, 1), (1, -1), (1, 0), (1, 1))


def halves(value):
    high = value.astype(BF16)
    return high, (value - high.astype(F32)).astype(BF16)


def weight_pack(weight, bias=None):
    high, low = halves(weight)
    if bias is None:
        return jnp.concatenate([high, high, low], axis=1)
    bias_high, bias_low = halves(bias)
    place = lax.broadcasted_iota(jnp.int32, (weight.shape[0], 16), 1)
    wide = jnp.where(
        place == 0, bias_high.astype(F32), jnp.where(place == 1, bias_low.astype(F32), 0.0)
    )
    return jnp.concatenate([high, high, wide.astype(BF16), low], axis=1)


def mxu(left, right):
    return jnp.dot(left, right, preferred_element_type=F32)


def outer(left, right):
    return lax.dot_general(
        left, right, (((1,), (1,)), ((), ())), preferred_element_type=F32
    )


def exact(left, right, dims):
    return lax.dot_general(
        left,
        right,
        (dims, ((), ())),
        precision=lax.Precision.HIGHEST,
        preferred_element_type=F32,
    )


def eye():
    return lax.broadcasted_iota(jnp.int32, (D, D), 0) == lax.broadcasted_iota(
        jnp.int32, (D, D), 1
    )


def to_column(row):
    return jnp.sum(jnp.where(eye(), row, 0.0), axis=1, keepdims=True)


def to_row(column):
    return jnp.sum(jnp.where(eye(), column, 0.0), axis=0, keepdims=True)


def lane_ids(rows=D):
    return lax.broadcasted_iota(jnp.int32, (rows, LANES), 1)


def halo_kernel(
    n_blk,
    n_lon,
    counts,
    nodes,
    mean,
    logstd,
    noise,
    w_ei,
    w_eo,
    w_ni,
    w_no,
    vectors,
    state,
    west_out,
    east_out,
    diverged,
    a_edge,
    a_state,
    a_hidden,
    a_edge_t,
    a_send_t,
    a_recv_t,
    a_node_in,
    a_node_out,
    a_node_out_t,
    a_node_in_t,
    columns,
    buf,
    tiles,
    landing,
    in_sem,
    send_sem,
    recv_sem,
):
    rows = nodes.shape[1]
    blk = lax.axis_index("blk")
    lon = lax.axis_index("lon")
    up = lax.rem(blk + n_blk - 1, n_blk)
    down = lax.rem(blk + 1, n_blk)
    west = lax.rem(lon + n_lon - 1, n_lon)
    east = lax.rem(lon + 1, n_lon)
    around = (
        (up, lon),
        (down, lon),
        (blk, west),
        (blk, east),
        (up, west),
        (up, east),
        (down, west),
        (down, east),
    )
    n_groups = in_sem.shape[0]
    group = rows // n_groups
    for g in range(n_groups):
        for r in range(g * group, (g + 1) * group):
            for which, source in enumerate((nodes, mean, logstd, noise)):
                pltpu.make_async_copy(
                    source.at[:, r, :], buf.at[r, which], in_sem.at[g]
                ).start()
    barrier = pltpu.get_barrier_semaphore()
    for place in around:
        pl.semaphore_signal(barrier, inc=1, device_id=place, device_id_type=MESH)

    lane = lane_ids()
    count = counts[blk]
    inside = lane < count
    total = jnp.zeros((D, LANES), F32)
    west_tile = jnp.zeros((D, LANES), F32)
    east_tile = jnp.zeros((D, LANES), F32)
    for g in range(n_groups):
        span = pl.ds(g * group, group)
        pltpu.make_async_copy(buf.at[span], buf.at[span], in_sem.at[g]).wait()
        for r in range(g * group, (g + 1) * group):
            mean_r = buf[r, 1]
            logstd_r = buf[r, 2]
            spread = jnp.exp(logstd_r)
            value = buf[r, 0] + mean_r + spread * buf[r, 3]
            state[r + 1] = value
            term = mean_r * mean_r + spread * spread - 1.0 - 2.0 * logstd_r
            total += jnp.where(inside, term, 0.0)
            moved = pltpu.roll(value, r + 1, 1)
            west_tile = jnp.where(lane == r + 1, moved, west_tile)
            east_tile = jnp.where(lane == r, moved, east_tile)
            if r == 0:
                tiles[0] = value
            if r == rows - 1:
                tiles[1] = value
    tiles[2] = west_tile
    tiles[3] = east_tile
    diverged[...] = jnp.broadcast_to(
        0.5 * jnp.sum(total, axis=1, keepdims=True), (D, LANES)
    )
    pl.semaphore_wait(barrier, 8)
    copies = []
    for slot, (place, tile) in enumerate(zip(around, (0, 1, 2, 3, 0, 0, 1, 1))):
        copies.append(
            pltpu.make_async_remote_copy(
                src_ref=tiles.at[tile],
                dst_ref=landing.at[slot],
                send_sem=send_sem.at[slot],
                recv_sem=recv_sem.at[slot],
                device_id=place,
                device_id_type=MESH,
            )
        )
        copies[-1].start()

    rows_of = [vectors[i] for i in range(8)]
    b_ei, b_eo, gain_e, shift_e, b_ni, b_no, gain_n, shift_n = [
        to_column(row) for row in rows_of
    ]
    for i, column in enumerate((0.5 * b_ei, gain_e, shift_e, 0.5 * b_ni, gain_n, shift_n)):
        columns[i] = jnp.broadcast_to(column, (D, LANES))
    w_in = w_ei[...]
    w_e, w_s, w_r = w_in[:, :D], w_in[:, D : 2 * D], w_in[:, 2 * D :]
    a_edge[...] = weight_pack(0.5 * w_e)
    a_state[...] = jnp.concatenate([weight_pack(0.5 * w_s), weight_pack(0.5 * w_r)], axis=0)
    w_o = w_eo[...]
    w_oc = w_o - jnp.mean(w_o, axis=0, keepdims=True)
    b_oc = b_eo - jnp.mean(b_eo, axis=0, keepdims=True)
    back = 0.5 * exact(w_o, w_oc, ((0,), (0,)))
    b_back = 0.5 * exact(w_o, b_oc, ((0,), (0,)))
    a_hidden[...] = jnp.concatenate(
        [weight_pack(w_oc, b_oc), weight_pack(back, b_back)], axis=0
    )
    a_edge_t[...] = weight_pack(w_e.T)
    a_send_t[...] = weight_pack(w_s.T)
    a_recv_t[...] = weight_pack(w_r.T)
    w_n = w_ni[...]
    a_node_in[...] = weight_pack(0.5 * w_n)
    w_no_v = w_no[...]
    a_node_out[...] = weight_pack(
        w_no_v - jnp.mean(w_no_v, axis=0, keepdims=True),
        b_no - jnp.mean(b_no, axis=0, keepdims=True),
    )
    a_node_out_t[...] = weight_pack(0.5 * w_no_v.T)
    w_nt = w_n.T
    scaled = gain_e * w_nt[D:]
    scaled = scaled - jnp.mean(scaled, axis=0, keepdims=True)
    a_node_in_t[...] = jnp.concatenate(
        [
            weight_pack(w_nt),
            weight_pack(scaled),
            weight_pack(0.5 * exact(w_o, scaled, ((0,), (0,)))),
        ],
        axis=0,
    )

    for copy in copies:
        copy.wait()
    state[rows + 1] = landing[0]
    state[0] = landing[1]
    from_east = landing[2]
    from_west = landing[3]
    corner = lambda slot, at, to: jnp.where(
        lane == to, pltpu.roll(landing[slot], (to - at) % LANES, 1), 0.0
    )
    east_out[...] = (
        pltpu.roll(jnp.where((lane >= 1) & (lane <= rows), from_east, 0.0), LANES - 1, 1)
        + corner(4, 0, rows)
        + corner(6, 0, LANES - 1)
    )
    west_out[...] = (
        pltpu.roll(jnp.where(lane < rows, from_west, 0.0), 1, 1)
        + corner(5, LANES - 1, rows + 1)
        + corner(7, LANES - 1, 0)
    )


def halo_call(n_blk, n_lon, counts, nodes, mean, logstd, noise, w_ei, w_eo, w_ni, w_no, vectors):
    rows = nodes.shape[1]
    tile = jax.ShapeDtypeStruct((D, LANES), F32)
    pack = lambda *shape: jax.ShapeDtypeStruct(shape, BF16)
    return pl.pallas_call(
        functools.partial(halo_kernel, n_blk, n_lon),
        name="state_halo",
        out_shape=(
            jax.ShapeDtypeStruct((rows + 2, D, LANES), F32),
            tile,
            tile,
            tile,
            pack(D, 3 * D),
            pack(2 * D, 3 * D),
            pack(2 * D, 3 * D + 16),
            pack(D, 3 * D),
            pack(D, 3 * D),
            pack(D, 3 * D),
            pack(D, 6 * D),
            pack(D, 3 * D + 16),
            pack(D, 3 * D),
            pack(4 * D, 3 * D),
            jax.ShapeDtypeStruct((6, D, LANES), F32),
        ),
        in_specs=[SMEM] + [HBM] * 4 + [VMEM] * 5,
        out_specs=[VMEM] * 15,
        scratch_shapes=[
            pltpu.VMEM((rows, 4, D, LANES), F32),
            pltpu.VMEM((4, D, LANES), F32),
            pltpu.VMEM((8, D, LANES), F32),
            pltpu.SemaphoreType.DMA((4,)),
            pltpu.SemaphoreType.DMA((8,)),
            pltpu.SemaphoreType.DMA((8,)),
        ],
        compiler_params=pltpu.CompilerParams(
            collective_id=0, has_side_effects=True, vmem_limit_bytes=32 * 2**20
        ),
    )(counts, nodes, mean, logstd, noise, w_ei, w_eo, w_ni, w_no, vectors)


def layer_kernel(
    counts,
    place,
    edges,
    cotangent,
    neighbors,
    edge_mask,
    state,
    west_col,
    east_col,
    diverged,
    a_edge,
    a_state,
    a_hidden,
    a_edge_t,
    a_send_t,
    a_recv_t,
    a_node_in,
    a_node_out,
    a_node_out_t,
    a_node_in_t,
    columns,
    new_states,
    grad_edges,
    part_nodes,
    row_halo,
    col_halo,
    packed,
    xb,
    xs,
    hs,
    cb,
    db,
    slope,
    windows,
    receiver,
    codes,
    valid,
    inverse,
    summed,
    qc_ref,
    qo_ref,
    cot,
    fresh,
    placed,
    grad_recv,
    acc_edge,
    acc_hidden,
    acc_send,
    acc_recv,
    acc_nin,
    acc_nout,
    acc_vec,
    edge_sem,
    cot_sem,
    out_sem,
    new_sem,
):
    rows = edges.shape[2]
    wide = NBR * LANES
    unroll = 2
    lane = lane_ids()
    lane8 = lane_ids(8)

    for r in range(rows):
        for k in range(NBR):
            pltpu.make_async_copy(
                edges.at[:, k, r, :],
                xb.at[r, :, pl.ds(k * LANES, LANES)],
                edge_sem.at[r],
            ).start()
    for r in range(rows):
        pltpu.make_async_copy(cotangent.at[:, r, :], cot.at[r], cot_sem).start()

    count_here, count_prev, count_next = counts[place[0]], counts[place[1]], counts[place[2]]
    row_id = lax.broadcasted_iota(jnp.int32, (rows, LANES), 0)
    col_id = lax.broadcasted_iota(jnp.int32, (rows, LANES), 1)
    above = jnp.where(row_id == 0, count_prev, count_here)
    below = jnp.where(row_id == rows - 1, count_next, count_here)
    codes[...] = jnp.zeros_like(codes)
    valid[...] = jnp.zeros_like(valid)
    inverse[...] = jnp.zeros_like(inverse)
    for k in range(NBR):
        delta = neighbors[k] - (row_id * (LANES + 2) + col_id)
        first = delta < LANES + 2
        middle = delta < 2 * (LANES + 2)
        step = jnp.where(
            first, delta, jnp.where(middle, delta - (LANES + 2), delta - 2 * (LANES + 2))
        )
        code = jnp.where(first, step, jnp.where(middle, 3 + (step >> 1), 5 + step))
        owner = col_id + step - 1
        owner = jnp.where(owner < 0, LANES - 1, jnp.where(owner >= LANES, 0, owner))
        limit = jnp.where(first, above, jnp.where(middle, count_here, below))
        codes[:, k, :] = code
        valid[:, k, :] = jnp.where(
            (col_id < count_here) & (owner < limit), edge_mask[k].astype(F32), 0.0
        )

    half_bias = columns[0]
    sides = []
    for column in (west_col, east_col):
        high, low = halves(column[...])
        sides.append(mxu(a_state[:D], jnp.concatenate([high, low, high], axis=0)))
    west_side, east_side = sides

    def project(t):
        high, low = halves(state[t])
        both = mxu(a_state[...], jnp.concatenate([high, low, high], axis=0))
        send = both[:D]
        windows[t, 1] = send
        mix = pltpu.roll(
            jnp.where(lane == t, west_side, east_side), lax.rem(LANES - t, LANES), 1
        )
        windows[t, 0] = jnp.where(lane == 0, mix, pltpu.roll(send, 1, 1))
        windows[t, 2] = jnp.where(lane == LANES - 1, mix, pltpu.roll(send, LANES - 1, 1))
        receiver[t] = both[D:] + half_bias

    lax.fori_loop(0, (rows + 2) // 2, lambda i, _: (project(2 * i), project(2 * i + 1))[0], None)

    ones16 = jnp.where(
        lax.broadcasted_iota(jnp.int32, (16, wide), 0) < 2, 1.0, 0.0
    ).astype(BF16)

    def forward_row(r):
        pltpu.make_async_copy(xb.at[r], xb.at[r], edge_sem.at[r]).wait()
        x_high, x_low = halves(xb[r])
        xs[r, :D] = x_high
        xs[r, D:] = x_low
        from_edge = mxu(a_edge[...], jnp.concatenate([x_high, x_low, x_high], axis=0))
        hidden = [[None] * 8 for _ in range(NBR)]
        for pair in ((0, 1), (2, 3), (4, 5)):
            masks = {}
            for k in pair:
                code = jnp.broadcast_to(codes[r, pl.ds(k, 1), :], (8, LANES))
                masks[k] = ((code & 1) != 0, (code & 2) != 0, (code & 4) != 0)
            for f in range(8):
                part = pl.ds(8 * f, 8)
                w = [windows[r + 1 + dr, 1 + dc, part, :] for dr, dc in WINDOWS]
                base = receiver[r + 1, part, :]
                for k in pair:
                    b0, b1, b2 = masks[k]
                    low = jnp.where(b1, jnp.where(b0, w[3], w[2]), jnp.where(b0, w[1], w[0]))
                    top = jnp.where(b1, jnp.where(b0, w[7], w[6]), jnp.where(b0, w[5], w[4]))
                    pre = (
                        from_edge[8 * f : 8 * f + 8, k * LANES : (k + 1) * LANES]
                        + base
                        + jnp.where(b2, top, low)
                    )
                    t = jnp.tanh(pre)
                    u = 1.0 + t
                    h = pre * u
                    slope[r, part, pl.ds(k * LANES, LANES)] = u + h * (1.0 - t)
                    hidden[k][f] = h
        highs, lows = [], []
        for k in range(NBR):
            high, low = halves(jnp.concatenate(hidden[k], axis=0))
            highs.append(high)
            lows.append(low)
        high = jnp.concatenate(highs, axis=1)
        low = jnp.concatenate(lows, axis=1)
        hs[r, :D] = high
        hs[r, D : 2 * D] = low
        hs[r, 2 * D :] = ones16
        both = mxu(a_hidden[...], jnp.concatenate([high, low, ones16, high], axis=0))
        cb[r] = both[:D]
        db[r] = both[D:]
        gathered = jnp.zeros((D, LANES), F32)
        for k in range(NBR):
            c = both[:D, k * LANES : (k + 1) * LANES]
            variance = jnp.sum(c * c, axis=0, keepdims=True) * (1.0 / D)
            inv = lax.rsqrt(variance + EPS)
            inverse[r, pl.ds(k, 1), :] = inv
            gathered += (inv * valid[r, pl.ds(k, 1), :]) * c
        summed[r] = gathered

    def forward(i, _):
        for u in range(unroll):
            forward_row(unroll * i + u)

    lax.fori_loop(0, rows // unroll, forward, None)

    for ref in (acc_edge, acc_hidden, acc_send, acc_recv, acc_nin, acc_nout, acc_vec, placed):
        ref[...] = jnp.zeros_like(ref)
    pltpu.make_async_copy(cot, cot, cot_sem).wait()
    chunk = 4

    def tile_cols(tile):
        return jnp.concatenate([tile] * chunk, axis=1)

    gain_e, shift_e = tile_cols(columns[1]), tile_cols(columns[2])
    half_bias_n, gain_n, shift_n = (
        tile_cols(columns[3]),
        tile_cols(columns[4]),
        tile_cols(columns[5]),
    )
    ones_node = ones16[:, : chunk * LANES]

    def node(i, _):
        first = i * chunk
        spread = lambda ref, offset: jnp.concatenate(
            [ref[first + offset + j] for j in range(chunk)], axis=1
        )
        st = spread(state, 1)
        total = spread(summed, 0)
        cot_c = spread(cot, 0)
        degree = jnp.concatenate(
            [jnp.sum(valid[first + j], axis=0, keepdims=True) for j in range(chunk)], axis=1
        )
        incoming = gain_e * total + shift_e * degree
        st_high, st_low = halves(st)
        inc_high, inc_low = halves(incoming)
        tops = jnp.concatenate([st_high, inc_high], axis=0)
        ends = jnp.concatenate([st_low, inc_low], axis=0)
        pre = mxu(a_node_in[...], jnp.concatenate([tops, ends, tops], axis=0)) + half_bias_n
        t = jnp.tanh(pre)
        u = 1.0 + t
        h = pre * u
        slope_n = u + h * (1.0 - t)
        h_high, h_low = halves(h)
        h_all = jnp.concatenate([h_high, h_low, ones_node], axis=0)
        c = mxu(a_node_out[...], jnp.concatenate([h_all, h_high], axis=0))
        inv = lax.rsqrt(jnp.sum(c * c, axis=0, keepdims=True) * (1.0 / D) + EPS)
        n = c * inv
        new = st + (gain_n * n + shift_n)
        q = cot_c * gain_n
        q = q - jnp.sum(q, axis=0, keepdims=True) * (1.0 / D)
        grad = inv * (q - n * (jnp.sum(q * n, axis=0, keepdims=True) * (1.0 / D)))
        g_high, g_low = halves(grad)
        acc_nout[...] += outer(jnp.concatenate([g_high, g_low], axis=0), h_all)
        pre_grad = mxu(a_node_out_t[...], jnp.concatenate([g_high, g_low, g_high], axis=0))
        pre_grad = pre_grad * slope_n
        p_high, p_low = halves(pre_grad)
        acc_nin[...] += outer(
            jnp.concatenate([p_high, p_low], axis=0), jnp.concatenate([tops, ends], axis=0)
        )
        back = mxu(a_node_in_t[...], jnp.concatenate([p_high, p_low, p_high], axis=0))
        grad_incoming = back[D : 2 * D]
        for j in range(chunk):
            s = slice(j * LANES, (j + 1) * LANES)
            fresh[first + j] = new[:, s]
            part_nodes[first + j] = cot_c[:, s] + back[:D, s]
            qc_ref[first + j] = back[2 * D : 3 * D, s]
            qo_ref[first + j] = back[3 * D :, s]
            acc_vec[0] += grad_incoming[:, s] * total[:, s]
            acc_vec[1] += grad_incoming[:, s] * degree[:, s]
            acc_vec[2] += pre_grad[:, s]
            acc_vec[3] += cot_c[:, s] * n[:, s]
            acc_vec[4] += cot_c[:, s]
            pltpu.make_async_copy(
                fresh.at[first + j], new_states.at[:, first + j, :], new_sem
            ).start()

    lax.fori_loop(0, rows // chunk, node, None)

    def backward_row(r):
        qc = qc_ref[r]
        qo = qo_ref[r]
        o_highs, o_lows, p_highs, p_lows = [], [], [], []
        grads = []
        received = None
        for k in range(NBR):
            s = pl.ds(k * LANES, LANES)
            c = cb[r, :, s]
            inv = inverse[r, pl.ds(k, 1), :]
            alpha = inv * valid[r, pl.ds(k, 1), :]
            moment = jnp.sum(qc * c, axis=0, keepdims=True) * (1.0 / D)
            beta = alpha * inv * inv * moment
            high, low = halves(alpha * qc - beta * c)
            o_highs.append(high)
            o_lows.append(low)
            grad = (alpha * qo - beta * db[r, :, s]) * slope[r, :, s]
            grads.append(grad)
            received = grad if received is None else received + grad
            high, low = halves(grad)
            p_highs.append(high)
            p_lows.append(low)
        grad_recv[r] = received
        o_high, o_low, p_high, p_low = [
            jnp.concatenate(x, axis=1) for x in (o_highs, o_lows, p_highs, p_lows)
        ]
        acc_hidden[...] += outer(jnp.concatenate([o_high, o_low], axis=0), hs[r])
        both = jnp.concatenate([p_high, p_low], axis=0)
        acc_edge[...] += outer(both, xs[r])
        xb[r] = mxu(a_edge_t[...], jnp.concatenate([both, p_high], axis=0))
        for k in range(NBR):
            pltpu.make_async_copy(
                xb.at[r, :, pl.ds(k * LANES, LANES)], grad_edges.at[:, k, r, :], out_sem
            ).start()
        code = [jnp.broadcast_to(codes[r, pl.ds(k, 1), :], (8, LANES)) for k in range(NBR)]
        for which, (dr, dc) in enumerate(WINDOWS):
            masks = [code[k] == which for k in range(NBR)]
            for f in range(8):
                part = pl.ds(8 * f, 8)
                value = placed[r + 1 + dr, 1 + dc, part, :]
                for k in range(NBR):
                    value += jnp.where(masks[k], grads[k][8 * f : 8 * f + 8], 0.0)
                placed[r + 1 + dr, 1 + dc, part, :] = value

    def backward(i, _):
        for u in range(unroll):
            backward_row(unroll * i + u)

    lax.fori_loop(0, rows // unroll, backward, None)

    def settle(t, cols):
        west_cells, east_cells = cols
        centre = placed[t, 1]
        to_west = placed[t, 0]
        to_east = placed[t, 2]
        own = (
            centre
            + jnp.where(lane == 0, 0.0, pltpu.roll(to_east, 1, 1))
            + jnp.where(lane == LANES - 1, 0.0, pltpu.roll(to_west, LANES - 1, 1))
        )
        mix = pltpu.roll(jnp.where(lane == 0, to_west, to_east), t, 1)
        west_cells = jnp.where(lane == t, mix, west_cells)
        east_cells = jnp.where(lane == lax.rem(t + LANES - 1, LANES), mix, east_cells)
        return own, (west_cells, east_cells)

    def sends(own, there):
        high, low = halves(own)
        there_high, there_low = halves(there)
        both = jnp.concatenate([high, low], axis=0)
        acc_send[...] += outer(both, jnp.concatenate([there_high, there_low], axis=0))
        return mxu(a_send_t[...], jnp.concatenate([both, high], axis=0))

    ones_row = ones16[:, :LANES]

    def finish(i, cols):
        for u in range(2):
            t = 1 + 2 * i + u
            own, cols = settle(t, cols)
            st = state[t]
            st_high, st_low = halves(st)
            high, low = halves(own)
            both = jnp.concatenate([high, low], axis=0)
            st_both = jnp.concatenate([st_high, st_low], axis=0)
            acc_send[...] += outer(both, st_both)
            grad = mxu(a_send_t[...], jnp.concatenate([both, high], axis=0))
            high, low = halves(grad_recv[t - 1])
            both = jnp.concatenate([high, low], axis=0)
            acc_recv[...] += outer(both, jnp.concatenate([st_both, ones_row], axis=0))
            grad += mxu(a_recv_t[...], jnp.concatenate([both, high], axis=0))
            part_nodes[t - 1] += grad
        return cols

    zero = jnp.zeros((D, LANES), F32)
    own, cols = settle(0, (zero, zero))
    row_halo[0] = sends(own, state[0])
    cols = lax.fori_loop(0, rows // 2, finish, cols)
    own, cols = settle(rows + 1, cols)
    row_halo[1] = sends(own, state[rows + 1])
    col_halo[0] = sends(cols[0], west_col[...])
    col_halo[1] = sends(cols[1], east_col[...])

    def folded(acc):
        half = acc[:D, : 2 * D] + acc[D:, : 2 * D]
        return half + pltpu.roll(half, D, 1)

    left = lane < D
    packed[0] = jnp.where(left, folded(acc_edge), folded(acc_send))
    block = jnp.where(left, folded(acc_recv), 0.0)
    ones_sum = lambda ref: jnp.sum(
        jnp.where(lane_ids()[:, :16] == 0, ref[:D, 2 * D :] + ref[D:, 2 * D :], 0.0),
        axis=1,
        keepdims=True,
    )
    lane_sum = lambda i: jnp.sum(acc_vec[i], axis=1, keepdims=True)
    vectors = (
        ones_sum(acc_recv),
        ones_sum(acc_hidden),
        lane_sum(0),
        lane_sum(1),
        lane_sum(2),
        ones_sum(acc_nout),
        lane_sum(3),
        lane_sum(4),
        diverged[:, :1],
    )
    for i, vector in enumerate(vectors):
        block = jnp.where(lane == D + i, vector, block)
    packed[1] = block
    packed[2] = (
        acc_nin[:D, : 2 * D]
        + acc_nin[D:, : 2 * D]
        + acc_nin[:D, 2 * D :]
        + acc_nin[D:, 2 * D :]
    )
    packed[3] = jnp.where(left, folded(acc_hidden), folded(acc_nout))
    pltpu.make_async_copy(fresh, fresh, new_sem).wait()
    pltpu.make_async_copy(xb, xb, out_sem).wait()


def layer_call(counts, place, edges, cotangent, neighbors, edge_mask, halo):
    rows = edges.shape[2]
    wide = NBR * LANES
    tile = (D, LANES)
    shape = lambda *dims: jax.ShapeDtypeStruct(dims, F32)
    vmem = lambda *dims: pltpu.VMEM(dims, F32)
    return pl.pallas_call(
        layer_kernel,
        name="layer",
        out_shape=(
            shape(D, rows, LANES),
            shape(D, NBR, rows, LANES),
            shape(rows, *tile),
            shape(2, *tile),
            shape(2, *tile),
            shape(4, *tile),
        ),
        in_specs=[SMEM, SMEM, HBM, HBM] + [VMEM] * (2 + len(halo)),
        out_specs=[HBM, HBM] + [VMEM] * 4,
        scratch_shapes=[
            vmem(rows, D, wide),
            pltpu.VMEM((rows, 2 * D, wide), BF16),
            pltpu.VMEM((rows, 2 * D + 16, wide), BF16),
            vmem(rows, D, wide),
            vmem(rows, D, wide),
            vmem(rows, D, wide),
            vmem(rows + 2, 3, *tile),
            vmem(rows + 2, *tile),
            pltpu.VMEM((rows, 8, LANES), jnp.int32),
            vmem(rows, 8, LANES),
            vmem(rows, 8, LANES),
            vmem(rows, *tile),
            vmem(rows, *tile),
            vmem(rows, *tile),
            vmem(rows, *tile),
            vmem(rows, *tile),
            vmem(rows + 2, 3, *tile),
            vmem(rows, *tile),
            vmem(2 * D, 2 * D),
            vmem(2 * D, 2 * D + 16),
            vmem(2 * D, 2 * D),
            vmem(2 * D, 2 * D + 16),
            vmem(2 * D, 4 * D),
            vmem(2 * D, 2 * D + 16),
            vmem(5, *tile),
            pltpu.SemaphoreType.DMA((rows,)),
            pltpu.SemaphoreType.DMA,
            pltpu.SemaphoreType.DMA,
            pltpu.SemaphoreType.DMA,
        ],
        compiler_params=pltpu.CompilerParams(vmem_limit_bytes=60 * 2**20),
    )(counts, place, edges, cotangent, neighbors, edge_mask, *halo)


def sum_kernel(
    n_blk,
    n_lon,
    n_rows,
    part,
    row_halo,
    col_halo,
    total,
    row_in,
    col_in,
    scattered,
    across,
    gathered,
    landing,
    rs_send,
    rs_recv,
    x_send,
    x_recv,
    ag_send,
    ag_recv,
    halo_send,
    halo_recv,
):
    blk = lax.axis_index("blk")
    lon = lax.axis_index("lon")
    up = lax.rem(blk + n_blk - 1, n_blk)
    down = lax.rem(blk + 1, n_blk)
    west = lax.rem(lon + n_lon - 1, n_lon)
    east = lax.rem(lon + 1, n_lon)
    around = (
        (up, lon),
        (down, lon),
        (blk, west),
        (blk, east),
        (up, west),
        (up, east),
        (down, west),
        (down, east),
    )
    size = scattered.shape[0]
    n_groups = across.shape[0]
    per = size // n_lon
    me = lax.rem(blk, per) * n_lon + lon
    own_group = blk // per

    def member(index):
        return (own_group * per + index // n_lon, lax.rem(index, n_lon))

    def other(step):
        return lax.rem(me + step, size)

    barrier = pltpu.get_barrier_semaphore()

    def greet(step, _):
        pl.semaphore_signal(
            barrier, inc=1, device_id=member(other(step)), device_id_type=MESH
        )

    lax.fori_loop(1, size, greet, None)
    expected = size - 1
    if n_groups > 1:
        for place in around:
            pl.semaphore_signal(barrier, inc=1, device_id=place, device_id_type=MESH)

        def greet_group(step, _):
            place = (lax.rem(own_group + step, n_groups) * per + lax.rem(blk, per), lon)
            pl.semaphore_signal(barrier, inc=1, device_id=place, device_id_type=MESH)

        lax.fori_loop(1, n_groups, greet_group, None)
        expected += 8 + n_groups - 1
    pl.semaphore_wait(barrier, expected)

    def scatter(step):
        target = other(step)
        return pltpu.make_async_remote_copy(
            src_ref=part.at[target],
            dst_ref=scattered.at[me],
            send_sem=rs_send,
            recv_sem=rs_recv,
            device_id=member(target),
            device_id_type=MESH,
        )

    lax.fori_loop(1, size, lambda step, _: scatter(step).start(), None)
    copies = []
    for slot, (place, source) in enumerate(
        zip(
            around,
            (
                row_halo.at[0],
                row_halo.at[1],
                col_halo.at[0],
                col_halo.at[1],
                col_halo.at[0],
                col_halo.at[1],
                col_halo.at[0],
                col_halo.at[1],
            ),
        )
    ):
        copies.append(
            pltpu.make_async_remote_copy(
                src_ref=source,
                dst_ref=landing.at[slot],
                send_sem=halo_send.at[slot],
                recv_sem=halo_recv.at[slot],
                device_id=place,
                device_id_type=MESH,
            )
        )
        copies[-1].start()
    scattered[me] = part[me]
    rest = pl.ds(0, size - 1)
    pltpu.make_async_copy(scattered.at[rest], scattered.at[rest], rs_recv).wait()
    mine = scattered[0]
    for i in range(1, size):
        mine = mine + scattered[i]
    if n_groups > 1:
        across[own_group] = mine

        def cross(step):
            place = (lax.rem(own_group + step, n_groups) * per + lax.rem(blk, per), lon)
            return pltpu.make_async_remote_copy(
                src_ref=across.at[own_group],
                dst_ref=across.at[own_group],
                send_sem=x_send,
                recv_sem=x_recv,
                device_id=place,
                device_id_type=MESH,
            )

        lax.fori_loop(1, n_groups, lambda step, _: cross(step).start(), None)
        others = pl.ds(0, n_groups - 1)
        pltpu.make_async_copy(across.at[others], across.at[others], x_recv).wait()
        pltpu.make_async_copy(across.at[others], across.at[others], x_send).wait()
        mine = across[0]
        for i in range(1, n_groups):
            mine = mine + across[i]
    gathered[me] = mine

    def gather(step):
        return pltpu.make_async_remote_copy(
            src_ref=gathered.at[me],
            dst_ref=gathered.at[me],
            send_sem=ag_send,
            recv_sem=ag_recv,
            device_id=member(other(step)),
            device_id_type=MESH,
        )

    lax.fori_loop(1, size, lambda step, _: gather(step).start(), None)
    for copy in copies:
        copy.wait()
    row_in[0] = landing[1]
    row_in[1] = landing[0]
    lane = lane_ids()
    corner = lambda slot, at, to: jnp.where(
        lane == to, pltpu.roll(landing[slot], (to - at) % LANES, 1), 0.0
    )
    col_in[0] = (
        pltpu.roll(jnp.where(lane < n_rows, landing[3], 0.0), 1, 1)
        + corner(7, n_rows, 1)
        + corner(5, LANES - 1, n_rows)
    )
    east_in = (
        jnp.where((lane >= 1) & (lane <= n_rows), landing[2], 0.0)
        + corner(6, n_rows + 1, 1)
        + corner(4, 0, n_rows)
    )
    col_in[1] = pltpu.roll(east_in, LANES - 1, 1)
    pltpu.make_async_copy(gathered.at[rest], gathered.at[rest], ag_recv).wait()
    total[...] = gathered[...]
    pltpu.make_async_copy(scattered.at[rest], scattered.at[rest], rs_send).wait()
    pltpu.make_async_copy(gathered.at[rest], gathered.at[rest], ag_send).wait()


def sum_call(n_blk, n_lon, n_rows, part, row_halo, col_halo):
    size = part.shape[0]
    n_groups = n_blk * n_lon // size
    chunk = part.shape[1:]
    tile = (D, LANES)
    return pl.pallas_call(
        functools.partial(sum_kernel, n_blk, n_lon, n_rows),
        name="sums",
        out_shape=(
            jax.ShapeDtypeStruct(part.shape, F32),
            jax.ShapeDtypeStruct((2, *tile), F32),
            jax.ShapeDtypeStruct((2, *tile), F32),
        ),
        in_specs=[VMEM] * 3,
        out_specs=[VMEM] * 3,
        scratch_shapes=[
            pltpu.VMEM(part.shape, F32),
            pltpu.VMEM((n_groups, *chunk), F32),
            pltpu.VMEM(part.shape, F32),
            pltpu.VMEM((8, *tile), F32),
            pltpu.SemaphoreType.DMA,
            pltpu.SemaphoreType.DMA,
            pltpu.SemaphoreType.DMA,
            pltpu.SemaphoreType.DMA,
            pltpu.SemaphoreType.DMA,
            pltpu.SemaphoreType.DMA,
            pltpu.SemaphoreType.DMA((8,)),
            pltpu.SemaphoreType.DMA((8,)),
        ],
        compiler_params=pltpu.CompilerParams(collective_id=1, has_side_effects=True),
    )(part, row_halo, col_halo)


def final_kernel(
    n_lon,
    counts,
    place,
    kl_weight,
    part_nodes,
    mean,
    logstd,
    noise,
    row_in,
    col_in,
    total,
    grad_nodes,
    grad_mean,
    grad_logstd,
    kl_value,
    g_w_ei,
    g_w_eo,
    g_w_ni,
    g_w_no,
    g_vec,
    buf,
    out,
    in_sem,
    out_sem,
):
    rows = mean.shape[1]
    lane = lane_ids()
    n_groups = in_sem.shape[0]
    group = rows // n_groups
    for g in range(n_groups):
        span = pl.ds(g * group, group)
        for r in range(g * group, (g + 1) * group):
            for which, source in enumerate((mean, logstd, noise)):
                pltpu.make_async_copy(
                    source.at[:, r, :], buf.at[r, which], in_sem.at[g]
                ).start()
            pltpu.make_async_copy(part_nodes.at[r], buf.at[r, 3], in_sem.at[g]).start()
    weight = kl_weight[0]
    inside = jnp.where(lane < counts[place[0]], weight, 0.0)
    blocks = [total[i] for i in range(4)]
    g_w_ei[:, : 2 * D] = blocks[0]
    g_w_ei[:, 2 * D :] = blocks[1][:, :D]
    g_w_ni[...] = blocks[2]
    g_w_eo[...] = blocks[3][:, :D]
    g_w_no[...] = pltpu.roll(blocks[3], D, 1)[:, :D]
    for i in range(8):
        g_vec[i] = to_row(blocks[1][:, D + i : D + i + 1])
    n_valid = counts[0]
    for i in range(1, counts.shape[0]):
        n_valid += counts[i]
    scale = (D * rows * n_lon * n_valid).astype(F32)
    diverged = jnp.sum(blocks[1][:, D + 8 : D + 9], axis=0, keepdims=True)
    kl_value[...] = diverged / jnp.full((1, 1), scale)
    west_in = col_in[0]
    east_in = col_in[1]
    for g in range(n_groups):
        span = pl.ds(g * group, group)
        pltpu.make_async_copy(buf.at[span], buf.at[span], in_sem.at[g]).wait()
        for r in range(g * group, (g + 1) * group):
            mix = pltpu.roll(jnp.where(lane == r + 1, west_in, east_in), LANES - 1 - r, 1)
            grad = buf[r, 3] + jnp.where((lane == 0) | (lane == LANES - 1), mix, 0.0)
            if r == 0:
                grad = grad + row_in[0]
            if r == rows - 1:
                grad = grad + row_in[1]
            spread = jnp.exp(buf[r, 1])
            out[r, 0] = grad
            out[r, 1] = grad + inside * buf[r, 0]
            out[r, 2] = grad * spread * buf[r, 2] + inside * (spread * spread - 1.0)
            for which, target in enumerate((grad_nodes, grad_mean, grad_logstd)):
                pltpu.make_async_copy(
                    out.at[r, which], target.at[:, r, :], out_sem
                ).start()
    pltpu.make_async_copy(out, out, out_sem).wait()


def final_call(n_lon, counts, place, kl_weight, part_nodes, mean, logstd, noise, sums):
    rows = mean.shape[1]
    total, row_in, col_in = sums
    shape = lambda *dims: jax.ShapeDtypeStruct(dims, F32)
    whole = shape(D, rows, LANES)
    return pl.pallas_call(
        functools.partial(final_kernel, n_lon),
        name="final",
        out_shape=(
            whole,
            whole,
            whole,
            shape(1, 1),
            shape(D, 3 * D),
            shape(D, D),
            shape(D, 2 * D),
            shape(D, D),
            shape(8, 1, D),
        ),
        in_specs=[SMEM] * 3 + [HBM] * 4 + [VMEM] * 3,
        out_specs=[HBM] * 3 + [VMEM] * 6,
        scratch_shapes=[
            pltpu.VMEM((rows, 4, D, LANES), F32),
            pltpu.VMEM((rows, 3, D, LANES), F32),
            pltpu.SemaphoreType.DMA((4,)),
            pltpu.SemaphoreType.DMA,
        ],
        compiler_params=pltpu.CompilerParams(vmem_limit_bytes=32 * 2**20),
    )(
        counts,
        place,
        kl_weight,
        part_nodes,
        mean,
        logstd,
        noise,
        row_in,
        col_in,
        total.reshape(4, D, LANES),
    )


def shards(
    nodes,
    edges,
    latent_mean,
    latent_logstd,
    latent_noise,
    kl_weight,
    band_counts,
    neighbors,
    edge_mask,
    w_edge_in,
    b_edge_in,
    w_edge_out,
    b_edge_out,
    edge_gain,
    edge_shift,
    w_node_in,
    b_node_in,
    w_node_out,
    b_node_out,
    node_gain,
    node_shift,
    cotangent,
):
    n_blk = lax.axis_size("blk")
    n_lon = lax.axis_size("lon")
    blk = lax.axis_index("blk").astype(jnp.int32)
    place = jnp.stack([blk, lax.rem(blk + n_blk - 1, n_blk), lax.rem(blk + 1, n_blk)])
    vectors = jnp.stack(
        [
            b_edge_in,
            b_edge_out,
            edge_gain,
            edge_shift,
            b_node_in,
            b_node_out,
            node_gain,
            node_shift,
        ]
    ).reshape(8, 1, D)
    halo = halo_call(
        n_blk,
        n_lon,
        band_counts,
        nodes,
        latent_mean,
        latent_logstd,
        latent_noise,
        w_edge_in,
        w_edge_out,
        w_node_in,
        w_node_out,
        vectors,
    )
    new_states, grad_edges, part_nodes, row_halo, col_halo, packed = layer_call(
        band_counts, place, edges, cotangent, neighbors, edge_mask, halo
    )
    size = min(32, n_blk * n_lon)
    sums = sum_call(
        n_blk, n_lon, nodes.shape[1], packed.reshape(size, 4 * D // size, LANES), row_halo, col_halo
    )
    grad_nodes, grad_mean, grad_logstd, kl_value, g_w_ei, g_w_eo, g_w_ni, g_w_no, g_vec = (
        final_call(
            n_lon,
            band_counts,
            place,
            kl_weight,
            part_nodes,
            latent_mean,
            latent_logstd,
            latent_noise,
            sums,
        )
    )
    g_vec = [g_vec[i, 0] for i in range(8)]
    return (
        new_states,
        kl_value.reshape(1),
        grad_nodes,
        grad_edges,
        grad_mean,
        grad_logstd,
        g_w_ei,
        g_vec[0],
        g_w_eo,
        g_vec[1],
        g_vec[2],
        g_vec[3],
        g_w_ni,
        g_vec[4],
        g_w_no,
        g_vec[5],
        g_vec[6],
        g_vec[7],
    )


def solution(mesh):
    node = P(None, "blk", "lon")
    slot = P(None, None, "blk", "lon")
    return jax.shard_map(
        shards,
        mesh=mesh,
        in_specs=(
            (node, slot, node, node, node, P(), P(), node, node) + (P(),) * 12 + (node,)
        ),
        out_specs=(node, P(), node, slot, node, node) + (P(),) * 12,
        check_vma=False,
    )
```

```python
import functools

import jax
import jax.numpy as jnp
from jax import lax
from jax.experimental import pallas as pl
from jax.experimental.pallas import tpu as pltpu
from jax.sharding import PartitionSpec as P

F32 = jnp.float32
BF16 = jnp.bfloat16
MESH = pl.DeviceIdType.MESH
D = 64
LANES = 128
NBR = 6
EPS = 1e-05
HBM = pl.BlockSpec(memory_space=pltpu.HBM)
VMEM = pl.BlockSpec(memory_space=pltpu.VMEM)
ROOM = 62 * 2**20
SMEM = pl.BlockSpec(memory_space=pltpu.SMEM)

WINDOWS = ((-1, -1), (-1, 0), (-1, 1), (0, -1), (0, 1), (1, -1), (1, 0), (1, 1))


def halves(value):
    high = value.astype(BF16)
    return high, (value - high.astype(F32)).astype(BF16)


def weight_pack(weight, bias=None):
    high, low = halves(weight)
    if bias is None:
        return jnp.concatenate([high, high, low], axis=1)
    bias_high, bias_low = halves(bias)
    place = lax.broadcasted_iota(jnp.int32, (weight.shape[0], 16), 1)
    wide = jnp.where(
        place == 0, bias_high.astype(F32), jnp.where(place == 1, bias_low.astype(F32), 0.0)
    )
    return jnp.concatenate([high, high, wide.astype(BF16), low], axis=1)


def mxu(left, right):
    return jnp.dot(left, right, preferred_element_type=F32)


def outer(left, right):
    return lax.dot_general(
        left, right, (((1,), (1,)), ((), ())), preferred_element_type=F32
    )


def exact(left, right, dims):
    return lax.dot_general(
        left,
        right,
        (dims, ((), ())),
        precision=lax.Precision.HIGHEST,
        preferred_element_type=F32,
    )


def eye():
    return lax.broadcasted_iota(jnp.int32, (D, D), 0) == lax.broadcasted_iota(
        jnp.int32, (D, D), 1
    )


def to_column(row):
    return jnp.sum(jnp.where(eye(), row, 0.0), axis=1, keepdims=True)


def to_row(column):
    return jnp.sum(jnp.where(eye(), column, 0.0), axis=0, keepdims=True)


def waits(ref, sem):
    pltpu.make_async_copy(ref, ref, sem).wait()


def in_turn(*routines):
    waiting = list(routines)
    while waiting:
        for routine in list(waiting):
            if next(routine, routine) is routine:
                waiting.remove(routine)


def lane_ids(rows=D):
    return lax.broadcasted_iota(jnp.int32, (rows, LANES), 1)


P_HIDDEN, P_EDGE_T, P_SEND_T, P_RECV_T = (0, 128), (128, 192), (192, 256), (256, 320)
P_NODE_IN, P_NODE_OUT, P_NODE_OUT_T, P_NODE_IN_T = (320, 384), (384, 448), (448, 512), (512, 768)
P_ROWS, P_LANES = 768, 384
C_GAIN_E, C_SHIFT_E, C_BIAS_N, C_GAIN_N, C_SHIFT_N, C_VALID, C_DIVERGED, C_COUNT = range(8)


def packed_rows(ref, rows, lanes=3 * D):
    return ref[rows[0] : rows[1], :lanes]


def neighbours(n_blk, n_lon):
    blk = lax.axis_index("blk")
    lon = lax.axis_index("lon")
    up = lax.rem(blk + n_blk - 1, n_blk)
    down = lax.rem(blk + 1, n_blk)
    west = lax.rem(lon + n_lon - 1, n_lon)
    east = lax.rem(lon + 1, n_lon)
    around = (
        (up, lon),
        (down, lon),
        (blk, west),
        (blk, east),
        (up, west),
        (up, east),
        (down, west),
        (down, east),
    )
    return blk, lon, around


def start_kernel(
    n_blk,
    n_lon,
    counts,
    nodes,
    mean,
    logstd,
    noise,
    edges,
    neighbors,
    edge_mask,
    w_ei,
    w_eo,
    w_ni,
    w_no,
    *rest,
):
    vectors = rest[:8]
    (
        state_out,
        cols_out,
        windows_out,
        from_edge_out,
        split_out,
        codes_out,
        valid_out,
        pack_out,
        columns_out,
        buf,
        state,
        windows,
        xb,
        from_edge,
        split,
        receiver,
        nb,
        mk,
        codes,
        valid,
        v_ei,
        v_eo,
        v_ni,
        v_no,
        v_vec,
        pack,
        columns,
        cols,
        tiles,
        landing,
        in_sem,
        edge_sem,
        slot_sem,
        weight_sem,
        send_sem,
        recv_sem,
        out_sem,
    ) = rest[8:]
    rows = nodes.shape[1]
    blk, lon, around = neighbours(n_blk, n_lon)
    barrier = pltpu.get_barrier_semaphore()
    for place in around:
        pl.semaphore_signal(barrier, inc=1, device_id=place, device_id_type=MESH)

    n_groups = in_sem.shape[0]
    group = rows // n_groups

    def load_rows(g):
        def load(i, _):
            r = g * group + i
            for which, source in enumerate((nodes, mean, logstd, noise)):
                pltpu.make_async_copy(
                    source.at[:, r, :], buf.at[r, which], in_sem.at[g]
                ).start()

        lax.fori_loop(0, group, load, None)

    weights = [(w_ei, v_ei), (w_eo, v_eo), (w_ni, v_ni), (w_no, v_no)]
    weights += [(vectors[i], v_vec.at[i]) for i in range(8)]
    for source, target in weights:
        pltpu.make_async_copy(source, target, weight_sem).start()
    for g in range(n_groups):
        load_rows(g)

    def load_edges(r):
        for k in range(NBR):
            pltpu.make_async_copy(
                edges.at[:, k, r, :],
                xb.at[r, :, pl.ds(k * LANES, LANES)],
                edge_sem.at[r],
            ).start()

    def load_slots(r, _):
        pltpu.make_async_copy(
            neighbors.at[:, r, :], nb.at[r, pl.ds(0, NBR), :], slot_sem
        ).start()
        pltpu.make_async_copy(
            edge_mask.at[:, r, :], mk.at[r, pl.ds(0, NBR), :], slot_sem
        ).start()

    ahead = 8
    for r in range(ahead):
        load_edges(r)
    lax.fori_loop(0, rows, load_slots, None)

    for _, target in weights:
        waits(target, weight_sem)
    b_ei, b_eo, gain_e, shift_e, b_ni, b_no, gain_n, shift_n = [
        to_column(v_vec[i]) for i in range(8)
    ]
    lane = lane_ids()
    count = counts[blk]
    inside = lane < count
    n_valid = counts[0]
    for i in range(1, counts.shape[0]):
        n_valid += counts[i]
    for i, column in (
        (C_GAIN_E, gain_e),
        (C_SHIFT_E, shift_e),
        (C_BIAS_N, 0.5 * b_ni),
        (C_GAIN_N, gain_n),
        (C_SHIFT_N, shift_n),
        (C_VALID, jnp.where(inside, 1.0, 0.0)),
        (C_COUNT, jnp.full((D, LANES), (D * rows * n_lon * n_valid).astype(F32))),
    ):
        columns[i] = jnp.broadcast_to(column, (D, LANES))
    w_in = v_ei[...]
    w_e, w_s, w_r = w_in[:, :D], w_in[:, D : 2 * D], w_in[:, 2 * D :]
    a_edge = weight_pack(0.5 * w_e)
    a_state = jnp.concatenate([weight_pack(0.5 * w_s), weight_pack(0.5 * w_r)], axis=0)
    w_o = v_eo[...]
    w_oc = w_o - jnp.mean(w_o, axis=0, keepdims=True)
    b_oc = b_eo - jnp.mean(b_eo, axis=0, keepdims=True)
    back = 0.5 * exact(w_o, w_oc, ((0,), (0,)))
    b_back = 0.5 * exact(w_o, b_oc, ((0,), (0,)))
    w_n = v_ni[...]
    w_nt = w_n.T
    w_out = v_no[...]
    scaled = gain_e * w_nt[D:]
    scaled = scaled - jnp.mean(scaled, axis=0, keepdims=True)

    def put(place, *parts):
        value = jnp.concatenate(parts, axis=0) if len(parts) > 1 else parts[0]
        pack[place[0] : place[1], : value.shape[1]] = value

    put(P_HIDDEN, weight_pack(w_oc, b_oc), weight_pack(back, b_back))
    put(P_EDGE_T, weight_pack(w_e.T))
    put(P_SEND_T, weight_pack(w_s.T))
    put(P_RECV_T, weight_pack(w_r.T))
    put(P_NODE_IN, weight_pack(0.5 * w_n))
    put(
        P_NODE_OUT,
        weight_pack(
            w_out - jnp.mean(w_out, axis=0, keepdims=True),
            b_no - jnp.mean(b_no, axis=0, keepdims=True),
        ),
    )
    put(P_NODE_OUT_T, weight_pack(0.5 * w_out.T))
    put(
        P_NODE_IN_T,
        weight_pack(w_nt),
        weight_pack(scaled),
        weight_pack(0.5 * exact(w_o, scaled, ((0,), (0,)))),
    )
    pltpu.make_async_copy(pack, pack_out, out_sem).start()

    total = jnp.zeros((D, LANES), F32)
    west_tile = jnp.zeros((D, LANES), F32)
    east_tile = jnp.zeros((D, LANES), F32)
    half_bias = 0.5 * b_ei

    def project(t, value):
        high, low = halves(value)
        both = mxu(a_state, jnp.concatenate([high, low, high], axis=0))
        send = both[:D]
        windows[t, 1] = send
        windows[t, 0] = jnp.where(lane == 0, 0.0, pltpu.roll(send, 1, 1))
        windows[t, 2] = jnp.where(lane == LANES - 1, 0.0, pltpu.roll(send, LANES - 1, 1))
        return both[D:] + half_bias

    for g in range(n_groups):
        waits(buf.at[pl.ds(g * group, group)], in_sem.at[g])

        def state_row(i, carry, g=g):
            total, west_tile, east_tile = carry
            r = g * group + i
            mean_r = buf[r, 1]
            logstd_r = buf[r, 2]
            spread = jnp.exp(logstd_r)
            value = buf[r, 0] + mean_r + spread * buf[r, 3]
            state[r + 1] = value
            term = mean_r * mean_r + spread * spread - 1.0 - 2.0 * logstd_r
            total += jnp.where(inside, term, 0.0)
            moved = pltpu.roll(value, r + 1, 1)
            west_tile = jnp.where(lane == r + 1, moved, west_tile)
            east_tile = jnp.where(lane == r, moved, east_tile)
            receiver[r] = project(r + 1, value)
            return total, west_tile, east_tile

        def state_rows(i, carry):
            return state_row(2 * i + 1, state_row(2 * i, carry))

        total, west_tile, east_tile = lax.fori_loop(
            0, group // 2, state_rows, (total, west_tile, east_tile)
        )
    tiles[0] = state[1]
    tiles[1] = state[rows]
    tiles[2] = west_tile
    tiles[3] = east_tile
    columns[C_DIVERGED] = jnp.broadcast_to(
        0.5 * jnp.sum(total, axis=1, keepdims=True), (D, LANES)
    )
    pltpu.make_async_copy(columns, columns_out, out_sem).start()

    waits(nb.at[:, pl.ds(0, NBR), :], slot_sem)
    waits(mk.at[:, pl.ds(0, NBR), :], slot_sem)
    before = counts[lax.rem(blk + n_blk - 1, n_blk)]
    after = counts[lax.rem(blk + 1, n_blk)]
    lane8 = lane_ids(8)
    used = lax.broadcasted_iota(jnp.int32, (8, LANES), 0) < NBR

    def slots(r, _):
        above = jnp.where(r == 0, before, count)
        below = jnp.where(r == rows - 1, after, count)
        delta = nb[r] - (r * (LANES + 2) + lane8)
        first = delta < LANES + 2
        middle = delta < 2 * (LANES + 2)
        step = jnp.where(
            first, delta, jnp.where(middle, delta - (LANES + 2), delta - 2 * (LANES + 2))
        )
        code = jnp.where(first, step, jnp.where(middle, 3 + (step >> 1), 5 + step))
        owner = lane8 + step - 1
        owner = jnp.where(owner < 0, LANES - 1, jnp.where(owner >= LANES, 0, owner))
        limit = jnp.where(first, above, jnp.where(middle, count, below))
        codes[r] = jnp.where(used, code, 0)
        valid[r] = jnp.where(
            used & (lane8 < count) & (owner < limit), mk[r].astype(F32), 0.0
        )

    lax.fori_loop(0, rows, slots, None)
    pltpu.make_async_copy(codes, codes_out, out_sem).start()
    pltpu.make_async_copy(valid, valid_out, out_sem).start()

    def edge_row(r):
        waits(xb.at[r], edge_sem.at[r])
        for k in range(NBR):
            s = pl.ds(k * LANES, LANES)
            high, low = halves(xb[r, :, s])
            split[r, :D, s] = high
            split[r, D:, s] = low
        own = receiver[r]
        for pair in range(NBR // 2):
            s = pl.ds(pair * 2 * LANES, 2 * LANES)
            high = split[r, :D, s]
            out = mxu(a_edge, jnp.concatenate([high, split[r, D:, s], high], axis=0))
            from_edge[r, :, s] = out + jnp.concatenate([own, own], axis=1)
        pltpu.make_async_copy(split.at[r], split_out.at[r], out_sem).start()
        pltpu.make_async_copy(from_edge.at[r], from_edge_out.at[r], out_sem).start()

    def edge_rows(i, _):
        for u in range(2):
            load_edges(2 * i + u + ahead)
            edge_row(2 * i + u)

    def last_rows(i, _):
        for u in range(2):
            edge_row(2 * i + u)

    pause = (rows - ahead) // 2
    lax.fori_loop(0, pause, edge_rows, None)

    pl.semaphore_wait(barrier, 8)
    copies = []
    for slot, (place, tile) in enumerate(zip(around, (0, 1, 2, 3, 0, 0, 1, 1))):
        copies.append(
            pltpu.make_async_remote_copy(
                src_ref=tiles.at[tile],
                dst_ref=landing.at[slot],
                send_sem=send_sem.at[slot],
                recv_sem=recv_sem.at[slot],
                device_id=place,
                device_id_type=MESH,
            )
        )
        copies[-1].start()
    lax.fori_loop(pause, rows // 2, last_rows, None)

    for copy in copies:
        copy.wait()
    state[rows + 1] = landing[0]
    state[0] = landing[1]
    corner = lambda slot, at, to: jnp.where(
        lane == to, pltpu.roll(landing[slot], (to - at) % LANES, 1), 0.0
    )
    cols[1] = (
        pltpu.roll(jnp.where((lane >= 1) & (lane <= rows), landing[2], 0.0), LANES - 1, 1)
        + corner(4, 0, rows)
        + corner(6, 0, LANES - 1)
    )
    cols[0] = (
        pltpu.roll(jnp.where(lane < rows, landing[3], 0.0), 1, 1)
        + corner(5, LANES - 1, rows + 1)
        + corner(7, LANES - 1, 0)
    )
    pltpu.make_async_copy(state, state_out, out_sem).start()
    pltpu.make_async_copy(cols, cols_out, out_sem).start()
    project(0, state[0])
    project(rows + 1, state[rows + 1])
    sides = []
    for i in range(2):
        high, low = halves(cols[i])
        sides.append(mxu(a_state[:D], jnp.concatenate([high, low, high], axis=0)))

    def fix(t, _):
        mix = pltpu.roll(
            jnp.where(lane == t, sides[0], sides[1]), lax.rem(LANES - t, LANES), 1
        )
        windows[t, 0] += jnp.where(lane == 0, mix, 0.0)
        windows[t, 2] += jnp.where(lane == LANES - 1, mix, 0.0)
        pltpu.make_async_copy(windows.at[t], windows_out.at[t], out_sem).start()

    lax.fori_loop(0, (rows + 2) // 2, lambda i, _: (fix(2 * i, _), fix(2 * i + 1, _))[0], None)
    for ref in (pack, columns, codes, valid, split, from_edge, state, cols, windows):
        waits(ref, out_sem)


def start_call(n_blk, n_lon, counts, nodes, mean, logstd, noise, edges, neighbors, mask, weights):
    rows = nodes.shape[1]
    wide = NBR * LANES
    tile = (D, LANES)
    shapes = (
        ((rows + 2, *tile), F32),
        ((2, *tile), F32),
        ((rows + 2, 3, *tile), F32),
        ((rows, D, wide), F32),
        ((rows, 2 * D, wide), BF16),
        ((rows, 8, LANES), jnp.int32),
        ((rows, 8, LANES), F32),
        ((P_ROWS, P_LANES), BF16),
        ((8, *tile), F32),
    )
    vmem = lambda *dims: pltpu.VMEM(dims, F32)
    return pl.pallas_call(
        functools.partial(start_kernel, n_blk, n_lon),
        name="start",
        out_shape=[jax.ShapeDtypeStruct(*shape) for shape in shapes],
        in_specs=[SMEM] + [HBM] * (7 + len(weights)),
        out_specs=[HBM] * len(shapes),
        scratch_shapes=[
            vmem(rows, 4, *tile),
            vmem(rows + 2, *tile),
            vmem(rows + 2, 3, *tile),
            vmem(rows, D, wide),
            vmem(rows, D, wide),
            pltpu.VMEM((rows, 2 * D, wide), BF16),
            vmem(rows, *tile),
            pltpu.VMEM((rows, 8, LANES), jnp.int32),
            pltpu.VMEM((rows, 8, LANES), jnp.int32),
            pltpu.VMEM((rows, 8, LANES), jnp.int32),
            vmem(rows, 8, LANES),
            vmem(D, 3 * D),
            vmem(D, D),
            vmem(D, 2 * D),
            vmem(D, D),
            vmem(8, 1, D),
            pltpu.VMEM((P_ROWS, P_LANES), BF16),
            vmem(8, *tile),
            vmem(2, *tile),
            vmem(4, *tile),
            vmem(8, *tile),
            pltpu.SemaphoreType.DMA((4,)),
            pltpu.SemaphoreType.DMA((rows,)),
            pltpu.SemaphoreType.DMA,
            pltpu.SemaphoreType.DMA,
            pltpu.SemaphoreType.DMA((8,)),
            pltpu.SemaphoreType.DMA((8,)),
            pltpu.SemaphoreType.DMA,
        ],
        compiler_params=pltpu.CompilerParams(
            collective_id=0, has_side_effects=True, vmem_limit_bytes=ROOM
        ),
    )(counts, nodes, mean, logstd, noise, edges, neighbors, mask, *weights)


def layer_kernel(
    cotangent,
    windows_in,
    from_edge_in,
    split_in,
    codes_in,
    valid_in,
    pack_in,
    columns_in,
    state_in,
    new_states,
    grad_edges,
    part_out,
    recv_out,
    placed_out,
    acc_out,
    slope,
    xs,
    hs,
    cb,
    db,
    windows,
    codes,
    valid,
    pack,
    columns,
    state,
    inverse,
    summed,
    qc_ref,
    qo_ref,
    cot,
    fresh,
    part,
    placed,
    grad_recv,
    gather_grads,
    acc_edge,
    acc_hidden,
    acc_nin,
    acc_nout,
    acc_vec,
    acc,
    row_sem,
    in_sem,
    split_sem,
    out_sem,
):
    rows = cotangent.shape[1]
    wide = NBR * LANES
    two = 2 * LANES
    lane = lane_ids()

    for source, target in (
        (codes_in, codes),
        (valid_in, valid),
        (pack_in, pack),
        (columns_in, columns),
    ):
        pltpu.make_async_copy(source, target, in_sem.at[0]).start()
    n_groups = row_sem.shape[0]
    group = rows // n_groups
    spans = []
    for g in range(n_groups):
        span = pl.ds(g * group, group)
        first = 0 if g == 0 else g * group + 2
        last = (g + 1) * group + 2
        spans.append((span, pl.ds(first, last - first)))
        pltpu.make_async_copy(
            windows_in.at[spans[g][1]], windows.at[spans[g][1]], row_sem.at[g]
        ).start()
        pltpu.make_async_copy(from_edge_in.at[span], slope.at[span], row_sem.at[g]).start()
    pltpu.make_async_copy(state_in, state, in_sem.at[1]).start()

    def load_cot(r, _):
        pltpu.make_async_copy(cotangent.at[:, r, :], cot.at[r], in_sem.at[1]).start()

    lax.fori_loop(0, rows, load_cot, None)
    pltpu.make_async_copy(split_in, xs, split_sem).start()

    ones16 = jnp.where(
        lax.broadcasted_iota(jnp.int32, (16, wide), 0) < 2, 1.0, 0.0
    ).astype(BF16)
    ones_two = ones16[:, :two]
    for ref in (codes, valid, pack, columns):
        waits(ref, in_sem.at[0])

    def hidden_unit(r, pair):
        slots = (2 * pair, 2 * pair + 1)
        hidden = {k: [None] * 8 for k in slots}
        masks = {}
        for k in slots:
            code = jnp.broadcast_to(codes[r, pl.ds(k, 1), :], (8, LANES))
            masks[k] = ((code & 1) != 0, (code & 2) != 0, (code & 4) != 0)
        for f in range(8):
            rows_f = pl.ds(8 * f, 8)
            w = [windows[r + 1 + dr, 1 + dc, rows_f, :] for dr, dc in WINDOWS]
            for k in slots:
                s = pl.ds(k * LANES, LANES)
                b0, b1, b2 = masks[k]
                low = jnp.where(b1, jnp.where(b0, w[3], w[2]), jnp.where(b0, w[1], w[0]))
                top = jnp.where(b1, jnp.where(b0, w[7], w[6]), jnp.where(b0, w[5], w[4]))
                pre = slope[r, rows_f, s] + jnp.where(b2, top, low)
                t = jnp.tanh(pre)
                u = 1.0 + t
                h = pre * u
                slope[r, rows_f, s] = u + h * (1.0 - t)
                hidden[k][f] = h
        s = pl.ds(pair * two, two)
        high, low = halves(
            jnp.concatenate([jnp.concatenate(hidden[k], axis=0) for k in slots], axis=1)
        )
        hs[r, :D, s] = high
        hs[r, D : 2 * D, s] = low
        hs[r, 2 * D :, s] = ones_two
        return mxu(
            packed_rows(pack, P_HIDDEN, 3 * D + 16),
            jnp.concatenate([high, low, ones_two, high], axis=0),
        )

    def norm_unit(r, pair, both, total):
        s = pl.ds(pair * two, two)
        cb[r, :, s] = both[:D]
        db[r, :, s] = both[D:]
        for j in range(2):
            k = 2 * pair + j
            c = both[:D, j * LANES : (j + 1) * LANES]
            variance = jnp.sum(c * c, axis=0, keepdims=True) * (1.0 / D)
            inv = lax.rsqrt(variance + EPS)
            inverse[r, pl.ds(k, 1), :] = inv
            total = total + (inv * valid[r, pl.ds(k, 1), :]) * c
        if pair == NBR // 2 - 1:
            summed[r] = total
            total = jnp.zeros((D, LANES), F32)
        return total

    def forward(i, _, unroll=2):
        units = [(unroll * i + u, pair) for u in range(unroll) for pair in range(NBR // 2)]
        total = jnp.zeros((D, LANES), F32)
        pending = None
        for unit in units:
            both = hidden_unit(*unit)
            if pending is not None:
                total = norm_unit(*pending, total)
            pending = (*unit, both)
        norm_unit(*pending, total)

    for g in range(n_groups):
        waits(slope.at[spans[g][0]], row_sem.at[g])
        waits(windows.at[spans[g][1]], row_sem.at[g])
        lax.fori_loop(g * group // 2, (g + 1) * group // 2, forward, None)

    for ref in (acc_edge, acc_hidden, acc_nin, acc_nout, acc_vec, placed):
        ref[...] = jnp.zeros_like(ref)
    waits(cot, in_sem.at[1])
    waits(state, in_sem.at[1])
    chunk = 4

    def node_chunk(first):
        tile_cols = lambda i: jnp.concatenate([columns[i]] * chunk, axis=1)
        spread = lambda ref, offset: jnp.concatenate(
            [ref[first + offset + j] for j in range(chunk)], axis=1
        )
        st = spread(state, 1)
        total = spread(summed, 0)
        degree = jnp.concatenate(
            [jnp.sum(valid[first + j], axis=0, keepdims=True) for j in range(chunk)], axis=1
        )
        incoming = tile_cols(C_GAIN_E) * total + tile_cols(C_SHIFT_E) * degree
        st_high, st_low = halves(st)
        inc_high, inc_low = halves(incoming)
        tops = jnp.concatenate([st_high, inc_high], axis=0)
        ends = jnp.concatenate([st_low, inc_low], axis=0)
        pre = mxu(
            packed_rows(pack, P_NODE_IN, 6 * D), jnp.concatenate([tops, ends, tops], axis=0)
        ) + tile_cols(C_BIAS_N)
        yield
        t = jnp.tanh(pre)
        u = 1.0 + t
        h = pre * u
        slope_n = u + h * (1.0 - t)
        h_high, h_low = halves(h)
        h_all = jnp.concatenate([h_high, h_low, ones16[:, : chunk * LANES]], axis=0)
        c = mxu(
            packed_rows(pack, P_NODE_OUT, 3 * D + 16),
            jnp.concatenate([h_all, h_high], axis=0),
        )
        yield
        cot_c = spread(cot, 0)
        inv = lax.rsqrt(jnp.sum(c * c, axis=0, keepdims=True) * (1.0 / D) + EPS)
        n = c * inv
        new = st + (tile_cols(C_GAIN_N) * n + tile_cols(C_SHIFT_N))
        q = cot_c * tile_cols(C_GAIN_N)
        q = q - jnp.sum(q, axis=0, keepdims=True) * (1.0 / D)
        grad = inv * (q - n * (jnp.sum(q * n, axis=0, keepdims=True) * (1.0 / D)))
        g_high, g_low = halves(grad)
        pre_grad = mxu(
            packed_rows(pack, P_NODE_OUT_T), jnp.concatenate([g_high, g_low, g_high], axis=0)
        )
        acc_nout[...] += outer(jnp.concatenate([g_high, g_low], axis=0), h_all)
        for j in range(chunk):
            s = slice(j * LANES, (j + 1) * LANES)
            fresh[first + j] = new[:, s]
            acc_vec[3] += cot_c[:, s] * n[:, s]
            acc_vec[4] += cot_c[:, s]
            pltpu.make_async_copy(
                fresh.at[first + j], new_states.at[:, first + j, :], out_sem
            ).start()
        yield
        pre_grad = pre_grad * slope_n
        p_high, p_low = halves(pre_grad)
        back = mxu(
            packed_rows(pack, P_NODE_IN_T), jnp.concatenate([p_high, p_low, p_high], axis=0)
        )
        acc_nin[...] += outer(
            jnp.concatenate([p_high, p_low], axis=0), jnp.concatenate([tops, ends], axis=0)
        )
        yield
        grad_incoming = back[D : 2 * D]
        for j in range(chunk):
            s = slice(j * LANES, (j + 1) * LANES)
            part[first + j] = cot_c[:, s] + back[:D, s]
            qc_ref[first + j] = back[2 * D : 3 * D, s]
            qo_ref[first + j] = back[3 * D :, s]
            acc_vec[0] += grad_incoming[:, s] * total[:, s]
            acc_vec[1] += grad_incoming[:, s] * degree[:, s]
            acc_vec[2] += pre_grad[:, s]

    def node(i, _):
        in_turn(node_chunk(2 * chunk * i), node_chunk(2 * chunk * i + chunk))

    lax.fori_loop(0, rows // (2 * chunk), node, None)
    pltpu.make_async_copy(part, part_out, out_sem).start()

    waits(xs, split_sem)

    def grad_unit(r, pair, u, received):
        qc = qc_ref[r]
        qo = qo_ref[r]
        hidden_grads, grads = [], []
        for k in (2 * pair, 2 * pair + 1):
            s = pl.ds(k * LANES, LANES)
            c = cb[r, :, s]
            inv = inverse[r, pl.ds(k, 1), :]
            alpha = inv * valid[r, pl.ds(k, 1), :]
            moment = jnp.sum(qc * c, axis=0, keepdims=True) * (1.0 / D)
            beta = alpha * inv * inv * moment
            hidden_grads.append(alpha * qc - beta * c)
            grad = (alpha * qo - beta * db[r, :, s]) * slope[r, :, s]
            grads.append(grad)
            received = grad if received is None else received + grad
        high, low = halves(jnp.concatenate(hidden_grads, axis=1))
        s = pl.ds(pair * two, two)
        gather_grads[u, :D, s] = high
        gather_grads[u, D : 2 * D, s] = low
        high, low = halves(jnp.concatenate(grads, axis=1))
        gather_grads[u, 2 * D : 3 * D, s] = high
        gather_grads[u, 3 * D :, s] = low
        ge = mxu(
            packed_rows(pack, P_EDGE_T), jnp.concatenate([high, low, high], axis=0)
        )
        return grads, received, ge

    def place_unit(r, pair, grads, ge):
        cb[r, :, pl.ds(pair * two, two)] = ge
        code = [
            jnp.broadcast_to(codes[r, pl.ds(k, 1), :], (8, LANES))
            for k in (2 * pair, 2 * pair + 1)
        ]
        for which, (dr, dc) in enumerate(WINDOWS):
            masks = [c == which for c in code]
            for f in range(8):
                rows_f = pl.ds(8 * f, 8)
                value = placed[r + 1 + dr, 1 + dc, rows_f, :]
                for j in range(2):
                    value += jnp.where(masks[j], grads[j][8 * f : 8 * f + 8], 0.0)
                placed[r + 1 + dr, 1 + dc, rows_f, :] = value

    def products(r, u):
        acc_hidden[...] += outer(gather_grads[u, : 2 * D], hs[r])
        acc_edge[...] += outer(gather_grads[u, 2 * D :], xs[r])

    def backward(i, _, unroll=2):
        pending = None
        for u in range(unroll):
            r = unroll * i + u
            received = None
            for pair in range(NBR // 2):
                grads, received, ge = grad_unit(r, pair, u, received)
                if pending is not None:
                    place_unit(*pending)
                pending = (r, pair, grads, ge)
                if pair == 0 and u > 0:
                    products(r - 1, u - 1)
            grad_recv[r] = received
        place_unit(*pending)
        products(unroll * i + unroll - 1, unroll - 1)
        for u in range(unroll):
            r = unroll * i + u
            pltpu.make_async_copy(grad_recv.at[r], recv_out.at[r], out_sem).start()
            pltpu.make_async_copy(placed.at[r], placed_out.at[r], out_sem).start()
            for k in range(NBR):
                pltpu.make_async_copy(
                    cb.at[r, :, pl.ds(k * LANES, LANES)], grad_edges.at[:, k, r, :], out_sem
                ).start()

    lax.fori_loop(0, rows // 2, backward, None)
    tail = pl.ds(rows, 2)
    pltpu.make_async_copy(placed.at[tail], placed_out.at[tail], out_sem).start()

    def folded(ref):
        half = ref[:D, : 2 * D] + ref[D:, : 2 * D]
        return half + pltpu.roll(half, D, 1)

    left = lane < D
    acc[0] = folded(acc_edge)
    acc[2] = (
        acc_nin[:D, : 2 * D]
        + acc_nin[D:, : 2 * D]
        + acc_nin[:D, 2 * D :]
        + acc_nin[D:, 2 * D :]
    )
    acc[3] = jnp.where(left, folded(acc_hidden), folded(acc_nout))
    ones_sum = lambda ref: jnp.sum(
        jnp.where(lane[:, :16] == 0, ref[:D, 2 * D :] + ref[D:, 2 * D :], 0.0),
        axis=1,
        keepdims=True,
    )
    lane_sum = lambda i: jnp.sum(acc_vec[i], axis=1, keepdims=True)
    block = jnp.zeros((D, LANES), F32)
    for i, vector in (
        (1, ones_sum(acc_hidden)),
        (2, lane_sum(0)),
        (3, lane_sum(1)),
        (4, lane_sum(2)),
        (5, ones_sum(acc_nout)),
        (6, lane_sum(3)),
        (7, lane_sum(4)),
        (8, columns[C_DIVERGED]),
    ):
        block = jnp.where(lane == D + i, vector, block)
    acc[1] = block
    pltpu.make_async_copy(acc, acc_out, out_sem).start()
    for ref in (fresh, part, grad_recv, placed, cb, acc):
        waits(ref, out_sem)


def layer_call(cotangent, windows, from_edge, split, codes, valid, pack, columns, state):
    rows = cotangent.shape[1]
    wide = NBR * LANES
    tile = (D, LANES)
    shape = lambda *dims: jax.ShapeDtypeStruct(dims, F32)
    vmem = lambda *dims: pltpu.VMEM(dims, F32)
    return pl.pallas_call(
        layer_kernel,
        name="layer",
        out_shape=(
            shape(D, rows, LANES),
            shape(D, NBR, rows, LANES),
            shape(rows, *tile),
            shape(rows, *tile),
            shape(rows + 2, 3, *tile),
            shape(4, *tile),
        ),
        in_specs=[HBM] * 9,
        out_specs=[HBM] * 6,
        scratch_shapes=[
            vmem(rows, D, wide),
            pltpu.VMEM((rows, 2 * D, wide), BF16),
            pltpu.VMEM((rows, 2 * D + 16, wide), BF16),
            vmem(rows, D, wide),
            vmem(rows, D, wide),
            vmem(rows + 2, 3, *tile),
            pltpu.VMEM((rows, 8, LANES), jnp.int32),
            vmem(rows, 8, LANES),
            pltpu.VMEM((P_ROWS, P_LANES), BF16),
            vmem(8, *tile),
            vmem(rows + 2, *tile),
            vmem(rows, 8, LANES),
            vmem(rows, *tile),
            vmem(rows, *tile),
            vmem(rows, *tile),
            vmem(rows, *tile),
            vmem(rows, *tile),
            vmem(rows, *tile),
            vmem(rows + 2, 3, *tile),
            vmem(rows, *tile),
            pltpu.VMEM((2, 4 * D, wide), BF16),
            vmem(2 * D, 2 * D),
            vmem(2 * D, 2 * D + 16),
            vmem(2 * D, 4 * D),
            vmem(2 * D, 2 * D + 16),
            vmem(5, *tile),
            vmem(4, *tile),
            pltpu.SemaphoreType.DMA((4,)),
            pltpu.SemaphoreType.DMA((2,)),
            pltpu.SemaphoreType.DMA,
            pltpu.SemaphoreType.DMA,
        ],
        compiler_params=pltpu.CompilerParams(vmem_limit_bytes=ROOM),
    )(cotangent, windows, from_edge, split, codes, valid, pack, columns, state)


def sum_kernel(
    n_blk,
    n_lon,
    acc_in,
    placed_in,
    recv_in,
    part_in,
    state_in,
    cols_in,
    pack_in,
    part_out,
    total_out,
    halo_out,
    acc,
    placed,
    grad_recv,
    part,
    state,
    cols,
    pack,
    own,
    halo,
    acc_send,
    acc_recv,
    packed,
    scattered,
    across,
    gathered,
    landing,
    halo_in,
    in_sem,
    row_sem,
    rs_send,
    rs_recv,
    x_send,
    x_recv,
    ag_send,
    ag_recv,
    halo_send,
    halo_recv,
    out_sem,
):
    rows = recv_in.shape[0]
    blk, lon, around = neighbours(n_blk, n_lon)
    size = scattered.shape[0]
    n_groups = across.shape[0]
    per = size // n_lon
    me = lax.rem(blk, per) * n_lon + lon
    own_group = blk // per
    lane = lane_ids()

    def member(index):
        return (own_group * per + index // n_lon, lax.rem(index, n_lon))

    def other(step):
        return lax.rem(me + step, size)

    def peer(step):
        return (lax.rem(own_group + step, n_groups) * per + lax.rem(blk, per), lon)

    half = rows // 2
    for h in range(2):
        span = pl.ds(h * half, half)
        span3 = pl.ds(0, half + 1) if h == 0 else pl.ds(half + 1, half + 1)
        for source, target in (
            (placed_in.at[span3], placed.at[span3]),
            (state_in.at[span3], state.at[span3]),
            (recv_in.at[span], grad_recv.at[span]),
        ):
            pltpu.make_async_copy(source, target, row_sem.at[h]).start()
    small = (
        (pack_in.at[pl.ds(P_SEND_T[0], 2 * D)], pack),
        (cols_in, cols),
        (acc_in, acc),
        (part_in, part),
    )
    for i, (source, target) in enumerate(small):
        pltpu.make_async_copy(source, target, in_sem.at[i]).start()

    barrier = pltpu.get_barrier_semaphore()

    def greet(step, _):
        pl.semaphore_signal(
            barrier, inc=1, device_id=member(other(step)), device_id_type=MESH
        )

    lax.fori_loop(1, size, greet, None)
    expected = size - 1
    if n_groups > 1:
        for place in around:
            pl.semaphore_signal(barrier, inc=1, device_id=place, device_id_type=MESH)

        def greet_group(step, _):
            pl.semaphore_signal(barrier, inc=1, device_id=peer(step), device_id_type=MESH)

        lax.fori_loop(1, n_groups, greet_group, None)
        expected += 8 + n_groups - 1

    acc_send[...] = jnp.zeros_like(acc_send)
    acc_recv[...] = jnp.zeros_like(acc_recv)

    def settle(t, cells):
        west_cells, east_cells = cells
        to_west = placed[t, 0]
        to_east = placed[t, 2]
        value = (
            placed[t, 1]
            + jnp.where(lane == 0, 0.0, pltpu.roll(to_east, 1, 1))
            + jnp.where(lane == LANES - 1, 0.0, pltpu.roll(to_west, LANES - 1, 1))
        )
        own[t] = value
        mix = pltpu.roll(jnp.where(lane == 0, to_west, to_east), t, 1)
        west_cells = jnp.where(lane == t, mix, west_cells)
        east_cells = jnp.where(lane == lax.rem(t + LANES - 1, LANES), mix, east_cells)
        return value, (west_cells, east_cells)

    def both_halves(value):
        return jnp.concatenate(halves(value), axis=0)

    ones_row = jnp.where(
        lax.broadcasted_iota(jnp.int32, (16, 4 * LANES), 0) < 1, 1.0, 0.0
    ).astype(BF16)

    def collect(i, cells):
        values, there, received = [], [], []
        for u in range(4):
            t = 1 + 4 * i + u
            value, cells = settle(t, cells)
            values.append(value)
            there.append(state[t])
            received.append(grad_recv[t - 1])
        wide = lambda parts: both_halves(jnp.concatenate(parts, axis=1))
        there = wide(there)
        acc_send[...] += outer(wide(values), there)
        acc_recv[...] += outer(wide(received), jnp.concatenate([there, ones_row], axis=0))
        return cells

    zero = jnp.zeros((D, LANES), F32)
    for h in range(2):
        span = pl.ds(h * half, half)
        waits(placed.at[pl.ds(h * (half + 1), half + 1)], row_sem.at[h])
        waits(state.at[pl.ds(h * (half + 1), half + 1)], row_sem.at[h])
        waits(grad_recv.at[span], row_sem.at[h])
        if h == 0:
            _, cells = settle(0, (zero, zero))
        cells = lax.fori_loop(h * half // 4, (h + 1) * half // 4, collect, cells)
    _, cells = settle(rows + 1, cells)
    waits(cols, in_sem.at[1])
    edge_values = jnp.concatenate([own[0], own[rows + 1], cells[0], cells[1]], axis=1)
    edge_states = jnp.concatenate([state[0], state[rows + 1], cols[0], cols[1]], axis=1)
    acc_send[...] += outer(both_halves(edge_values), both_halves(edge_states))

    def folded(ref):
        part_sum = ref[:D, : 2 * D] + ref[D:, : 2 * D]
        return part_sum + pltpu.roll(part_sum, D, 1)

    left = lane < D
    waits(acc, in_sem.at[2])
    ones_sum = jnp.sum(
        jnp.where(lane[:, :16] == 0, acc_recv[:D, 2 * D :] + acc_recv[D:, 2 * D :], 0.0),
        axis=1,
        keepdims=True,
    )
    chunk = packed.shape[1]
    blocks = (
        jnp.where(left, acc[0], folded(acc_send)),
        jnp.where(left, folded(acc_recv), jnp.where(lane == D, ones_sum, acc[1])),
        acc[2],
        acc[3],
    )
    per_block = D // chunk
    for i, block in enumerate(blocks):
        for j in range(per_block):
            packed[i * per_block + j] = block[j * chunk : (j + 1) * chunk]
    pl.semaphore_wait(barrier, expected)

    def scatter(step, _):
        target = other(step)
        pltpu.make_async_remote_copy(
            src_ref=packed.at[target],
            dst_ref=scattered.at[me],
            send_sem=rs_send,
            recv_sem=rs_recv,
            device_id=member(target),
            device_id_type=MESH,
        ).start()

    lax.fori_loop(1, size, scatter, None)
    scattered[me] = packed[me]

    waits(pack, in_sem.at[0])
    a_send = pack[:D, : 3 * D]
    a_recv = pack[D : 2 * D, : 3 * D]
    high, low = halves(edge_values)
    edge_grads = mxu(a_send, jnp.concatenate([high, low, high], axis=0))
    for i in range(4):
        halo[i] = edge_grads[:, i * LANES : (i + 1) * LANES]
    copies = []
    for slot, (place, source) in enumerate(zip(around, (0, 1, 2, 3, 2, 3, 2, 3))):
        copies.append(
            pltpu.make_async_remote_copy(
                src_ref=halo.at[source],
                dst_ref=landing.at[slot],
                send_sem=halo_send.at[slot],
                recv_sem=halo_recv.at[slot],
                device_id=place,
                device_id_type=MESH,
            )
        )
        copies[-1].start()
    waits(part, in_sem.at[3])

    def finish(i, _):
        for u in range(2):
            first = 4 * i + 2 * u
            grads = None
            for weights, ref, offset in ((a_send, own, 1), (a_recv, grad_recv, 0)):
                high, low = halves(
                    jnp.concatenate([ref[first + offset], ref[first + offset + 1]], axis=1)
                )
                product = mxu(weights, jnp.concatenate([high, low, high], axis=0))
                grads = product if grads is None else grads + product
            for j in range(2):
                part[first + j] += grads[:, j * LANES : (j + 1) * LANES]

    lax.fori_loop(0, rows // 4, finish, None)
    pltpu.make_async_copy(part, part_out, out_sem).start()

    others = pl.ds(0, size - 1)
    waits(scattered.at[others], rs_recv)
    mine = scattered[0]
    for i in range(1, size):
        mine = mine + scattered[i]
    if n_groups > 1:
        across[own_group] = mine

        def cross(step, _):
            pltpu.make_async_remote_copy(
                src_ref=across.at[own_group],
                dst_ref=across.at[own_group],
                send_sem=x_send,
                recv_sem=x_recv,
                device_id=peer(step),
                device_id_type=MESH,
            ).start()

        lax.fori_loop(1, n_groups, cross, None)
        rest = pl.ds(0, n_groups - 1)
        waits(across.at[rest], x_recv)
        waits(across.at[rest], x_send)
        mine = across[0]
        for i in range(1, n_groups):
            mine = mine + across[i]
    gathered[me] = mine

    def gather(step, _):
        pltpu.make_async_remote_copy(
            src_ref=gathered.at[me],
            dst_ref=gathered.at[me],
            send_sem=ag_send,
            recv_sem=ag_recv,
            device_id=member(other(step)),
            device_id_type=MESH,
        ).start()

    lax.fori_loop(1, size, gather, None)
    for copy in copies:
        copy.wait()
    halo_in[0] = landing[1]
    halo_in[1] = landing[0]
    corner = lambda slot, at, to: jnp.where(
        lane == to, pltpu.roll(landing[slot], (to - at) % LANES, 1), 0.0
    )
    halo_in[2] = (
        pltpu.roll(jnp.where(lane < rows, landing[3], 0.0), 1, 1)
        + corner(7, rows, 1)
        + corner(5, LANES - 1, rows)
    )
    east_in = (
        jnp.where((lane >= 1) & (lane <= rows), landing[2], 0.0)
        + corner(6, rows + 1, 1)
        + corner(4, 0, rows)
    )
    halo_in[3] = pltpu.roll(east_in, LANES - 1, 1)
    pltpu.make_async_copy(halo_in, halo_out, out_sem).start()
    waits(gathered.at[others], ag_recv)
    pltpu.make_async_copy(gathered, total_out, out_sem).start()
    waits(scattered.at[others], rs_send)
    waits(gathered.at[others], ag_send)
    for ref in (part, halo_in, gathered):
        waits(ref, out_sem)


def sum_call(n_blk, n_lon, acc, placed, recv, part, state, cols, pack):
    rows = recv.shape[0]
    size = min(32, n_blk * n_lon)
    n_groups = n_blk * n_lon // size
    chunk = (4 * D // size, LANES)
    tile = (D, LANES)
    shape = lambda *dims: jax.ShapeDtypeStruct(dims, F32)
    vmem = lambda *dims: pltpu.VMEM(dims, F32)
    dma = pltpu.SemaphoreType.DMA
    return pl.pallas_call(
        functools.partial(sum_kernel, n_blk, n_lon),
        name="sums",
        out_shape=(shape(rows, *tile), shape(size, *chunk), shape(4, *tile)),
        in_specs=[HBM] * 7,
        out_specs=[HBM] * 3,
        scratch_shapes=[
            vmem(4, *tile),
            vmem(rows + 2, 3, *tile),
            vmem(rows, *tile),
            vmem(rows, *tile),
            vmem(rows + 2, *tile),
            vmem(2, *tile),
            pltpu.VMEM((2 * D, P_LANES), BF16),
            vmem(rows + 2, *tile),
            vmem(4, *tile),
            vmem(2 * D, 2 * D),
            vmem(2 * D, 2 * D + 16),
            vmem(size, *chunk),
            vmem(size, *chunk),
            vmem(n_groups, *chunk),
            vmem(size, *chunk),
            vmem(8, *tile),
            vmem(4, *tile),
            dma((4,)),
            dma((2,)),
            dma,
            dma,
            dma,
            dma,
            dma,
            dma,
            dma((8,)),
            dma((8,)),
            dma,
        ],
        compiler_params=pltpu.CompilerParams(
            collective_id=1, has_side_effects=True, vmem_limit_bytes=ROOM
        ),
    )(acc, placed, recv, part, state, cols, pack)


def final_kernel(
    kl_weight,
    part_nodes,
    mean,
    logstd,
    noise,
    total_in,
    halo_in,
    columns_in,
    grad_nodes,
    grad_mean,
    grad_logstd,
    kl_value,
    g_w_ei,
    g_w_eo,
    g_w_ni,
    g_w_no,
    *rest,
):
    g_vec = rest[:8]
    buf, out, total, halo, columns, in_sem, small_sem, out_sem = rest[8:]
    rows = mean.shape[1]
    lane = lane_ids()
    for i, (source, target) in enumerate(
        ((total_in, total), (halo_in, halo), (columns_in, columns))
    ):
        pltpu.make_async_copy(source, target, small_sem.at[i]).start()
    n_groups = in_sem.shape[0]
    group = rows // n_groups
    for g in range(n_groups):

        def load(i, _, g=g):
            r = g * group + i
            for which, source in enumerate((mean, logstd, noise)):
                pltpu.make_async_copy(
                    source.at[:, r, :], buf.at[r, which], in_sem.at[g]
                ).start()
            pltpu.make_async_copy(part_nodes.at[r], buf.at[r, 3], in_sem.at[g]).start()

        lax.fori_loop(0, group, load, None)
    waits(halo, small_sem.at[1])
    waits(columns, small_sem.at[2])
    inside = kl_weight[0] * columns[C_VALID]
    west_in = halo[2]
    east_in = halo[3]
    for g in range(n_groups):
        span = pl.ds(g * group, group)
        waits(buf.at[span], in_sem.at[g])

        def finish(i, _, g=g):
            for u in range(2):
                r = g * group + 2 * i + u
                mix = pltpu.roll(
                    jnp.where(lane == r + 1, west_in, east_in), LANES - 1 - r, 1
                )
                grad = buf[r, 3] + jnp.where((lane == 0) | (lane == LANES - 1), mix, 0.0)
                grad = grad + jnp.where(r == 0, 1.0, 0.0) * halo[0]
                grad = grad + jnp.where(r == rows - 1, 1.0, 0.0) * halo[1]
                spread = jnp.exp(buf[r, 1])
                out[r, 0] = grad
                out[r, 1] = grad + inside * buf[r, 0]
                out[r, 2] = grad * spread * buf[r, 2] + inside * (spread * spread - 1.0)
                for which, target in enumerate((grad_nodes, grad_mean, grad_logstd)):
                    pltpu.make_async_copy(
                        out.at[r, which], target.at[:, r, :], out_sem
                    ).start()

        lax.fori_loop(0, group // 2, finish, None)
    waits(total, small_sem.at[0])
    chunk = total.shape[1]
    per_block = D // chunk
    blocks = [
        jnp.concatenate([total[i * per_block + j] for j in range(per_block)], axis=0)
        for i in range(4)
    ]
    g_w_ei[:, : 2 * D] = blocks[0]
    g_w_ei[:, 2 * D :] = blocks[1][:, :D]
    g_w_ni[...] = blocks[2]
    g_w_eo[...] = blocks[3][:, :D]
    g_w_no[...] = pltpu.roll(blocks[3], D, 1)[:, :D]
    for i in range(8):
        g_vec[i][...] = to_row(blocks[1][:, D + i : D + i + 1])
    diverged = jnp.sum(blocks[1][:, D + 8 : D + 9], axis=0, keepdims=True)
    kl_value[...] = diverged / columns[C_COUNT][:1, :1]
    waits(out, out_sem)


def final_call(kl_weight, part_nodes, mean, logstd, noise, total, halo, columns):
    rows = mean.shape[1]
    tile = (D, LANES)
    shape = lambda *dims: jax.ShapeDtypeStruct(dims, F32)
    whole = shape(D, rows, LANES)
    return pl.pallas_call(
        final_kernel,
        name="final",
        out_shape=(
            whole,
            whole,
            whole,
            shape(1, 1),
            shape(D, 3 * D),
            shape(D, D),
            shape(D, 2 * D),
            shape(D, D),
        )
        + (shape(1, D),) * 8,
        in_specs=[SMEM] + [HBM] * 7,
        out_specs=[HBM] * 3 + [VMEM] * 13,
        scratch_shapes=[
            pltpu.VMEM((rows, 4, *tile), F32),
            pltpu.VMEM((rows, 3, *tile), F32),
            pltpu.VMEM(total.shape, F32),
            pltpu.VMEM((4, *tile), F32),
            pltpu.VMEM((8, *tile), F32),
            pltpu.SemaphoreType.DMA((4,)),
            pltpu.SemaphoreType.DMA((3,)),
            pltpu.SemaphoreType.DMA,
        ],
        compiler_params=pltpu.CompilerParams(vmem_limit_bytes=ROOM),
    )(kl_weight, part_nodes, mean, logstd, noise, total, halo, columns)


def shards(
    nodes,
    edges,
    latent_mean,
    latent_logstd,
    latent_noise,
    kl_weight,
    band_counts,
    neighbors,
    edge_mask,
    w_edge_in,
    b_edge_in,
    w_edge_out,
    b_edge_out,
    edge_gain,
    edge_shift,
    w_node_in,
    b_node_in,
    w_node_out,
    b_node_out,
    node_gain,
    node_shift,
    cotangent,
):
    n_blk = lax.axis_size("blk")
    n_lon = lax.axis_size("lon")
    vectors = (
        b_edge_in,
        b_edge_out,
        edge_gain,
        edge_shift,
        b_node_in,
        b_node_out,
        node_gain,
        node_shift,
    )
    weights = (w_edge_in, w_edge_out, w_node_in, w_node_out)
    weights += tuple(vector.reshape(1, D) for vector in vectors)
    state, cols, windows, from_edge, split, codes, valid, pack, columns = start_call(
        n_blk,
        n_lon,
        band_counts,
        nodes,
        latent_mean,
        latent_logstd,
        latent_noise,
        edges,
        neighbors,
        edge_mask,
        weights,
    )
    new_states, grad_edges, part, recv, placed, acc = layer_call(
        cotangent, windows, from_edge, split, codes, valid, pack, columns, state
    )
    part, total, halo = sum_call(n_blk, n_lon, acc, placed, recv, part, state, cols, pack)
    grad_nodes, grad_mean, grad_logstd, kl_value, g_w_ei, g_w_eo, g_w_ni, g_w_no, *g_vec = (
        final_call(
            kl_weight,
            part,
            latent_mean,
            latent_logstd,
            latent_noise,
            total,
            halo,
            columns,
        )
    )
    g_vec = [vector.reshape(D) for vector in g_vec]
    return (
        new_states,
        kl_value.reshape(1),
        grad_nodes,
        grad_edges,
        grad_mean,
        grad_logstd,
        g_w_ei,
        g_vec[0],
        g_w_eo,
        g_vec[1],
        g_vec[2],
        g_vec[3],
        g_w_ni,
        g_vec[4],
        g_w_no,
        g_vec[5],
        g_vec[6],
        g_vec[7],
    )


def solution(mesh):
    node = P(None, "blk", "lon")
    slot = P(None, None, "blk", "lon")
    return jax.shard_map(
        shards,
        mesh=mesh,
        in_specs=(
            (node, slot, node, node, node, P(), P(), node, node) + (P(),) * 12 + (node,)
        ),
        out_specs=(node, P(), node, slot, node, node) + (P(),) * 12,
        check_vma=False,
    )
```

```python
import functools

import jax
import jax.numpy as jnp
from jax import lax
from jax.experimental import pallas as pl
from jax.experimental.pallas import tpu as pltpu
from jax.sharding import PartitionSpec as P

F32 = jnp.float32
BF16 = jnp.bfloat16
MESH = pl.DeviceIdType.MESH
D = 64
LANES = 128
NBR = 6
EPS = 1e-05
HBM = pl.BlockSpec(memory_space=pltpu.HBM)
VMEM = pl.BlockSpec(memory_space=pltpu.VMEM)
ROOM = 62 * 2**20
SMEM = pl.BlockSpec(memory_space=pltpu.SMEM)

WINDOWS = ((-1, -1), (-1, 0), (-1, 1), (0, -1), (0, 1), (1, -1), (1, 0), (1, 1))


def halves(value):
    high = value.astype(BF16)
    return high, (value - high.astype(F32)).astype(BF16)


def weight_pack(weight, *biases):
    high, low = halves(weight)
    if not biases:
        return jnp.concatenate([high, high, low], axis=1)
    place = lax.broadcasted_iota(jnp.int32, (weight.shape[0], 16), 1)
    wide = jnp.zeros((weight.shape[0], 16), F32)
    for i, bias in enumerate(biases):
        for j, part in enumerate(halves(bias)):
            wide = jnp.where(place == 2 * i + j, part.astype(F32), wide)
    return jnp.concatenate([high, high, wide.astype(BF16), low], axis=1)


def mxu(left, right):
    return jnp.dot(left, right, preferred_element_type=F32)


def outer(left, right):
    return lax.dot_general(
        left, right, (((1,), (1,)), ((), ())), preferred_element_type=F32
    )


def exact(left, right, dims):
    return lax.dot_general(
        left,
        right,
        (dims, ((), ())),
        precision=lax.Precision.HIGHEST,
        preferred_element_type=F32,
    )


def eye():
    return lax.broadcasted_iota(jnp.int32, (D, D), 0) == lax.broadcasted_iota(
        jnp.int32, (D, D), 1
    )


def to_column(row):
    return jnp.sum(jnp.where(eye(), row, 0.0), axis=1, keepdims=True)


def to_row(column):
    return jnp.sum(jnp.where(eye(), column, 0.0), axis=0, keepdims=True)


def waits(ref, sem):
    pltpu.make_async_copy(ref, ref, sem).wait()


def in_turn(*routines):
    waiting = list(routines)
    while waiting:
        for routine in list(waiting):
            if next(routine, routine) is routine:
                waiting.remove(routine)


def lane_ids(rows=D):
    return lax.broadcasted_iota(jnp.int32, (rows, LANES), 1)


P_HIDDEN, P_EDGE, P_EDGE_T, P_NODE_OUT = (0, 128), (128, 192), (192, 256), (256, 320)
P_NODE_OUT_T, P_NODE_IN_T, P_SEND_T, P_RECV_T = (320, 384), (384, 576), (576, 640), (640, 704)
P_NODE_IN, P_NODE_IN_END = (704, 768), (768, 832)
P_ROWS, P_LANES = 832, 256
C_GAIN_N, C_SHIFT_N, C_VALID, C_DIVERGED, C_COUNT, C_WEIGHT_N, C_ROWS = range(7)
C_TILES = 7


def packed_rows(ref, rows, lanes=3 * D):
    return ref[rows[0] : rows[1], :lanes]


def neighbours(n_blk, n_lon):
    blk = lax.axis_index("blk")
    lon = lax.axis_index("lon")
    up = lax.rem(blk + n_blk - 1, n_blk)
    down = lax.rem(blk + 1, n_blk)
    west = lax.rem(lon + n_lon - 1, n_lon)
    east = lax.rem(lon + 1, n_lon)
    around = (
        (up, lon),
        (down, lon),
        (blk, west),
        (blk, east),
        (up, west),
        (up, east),
        (down, west),
        (down, east),
    )
    return blk, lon, around


def start_kernel(
    n_blk,
    n_lon,
    counts,
    nodes,
    mean,
    logstd,
    noise,
    neighbors,
    edge_mask,
    w_ei,
    w_eo,
    w_ni,
    w_no,
    *rest,
):
    vectors = rest[:8]
    (
        state_out,
        cols_out,
        project_out,
        receive_out,
        sides_out,
        codes_out,
        valid_out,
        pack_out,
        columns_out,
        buf,
        state,
        projected,
        receiver,
        sides,
        nb,
        mk,
        codes,
        valid,
        v_ei,
        v_eo,
        v_ni,
        v_no,
        v_vec,
        pack,
        columns,
        cols,
        tiles,
        landing,
        in_sem,
        slot_sem,
        weight_sem,
        send_sem,
        recv_sem,
        out_sem,
    ) = rest[8:]
    rows = nodes.shape[1]
    blk, lon, around = neighbours(n_blk, n_lon)
    barrier = pltpu.get_barrier_semaphore()
    for place in around:
        pl.semaphore_signal(barrier, inc=1, device_id=place, device_id_type=MESH)

    n_groups = in_sem.shape[0]
    group = rows // n_groups

    def load_row(g, i):
        r = g * group + i
        for which, source in enumerate((nodes, mean, logstd, noise)):
            pltpu.make_async_copy(source.at[:, r, :], buf.at[r, which], in_sem.at[g]).start()

    for g in range(2):
        for i in range(group):
            load_row(g, i)
    weights = [(w_ei, v_ei), (w_eo, v_eo), (w_ni, v_ni), (w_no, v_no)]
    weights += [(vectors[i], v_vec.at[i]) for i in range(8)]
    lane = lane_ids()
    count = counts[blk]
    inside = lane < count

    def state_row(r, carry):
        total, west_tile, east_tile = carry
        mean_r = buf[r, 1]
        logstd_r = buf[r, 2]
        spread = jnp.exp(logstd_r)
        value = buf[r, 0] + mean_r + spread * buf[r, 3]
        state[r + 1] = value
        total += jnp.where(inside, mean_r * mean_r + spread * spread - 2.0 * logstd_r, 0.0)
        moved = pltpu.roll(value, r + 1, 1)
        west_tile = jnp.where(lane == r + 1, moved, west_tile)
        east_tile = jnp.where(lane == r, moved, east_tile)
        return total, west_tile, east_tile

    carry = (jnp.zeros((D, LANES), F32),) * 3
    for g in range(n_groups):
        if g == 2:
            for source, target in weights:
                pltpu.make_async_copy(source, target, weight_sem).start()
        waits(buf.at[pl.ds(g * group, group)], in_sem.at[g])

        def state_rows(i, carry, g=g):
            for u in range(2):
                if g + 2 < n_groups:
                    load_row(g + 2, 2 * i + u)
                carry = state_row(g * group + 2 * i + u, carry)
            return carry

        carry = lax.fori_loop(0, group // 2, state_rows, carry)
    total, west_tile, east_tile = carry
    tiles[0] = state[1]
    tiles[1] = state[rows]
    tiles[2] = west_tile
    tiles[3] = east_tile

    pl.semaphore_wait(barrier, 8)
    copies = []
    for slot, (place, tile) in enumerate(zip(around, (0, 1, 2, 3, 0, 0, 1, 1))):
        copies.append(
            pltpu.make_async_remote_copy(
                src_ref=tiles.at[tile],
                dst_ref=landing.at[slot],
                send_sem=send_sem.at[slot],
                recv_sem=recv_sem.at[slot],
                device_id=place,
                device_id_type=MESH,
            )
        )
        copies[-1].start()

    pltpu.make_async_copy(neighbors, nb, slot_sem).start()
    pltpu.make_async_copy(edge_mask, mk, slot_sem).start()
    inner = pl.ds(1, rows)
    pltpu.make_async_copy(state.at[inner], state_out.at[inner], out_sem).start()

    for _, target in weights:
        waits(target, weight_sem)
    b_ei, b_eo, gain_e, shift_e, b_ni, b_no, gain_n, shift_n = [
        to_column(v_vec[i]) for i in range(8)
    ]
    n_valid = counts[0]
    for i in range(1, counts.shape[0]):
        n_valid += counts[i]
    for i, column in (
        (C_GAIN_N, gain_n),
        (C_SHIFT_N, shift_n),
        (C_VALID, jnp.where(inside, 1.0, 0.0)),
        (C_COUNT, jnp.full((D, LANES), (D * rows * n_lon * n_valid).astype(F32))),
        (
            C_DIVERGED,
            0.5 * jnp.sum(total - rows * jnp.where(inside, 1.0, 0.0), axis=1, keepdims=True),
        ),
    ):
        columns[i] = jnp.broadcast_to(column, (D, LANES))
    w_in = v_ei[...]
    w_e, w_s, w_r = w_in[:, :D], w_in[:, D : 2 * D], w_in[:, 2 * D :]
    a_state = jnp.concatenate([weight_pack(0.5 * w_s), weight_pack(0.5 * w_r)], axis=0)
    w_o = v_eo[...]
    w_oc = w_o - jnp.mean(w_o, axis=0, keepdims=True)
    b_oc = b_eo - jnp.mean(b_eo, axis=0, keepdims=True)
    back = 0.5 * exact(w_o, w_oc, ((0,), (0,)))
    b_back = 0.5 * exact(w_o, b_oc, ((0,), (0,)))
    w_n = v_ni[...]
    w_nt = w_n.T
    gain_row, shift_row = v_vec[2], v_vec[3]
    one_row = jnp.ones_like(gain_row)
    scale_row = jnp.concatenate([one_row, gain_row], axis=1)
    add_row = jnp.concatenate([0.0 * one_row, shift_row], axis=1)
    columns[C_WEIGHT_N] = w_n
    row_id = lax.broadcasted_iota(jnp.int32, (D, LANES), 0)
    columns[C_ROWS] = jnp.where(row_id == 0, scale_row, jnp.where(row_id == 1, add_row, 0.0))
    w_shift = jnp.sum(w_n * add_row, axis=1, keepdims=True)
    w_out = v_no[...]
    scaled = gain_e * w_nt[D:]
    scaled = scaled - jnp.mean(scaled, axis=0, keepdims=True)

    def put(place, *parts):
        value = jnp.concatenate(parts, axis=0) if len(parts) > 1 else parts[0]
        pack[place[0] : place[1], : value.shape[1]] = value

    put(P_EDGE, weight_pack(0.5 * w_e))
    put(P_HIDDEN, weight_pack(w_oc, b_oc), weight_pack(back, b_back))
    put(P_EDGE_T, weight_pack(w_e.T))
    put(P_SEND_T, weight_pack(w_s.T))
    put(P_RECV_T, weight_pack(w_r.T))
    node_in = weight_pack(0.5 * w_n * scale_row, 0.5 * b_ni, 0.5 * w_shift)
    put(P_NODE_IN, node_in[:, :P_LANES])
    put(P_NODE_IN_END, node_in[:, P_LANES:])
    put(
        P_NODE_OUT,
        weight_pack(
            w_out - jnp.mean(w_out, axis=0, keepdims=True),
            b_no - jnp.mean(b_no, axis=0, keepdims=True),
        ),
    )
    put(P_NODE_OUT_T, weight_pack(0.5 * w_out.T))
    put(
        P_NODE_IN_T,
        weight_pack(w_nt[:D]),
        weight_pack(scaled),
        weight_pack(0.5 * exact(w_o, scaled, ((0,), (0,)))),
    )
    pltpu.make_async_copy(pack, pack_out, out_sem).start()
    pltpu.make_async_copy(columns, columns_out, out_sem).start()

    waits(nb, slot_sem)
    waits(mk, slot_sem)
    before = counts[lax.rem(blk + n_blk - 1, n_blk)]
    after = counts[lax.rem(blk + 1, n_blk)]
    row_id = lax.broadcasted_iota(jnp.int32, (rows, LANES), 0)
    col_id = lax.broadcasted_iota(jnp.int32, (rows, LANES), 1)
    above = jnp.where(row_id == 0, before, count)
    below = jnp.where(row_id == rows - 1, after, count)
    for k in range(NBR):
        delta = nb[k] - (row_id * (LANES + 2) + col_id)
        first = delta < LANES + 2
        middle = delta < 2 * (LANES + 2)
        step = jnp.where(
            first, delta, jnp.where(middle, delta - (LANES + 2), delta - 2 * (LANES + 2))
        )
        codes[k] = jnp.where(first, step, jnp.where(middle, 3 + (step >> 1), 5 + step))
        owner = col_id + step - 1
        owner = jnp.where(owner < 0, LANES - 1, jnp.where(owner >= LANES, 0, owner))
        limit = jnp.where(first, above, jnp.where(middle, count, below))
        valid[k] = jnp.where((col_id < count) & (owner < limit), mk[k].astype(F32), 0.0)
    for k in range(NBR, 8):
        codes[k] = jnp.zeros((rows, LANES), jnp.int32)
        valid[k] = jnp.zeros((rows, LANES), F32)
    for k in range(8):
        pltpu.make_async_copy(codes.at[k], codes_out.at[:, k, :], out_sem).start()
        pltpu.make_async_copy(valid.at[k], valid_out.at[:, k, :], out_sem).start()

    half_bias = 0.5 * b_ei

    def project(i, _):
        high, low = halves(
            jnp.concatenate([state[1 + 4 * i + u] for u in range(4)], axis=1)
        )
        both = mxu(a_state, jnp.concatenate([high, low, high], axis=0))
        for u in range(4):
            s = slice(u * LANES, (u + 1) * LANES)
            projected[1 + 4 * i + u] = both[:D, s]
            receiver[4 * i + u] = both[D:, s] + half_bias

    lax.fori_loop(0, rows // 4, project, None)
    pltpu.make_async_copy(projected.at[inner], project_out.at[inner], out_sem).start()
    pltpu.make_async_copy(receiver, receive_out, out_sem).start()

    for copy in copies:
        copy.wait()
    state[rows + 1] = landing[0]
    state[0] = landing[1]
    corner = lambda slot, at, to: jnp.where(
        lane == to, pltpu.roll(landing[slot], (to - at) % LANES, 1), 0.0
    )
    cols[1] = (
        pltpu.roll(jnp.where((lane >= 1) & (lane <= rows), landing[2], 0.0), LANES - 1, 1)
        + corner(4, 0, rows)
        + corner(6, 0, LANES - 1)
    )
    cols[0] = (
        pltpu.roll(jnp.where(lane < rows, landing[3], 0.0), 1, 1)
        + corner(5, LANES - 1, rows + 1)
        + corner(7, LANES - 1, 0)
    )
    high, low = halves(
        jnp.concatenate([landing[1], landing[0], cols[0], cols[1]], axis=1)
    )
    rim = mxu(a_state[:D], jnp.concatenate([high, low, high], axis=0))
    projected[0] = rim[:, :LANES]
    projected[rows + 1] = rim[:, LANES : 2 * LANES]
    sides[0] = rim[:, 2 * LANES : 3 * LANES]
    sides[1] = rim[:, 3 * LANES :]
    for t in (0, rows + 1):
        pltpu.make_async_copy(projected.at[t], project_out.at[t], out_sem).start()
        pltpu.make_async_copy(state.at[t], state_out.at[t], out_sem).start()
    pltpu.make_async_copy(sides, sides_out, out_sem).start()
    pltpu.make_async_copy(cols, cols_out, out_sem).start()
    for ref in (pack, columns, codes, valid, receiver, state, projected, cols, sides):
        waits(ref, out_sem)


def start_call(n_blk, n_lon, counts, nodes, mean, logstd, noise, neighbors, mask, weights):
    rows = nodes.shape[1]
    tile = (D, LANES)
    shapes = (
        ((rows + 2, *tile), F32),
        ((2, *tile), F32),
        ((rows + 2, *tile), F32),
        ((rows, *tile), F32),
        ((2, *tile), F32),
        ((rows, 8, LANES), jnp.int32),
        ((rows, 8, LANES), F32),
        ((P_ROWS, P_LANES), BF16),
        ((C_TILES, *tile), F32),
    )
    vmem = lambda *dims: pltpu.VMEM(dims, F32)
    ints = lambda *dims: pltpu.VMEM(dims, jnp.int32)
    dma = pltpu.SemaphoreType.DMA
    return pl.pallas_call(
        functools.partial(start_kernel, n_blk, n_lon),
        name="start",
        out_shape=[jax.ShapeDtypeStruct(*shape) for shape in shapes],
        in_specs=[SMEM] + [HBM] * (6 + len(weights)),
        out_specs=[HBM] * len(shapes),
        scratch_shapes=[
            vmem(rows, 4, *tile),
            vmem(rows + 2, *tile),
            vmem(rows + 2, *tile),
            vmem(rows, *tile),
            vmem(2, *tile),
            ints(NBR, rows, LANES),
            ints(NBR, rows, LANES),
            ints(8, rows, LANES),
            vmem(8, rows, LANES),
            vmem(D, 3 * D),
            vmem(D, D),
            vmem(D, 2 * D),
            vmem(D, D),
            vmem(8, 1, D),
            pltpu.VMEM((P_ROWS, P_LANES), BF16),
            vmem(C_TILES, *tile),
            vmem(2, *tile),
            vmem(4, *tile),
            vmem(8, *tile),
            dma((4,)),
            dma,
            dma,
            dma((8,)),
            dma((8,)),
            dma,
        ],
        compiler_params=pltpu.CompilerParams(
            collective_id=0, has_side_effects=True, vmem_limit_bytes=ROOM
        ),
    )(counts, nodes, mean, logstd, noise, neighbors, mask, *weights)


def layer_kernel(
    edges,
    cotangent,
    project_in,
    receive_in,
    sides_in,
    codes_in,
    valid_in,
    pack_in,
    columns_in,
    state_in,
    new_states,
    grad_edges,
    part_out,
    recv_out,
    placed_out,
    acc_out,
    slope,
    xs,
    hs,
    cb,
    db,
    staged,
    windows,
    projected,
    receiver,
    sides,
    codes,
    valid,
    pack,
    columns,
    state,
    inverse,
    summed,
    qc_ref,
    qo_ref,
    cot,
    fresh,
    part,
    placed,
    grad_recv,
    gather_grads,
    acc_edge,
    acc_hidden,
    acc_nin,
    acc_nout,
    acc_vec,
    acc,
    row_sem,
    edge_sem,
    in_sem,
    out_sem,
):
    rows = cotangent.shape[1]
    wide = NBR * LANES
    two = 2 * LANES
    lane = lane_ids()

    halfway = 14
    ahead = 8

    def load_edges(r):
        for k in range(NBR):
            pltpu.make_async_copy(
                edges.at[:, k, r, :],
                staged.at[r, :, pl.ds(k * LANES, LANES)],
                edge_sem.at[r],
            ).start()

    first_weights = pl.ds(P_HIDDEN[0], P_EDGE[1])
    first_small = (
        (sides_in, sides),
        (pack_in.at[first_weights], pack.at[first_weights]),
        (codes_in, codes),
        (valid_in, valid),
    )
    parts = []
    for g, (first, last) in enumerate(((0, halfway), (halfway, rows + 2))):
        send, receive = pl.ds(first, last - first), pl.ds(first, min(last, rows) - first)
        part_g = ((project_in, projected, send), (receive_in, receiver, receive))
        for source, target, span in part_g:
            pltpu.make_async_copy(source.at[span], target.at[span], row_sem.at[g]).start()
        parts.append([target.at[span] for _, target, span in part_g])
        if g == 0:
            for source, target in first_small[:2]:
                pltpu.make_async_copy(source, target, in_sem.at[0]).start()
            for r in range(4):
                load_edges(r)
            for source, target in first_small[2:]:
                pltpu.make_async_copy(source, target, in_sem.at[0]).start()
    for r in range(4, ahead + 2):
        load_edges(r)

    def load_rest():
        rest = pl.ds(P_EDGE[1], P_ROWS - P_EDGE[1])
        pltpu.make_async_copy(pack_in.at[rest], pack.at[rest], in_sem.at[1]).start()
        pltpu.make_async_copy(columns_in, columns, in_sem.at[1]).start()
        pltpu.make_async_copy(state_in, state, in_sem.at[1]).start()

        def load_cot(r, _):
            pltpu.make_async_copy(cotangent.at[:, r, :], cot.at[r], in_sem.at[1]).start()

        lax.fori_loop(0, rows, load_cot, None)
        return (cot, state, columns, pack.at[rest])

    ones16 = jnp.where(
        lax.broadcasted_iota(jnp.int32, (16, wide), 0) < 2, 1.0, 0.0
    ).astype(BF16)
    ones_two = ones16[:, :two]
    for _, target in first_small:
        waits(target, in_sem.at[0])

    def shift(t):
        centre = projected[t]
        mix = pltpu.roll(
            jnp.where(lane == t, sides[0], sides[1]), lax.rem(LANES - t, LANES), 1
        )
        windows[t, 1] = centre
        windows[t, 0] = jnp.where(lane == 0, mix, pltpu.roll(centre, 1, 1))
        windows[t, 2] = jnp.where(lane == LANES - 1, mix, pltpu.roll(centre, LANES - 1, 1))

    def shifts(i, _):
        shift(2 * i)
        shift(2 * i + 1)

    def edge_product(r, pair):
        own = receiver[r]
        s = pl.ds(pair * two, two)
        high, low = halves(staged[r, :, s])
        xs[r, :D, s] = high
        xs[r, D:, s] = low
        out = mxu(packed_rows(pack, P_EDGE), jnp.concatenate([high, low, high], axis=0))
        slope[r, :, s] = out + jnp.concatenate([own, own], axis=1)

    def hidden_values(r, pair):
        slots = (2 * pair, 2 * pair + 1)
        hidden = {k: [None] * 8 for k in slots}
        masks = {}
        for k in slots:
            code = jnp.broadcast_to(codes[r, pl.ds(k, 1), :], (8, LANES))
            masks[k] = ((code & 1) != 0, (code & 2) != 0, (code & 4) != 0)
        for f in range(8):
            rows_f = pl.ds(8 * f, 8)
            w = [windows[r + 1 + dr, 1 + dc, rows_f, :] for dr, dc in WINDOWS]
            for k in slots:
                s = pl.ds(k * LANES, LANES)
                b0, b1, b2 = masks[k]
                low = jnp.where(b1, jnp.where(b0, w[3], w[2]), jnp.where(b0, w[1], w[0]))
                top = jnp.where(b1, jnp.where(b0, w[7], w[6]), jnp.where(b0, w[5], w[4]))
                pre = slope[r, rows_f, s] + jnp.where(b2, top, low)
                t = jnp.tanh(pre)
                u = 1.0 + t
                h = pre * u
                slope[r, rows_f, s] = u + h * (1.0 - t)
                hidden[k][f] = h
        s = pl.ds(pair * two, two)
        high, low = halves(
            jnp.concatenate([jnp.concatenate(hidden[k], axis=0) for k in slots], axis=1)
        )
        hs[r, :D, s] = high
        hs[r, D : 2 * D, s] = low
        hs[r, 2 * D :, s] = ones_two

    def hidden_product(r, pair):
        s = pl.ds(pair * two, two)
        both = mxu(
            packed_rows(pack, P_HIDDEN, 3 * D + 16),
            jnp.concatenate([hs[r, :, s], hs[r, :D, s]], axis=0),
        )
        cb[r, :, s] = both[:D]
        db[r, :, s] = both[D:]
        return r, pair, both[:D]

    def norm(r, pair, pair_c, total):
        for j in range(2):
            k = 2 * pair + j
            c = pair_c[:, j * LANES : (j + 1) * LANES]
            variance = jnp.sum(c * c, axis=0, keepdims=True) * (1.0 / D)
            inv = lax.rsqrt(variance + EPS)
            inverse[r, pl.ds(k, 1), :] = inv
            term = (inv * valid[r, pl.ds(k, 1), :]) * c
            total = term if total is None else total + term
        if pair == NBR // 2 - 1:
            summed[r] = total
            total = None
        return total

    def forward(i, _, first=0, last=2, more=True):
        if first == 0:
            for r in (2 * i, 2 * i + 1):
                if more:
                    load_edges(r + 2 + ahead)
                waits(staged.at[r + 2], edge_sem.at[r + 2])
        units = [(2 * i + u, pair) for u in range(2) for pair in range(NBR // 2)]
        products = []
        total = None
        if last >= 2:
            products.append(hidden_product(units[0][0] - 2, units[0][1]))
        for i_unit, (r, pair) in enumerate(units):
            if last >= 2 and i_unit + 1 < len(units):
                ahead_r, ahead_pair = units[i_unit + 1]
                products.append(hidden_product(ahead_r - 2, ahead_pair))
            if first <= 1 <= last:
                if pair == 0:
                    placed[r + 2] = jnp.zeros((3, D, LANES), F32)
                hidden_values(r, pair)
            if last >= 2:
                total = norm(*products[i_unit], total)
            if first == 0:
                edge_product(r + 2, pair)

    for ref in parts[0]:
        waits(ref, row_sem.at[0])
    lax.fori_loop(0, halfway // 2, shifts, None)
    for r in range(2):
        placed[r] = jnp.zeros((3, D, LANES), F32)
        waits(staged.at[r], edge_sem.at[r])
        for pair in range(NBR // 2):
            edge_product(r, pair)
    forward(0, None, last=1)
    for ref in parts[1]:
        waits(ref, row_sem.at[1])
    lax.fori_loop(halfway // 2, rows // 2 + 1, shifts, None)
    node_inputs = load_rest()
    forward(1, None)
    turns = rows // 2
    full = turns - 1 - ahead // 2
    lax.fori_loop(2, full, forward, None)
    lax.fori_loop(full, turns - 1, functools.partial(forward, more=False), None)
    forward(turns - 1, None, first=1)
    forward(turns, None, first=2)

    for ref in (acc_edge, acc_hidden, acc_nin, acc_nout, acc_vec):
        ref[...] = jnp.zeros_like(ref)
    for ref in node_inputs:
        waits(ref, in_sem.at[1])
    chunk = 4
    span = chunk * LANES

    def node_chunk(first):
        tile_cols = lambda i: jnp.concatenate([columns[i]] * chunk, axis=1)
        spread = lambda ref, offset: jnp.concatenate(
            [ref[first + offset + j] for j in range(chunk)], axis=1
        )
        degree = jnp.concatenate(
            [jnp.sum(valid[first + j], axis=0, keepdims=True) for j in range(chunk)], axis=1
        )
        st_high, st_low = halves(spread(state, 1))
        sum_high, sum_low = halves(spread(summed, 0))
        place = lax.broadcasted_iota(jnp.int32, (16, span), 0)
        extra = jnp.where(place < 2, 1.0, jnp.where(place < 4, degree, 0.0)).astype(BF16)
        tops = jnp.concatenate([st_high, sum_high], axis=0)
        ends = jnp.concatenate([st_low, sum_low], axis=0)
        pre = mxu(
            jnp.concatenate(
                [
                    packed_rows(pack, P_NODE_IN, P_LANES),
                    packed_rows(pack, P_NODE_IN_END, 6 * D + 16 - P_LANES),
                ],
                axis=1,
            ),
            jnp.concatenate([tops, ends, extra, tops], axis=0),
        )
        yield
        t = jnp.tanh(pre)
        u = 1.0 + t
        h = pre * u
        slope_n = u + h * (1.0 - t)
        h_high, h_low = halves(h)
        h_all = jnp.concatenate([h_high, h_low, ones16[:, :span]], axis=0)
        c = mxu(
            packed_rows(pack, P_NODE_OUT, 3 * D + 16),
            jnp.concatenate([h_all, h_high], axis=0),
        )
        yield
        cot_c = spread(cot, 0)
        inv = lax.rsqrt(jnp.sum(c * c, axis=0, keepdims=True) * (1.0 / D) + EPS)
        n = c * inv
        new = spread(state, 1) + (tile_cols(C_GAIN_N) * n + tile_cols(C_SHIFT_N))
        q = cot_c * tile_cols(C_GAIN_N)
        q = q - jnp.sum(q, axis=0, keepdims=True) * (1.0 / D)
        grad = inv * (q - n * (jnp.sum(q * n, axis=0, keepdims=True) * (1.0 / D)))
        g_high, g_low = halves(grad)
        pre_grad = mxu(
            packed_rows(pack, P_NODE_OUT_T), jnp.concatenate([g_high, g_low, g_high], axis=0)
        )
        for j in range(chunk):
            s = slice(j * LANES, (j + 1) * LANES)
            fresh[first + j] = new[:, s]
            acc_vec[0] += cot_c[:, s] * n[:, s]
            acc_vec[1] += cot_c[:, s]
        yield
        acc_nout[...] += outer(jnp.concatenate([g_high, g_low], axis=0), h_all)
        pre_grad = pre_grad * slope_n
        p_high, p_low = halves(pre_grad)
        back = mxu(
            packed_rows(pack, P_NODE_IN_T), jnp.concatenate([p_high, p_low, p_high], axis=0)
        )
        for j in range(chunk):
            s = slice(j * LANES, (j + 1) * LANES)
            acc_vec[2] += pre_grad[:, s]
            acc_vec[3] += pre_grad[:, s] * degree[:, s]
        yield
        acc_nin[...] += outer(
            jnp.concatenate([p_high, p_low], axis=0), jnp.concatenate([tops, ends], axis=0)
        )
        for j in range(chunk):
            s = slice(j * LANES, (j + 1) * LANES)
            part[first + j] = cot[first + j] + back[:D, s]
            qc_ref[first + j] = back[D : 2 * D, s]
            qo_ref[first + j] = back[2 * D :, s]

    in_flight = []
    for first in range(0, rows + 4 * chunk, chunk):
        if first < rows:
            in_flight.append(node_chunk(first))
        for routine in list(in_flight):
            if next(routine, routine) is routine:
                in_flight.remove(routine)

    def send_new(r, _):
        pltpu.make_async_copy(fresh.at[r], new_states.at[:, r, :], out_sem).start()

    lax.fori_loop(0, rows, send_new, None)
    pltpu.make_async_copy(part, part_out, out_sem).start()

    def grad_unit(r, pair, u, received):
        qc = qc_ref[r]
        qo = qo_ref[r]
        hidden_grads, grads = [], []
        for k in (2 * pair, 2 * pair + 1):
            s = pl.ds(k * LANES, LANES)
            c = cb[r, :, s]
            inv = inverse[r, pl.ds(k, 1), :]
            alpha = inv * valid[r, pl.ds(k, 1), :]
            moment = jnp.sum(qc * c, axis=0, keepdims=True) * (1.0 / D)
            beta = alpha * inv * inv * moment
            hidden_grads.append(alpha * qc - beta * c)
            grad = (alpha * qo - beta * db[r, :, s]) * slope[r, :, s]
            grads.append(grad)
            received = grad if received is None else received + grad
        high, low = halves(jnp.concatenate(hidden_grads, axis=1))
        s = pl.ds(pair * two, two)
        gather_grads[u, :D, s] = high
        gather_grads[u, D : 2 * D, s] = low
        high, low = halves(jnp.concatenate(grads, axis=1))
        gather_grads[u, 2 * D : 3 * D, s] = high
        gather_grads[u, 3 * D :, s] = low
        ge = mxu(
            packed_rows(pack, P_EDGE_T), jnp.concatenate([high, low, high], axis=0)
        )
        return grads, received, ge

    def place_unit(r, pair, grads):
        code = [
            jnp.broadcast_to(codes[r, pl.ds(k, 1), :], (8, LANES))
            for k in (2 * pair, 2 * pair + 1)
        ]
        for which, (dr, dc) in enumerate(WINDOWS):
            masks = [c == which for c in code]
            for f in range(8):
                rows_f = pl.ds(8 * f, 8)
                value = placed[r + 1 + dr, 1 + dc, rows_f, :]
                for j in range(2):
                    value += jnp.where(masks[j], grads[j][8 * f : 8 * f + 8], 0.0)
                placed[r + 1 + dr, 1 + dc, rows_f, :] = value

    def store_unit(r, pair, ge):
        staged[r, :, pl.ds(pair * two, two)] = ge

    def products(r, u):
        r = jnp.maximum(r, 0)
        acc_hidden[...] += outer(gather_grads[u, : 2 * D], hs[r])
        acc_edge[...] += outer(gather_grads[u, 2 * D :], xs[r])

    def send_rows(i, unroll=2):
        for u in range(unroll):
            r = unroll * i + u
            pltpu.make_async_copy(grad_recv.at[r], recv_out.at[r], out_sem).start()
            pltpu.make_async_copy(placed.at[r], placed_out.at[r], out_sem).start()
            for k in range(NBR):
                pltpu.make_async_copy(
                    staged.at[r, :, pl.ds(k * LANES, LANES)],
                    grad_edges.at[:, k, r, :],
                    out_sem,
                ).start()

    def backward(i, _, unroll=2):
        if not isinstance(i, int):
            send_rows(i - 1)
        pending = None
        for u in range(unroll):
            r = unroll * i + u
            products(r - unroll, u)
            received = None
            for pair in range(NBR // 2):
                grads, received, ge = grad_unit(r, pair, u, received)
                place_unit(r, pair, grads)
                if pending is not None:
                    store_unit(*pending)
                pending = (r, pair, ge)
            grad_recv[r] = received
        store_unit(*pending)

    gather_grads[...] = jnp.zeros_like(gather_grads)
    backward(0, None)
    lax.fori_loop(1, rows // 2, backward, None)
    products(rows - 2, 0)
    products(rows - 1, 1)
    send_rows(rows // 2 - 1)
    tail = pl.ds(rows, 2)
    pltpu.make_async_copy(placed.at[tail], placed_out.at[tail], out_sem).start()

    def folded(ref):
        half = ref[:D, : 2 * D] + ref[D:, : 2 * D]
        return half + pltpu.roll(half, D, 1)

    left = lane < D
    acc[0] = folded(acc_edge)
    plain = (
        acc_nin[:D, : 2 * D]
        + acc_nin[D:, : 2 * D]
        + acc_nin[:D, 2 * D :]
        + acc_nin[D:, 2 * D :]
    )
    pick = lambda ref, start, i: jnp.sum(
        jnp.where(lane[:, :16] == i, ref[:D, start:] + ref[D:, start:], 0.0),
        axis=1,
        keepdims=True,
    )
    lane_sum = lambda i: jnp.sum(acc_vec[i], axis=1, keepdims=True)
    by_degree = lane_sum(3)
    acc[2] = plain * columns[C_ROWS, 0:1, :] + by_degree * columns[C_ROWS, 1:2, :]
    acc[3] = jnp.where(left, folded(acc_hidden), folded(acc_nout))
    weight_n = columns[C_WEIGHT_N]
    gain_row = jnp.sum(weight_n * plain, axis=0, keepdims=True)[:, D:]
    shift_row = jnp.sum(weight_n * by_degree, axis=0, keepdims=True)[:, D:]
    block = jnp.zeros((D, LANES), F32)
    for i, vector in (
        (1, pick(acc_hidden, 2 * D, 0)),
        (2, to_column(gain_row)),
        (3, to_column(shift_row)),
        (4, lane_sum(2)),
        (5, pick(acc_nout, 2 * D, 0)),
        (6, lane_sum(0)),
        (7, lane_sum(1)),
        (8, columns[C_DIVERGED]),
    ):
        block = jnp.where(lane == D + i, vector, block)
    acc[1] = block
    pltpu.make_async_copy(acc, acc_out, out_sem).start()
    for ref in (fresh, part, grad_recv, placed, staged, acc):
        waits(ref, out_sem)


def layer_call(edges, cotangent, projected, receiver, sides, codes, valid, pack, columns, state):
    rows = cotangent.shape[1]
    wide = NBR * LANES
    tile = (D, LANES)
    shape = lambda *dims: jax.ShapeDtypeStruct(dims, F32)
    vmem = lambda *dims: pltpu.VMEM(dims, F32)
    return pl.pallas_call(
        layer_kernel,
        name="layer",
        out_shape=(
            shape(D, rows, LANES),
            shape(D, NBR, rows, LANES),
            shape(rows, *tile),
            shape(rows, *tile),
            shape(rows + 2, 3, *tile),
            shape(4, *tile),
        ),
        in_specs=[HBM] * 10,
        out_specs=[HBM] * 6,
        scratch_shapes=[
            vmem(rows, D, wide),
            pltpu.VMEM((rows, 2 * D, wide), BF16),
            pltpu.VMEM((rows, 2 * D + 16, wide), BF16),
            vmem(rows, D, wide),
            vmem(rows, D, wide),
            vmem(rows, D, wide),
            vmem(rows + 2, 3, *tile),
            vmem(rows + 2, *tile),
            vmem(rows, *tile),
            vmem(2, *tile),
            pltpu.VMEM((rows, 8, LANES), jnp.int32),
            vmem(rows, 8, LANES),
            pltpu.VMEM((P_ROWS, P_LANES), BF16),
            vmem(C_TILES, *tile),
            vmem(rows + 2, *tile),
            vmem(rows, 8, LANES),
            vmem(rows, *tile),
            vmem(rows, *tile),
            vmem(rows, *tile),
            vmem(rows, *tile),
            vmem(rows, *tile),
            vmem(rows, *tile),
            vmem(rows + 2, 3, *tile),
            vmem(rows, *tile),
            pltpu.VMEM((2, 4 * D, wide), BF16),
            vmem(2 * D, 2 * D),
            vmem(2 * D, 2 * D + 16),
            vmem(2 * D, 4 * D),
            vmem(2 * D, 2 * D + 16),
            vmem(4, *tile),
            vmem(4, *tile),
            pltpu.SemaphoreType.DMA((2,)),
            pltpu.SemaphoreType.DMA((rows,)),
            pltpu.SemaphoreType.DMA((2,)),
            pltpu.SemaphoreType.DMA,
        ],
        compiler_params=pltpu.CompilerParams(vmem_limit_bytes=ROOM),
    )(edges, cotangent, projected, receiver, sides, codes, valid, pack, columns, state)


def sum_kernel(
    n_blk,
    n_lon,
    acc_in,
    placed_in,
    recv_in,
    part_in,
    state_in,
    cols_in,
    pack_in,
    part_out,
    total_out,
    acc,
    placed,
    grad_recv,
    part,
    state,
    cols,
    pack,
    own,
    halo,
    acc_send,
    acc_recv,
    packed,
    scattered,
    across,
    gathered,
    landing,
    halo_in,
    in_sem,
    row_sem,
    rs_send,
    rs_recv,
    x_send,
    x_recv,
    ag_send,
    ag_recv,
    halo_send,
    halo_recv,
    out_sem,
):
    rows = recv_in.shape[0]
    blk, lon, around = neighbours(n_blk, n_lon)
    size = scattered.shape[0]
    n_groups = across.shape[0]
    per = size // n_lon
    me = lax.rem(blk, per) * n_lon + lon
    own_group = blk // per
    lane = lane_ids()

    def member(index):
        return (own_group * per + index // n_lon, lax.rem(index, n_lon))

    def other(step):
        return lax.rem(me + step, size)

    def peer(step):
        return (lax.rem(own_group + step, n_groups) * per + lax.rem(blk, per), lon)

    half = rows // 2
    for h in range(2):
        span = pl.ds(h * half, half)
        span3 = pl.ds(0, half + 1) if h == 0 else pl.ds(half + 1, half + 1)
        for source, target in (
            (placed_in.at[span3], placed.at[span3]),
            (state_in.at[span3], state.at[span3]),
            (recv_in.at[span], grad_recv.at[span]),
        ):
            pltpu.make_async_copy(source, target, row_sem.at[h]).start()
    small = (
        (pack_in.at[pl.ds(P_SEND_T[0], 2 * D)], pack),
        (cols_in, cols),
        (acc_in, acc),
        (part_in, part),
    )
    for i, (source, target) in enumerate(small):
        pltpu.make_async_copy(source, target, in_sem.at[i]).start()

    barrier = pltpu.get_barrier_semaphore()

    def greet(step, _):
        pl.semaphore_signal(
            barrier, inc=1, device_id=member(other(step)), device_id_type=MESH
        )

    lax.fori_loop(1, size, greet, None)
    expected = size - 1
    if n_groups > 1:
        for place in around:
            pl.semaphore_signal(barrier, inc=1, device_id=place, device_id_type=MESH)

        def greet_group(step, _):
            pl.semaphore_signal(barrier, inc=1, device_id=peer(step), device_id_type=MESH)

        lax.fori_loop(1, n_groups, greet_group, None)
        expected += 8 + n_groups - 1

    acc_send[...] = jnp.zeros_like(acc_send)
    acc_recv[...] = jnp.zeros_like(acc_recv)

    def settle(t, cells):
        west_cells, east_cells = cells
        to_west = placed[t, 0]
        to_east = placed[t, 2]
        value = (
            placed[t, 1]
            + jnp.where(lane == 0, 0.0, pltpu.roll(to_east, 1, 1))
            + jnp.where(lane == LANES - 1, 0.0, pltpu.roll(to_west, LANES - 1, 1))
        )
        own[t] = value
        mix = pltpu.roll(jnp.where(lane == 0, to_west, to_east), t, 1)
        west_cells = jnp.where(lane == t, mix, west_cells)
        east_cells = jnp.where(lane == lax.rem(t + LANES - 1, LANES), mix, east_cells)
        return value, (west_cells, east_cells)

    def both_halves(value):
        return jnp.concatenate(halves(value), axis=0)

    ones_row = jnp.where(
        lax.broadcasted_iota(jnp.int32, (16, 4 * LANES), 0) < 1, 1.0, 0.0
    ).astype(BF16)

    def collect(i, cells):
        values, there, received = [], [], []
        for u in range(4):
            t = 1 + 4 * i + u
            value, cells = settle(t, cells)
            values.append(value)
            there.append(state[t])
            received.append(grad_recv[t - 1])
        wide = lambda parts: both_halves(jnp.concatenate(parts, axis=1))
        there = wide(there)
        acc_send[...] += outer(wide(values), there)
        acc_recv[...] += outer(wide(received), jnp.concatenate([there, ones_row], axis=0))
        return cells

    zero = jnp.zeros((D, LANES), F32)
    for h in range(2):
        span = pl.ds(h * half, half)
        waits(placed.at[pl.ds(h * (half + 1), half + 1)], row_sem.at[h])
        waits(state.at[pl.ds(h * (half + 1), half + 1)], row_sem.at[h])
        waits(grad_recv.at[span], row_sem.at[h])
        if h == 0:
            _, cells = settle(0, (zero, zero))
        cells = lax.fori_loop(h * half // 4, (h + 1) * half // 4, collect, cells)
    _, cells = settle(rows + 1, cells)
    waits(cols, in_sem.at[1])
    edge_values = jnp.concatenate([own[0], own[rows + 1], cells[0], cells[1]], axis=1)
    edge_states = jnp.concatenate([state[0], state[rows + 1], cols[0], cols[1]], axis=1)
    acc_send[...] += outer(both_halves(edge_values), both_halves(edge_states))

    def folded(ref):
        part_sum = ref[:D, : 2 * D] + ref[D:, : 2 * D]
        return part_sum + pltpu.roll(part_sum, D, 1)

    left = lane < D
    waits(acc, in_sem.at[2])
    ones_sum = jnp.sum(
        jnp.where(lane[:, :16] == 0, acc_recv[:D, 2 * D :] + acc_recv[D:, 2 * D :], 0.0),
        axis=1,
        keepdims=True,
    )
    chunk = packed.shape[1]
    blocks = (
        jnp.where(left, acc[0], folded(acc_send)),
        jnp.where(left, folded(acc_recv), jnp.where(lane == D, ones_sum, acc[1])),
        acc[2],
        acc[3],
    )
    per_block = D // chunk
    for i, block in enumerate(blocks):
        for j in range(per_block):
            packed[i * per_block + j] = block[j * chunk : (j + 1) * chunk]
    pl.semaphore_wait(barrier, expected)

    def scatter(step, _):
        target = other(step)
        pltpu.make_async_remote_copy(
            src_ref=packed.at[target],
            dst_ref=scattered.at[me],
            send_sem=rs_send,
            recv_sem=rs_recv,
            device_id=member(target),
            device_id_type=MESH,
        ).start()

    lax.fori_loop(1, size, scatter, None)
    scattered[me] = packed[me]

    waits(pack, in_sem.at[0])
    a_send = pack[:D, : 3 * D]
    a_recv = pack[D : 2 * D, : 3 * D]
    high, low = halves(edge_values)
    edge_grads = mxu(a_send, jnp.concatenate([high, low, high], axis=0))
    for i in range(4):
        halo[i] = edge_grads[:, i * LANES : (i + 1) * LANES]
    copies = []
    for slot, (place, source) in enumerate(zip(around, (0, 1, 2, 3, 2, 3, 2, 3))):
        copies.append(
            pltpu.make_async_remote_copy(
                src_ref=halo.at[source],
                dst_ref=landing.at[slot],
                send_sem=halo_send.at[slot],
                recv_sem=halo_recv.at[slot],
                device_id=place,
                device_id_type=MESH,
            )
        )
        copies[-1].start()
    waits(part, in_sem.at[3])

    def finish(i, _):
        for u in range(2):
            first = 4 * i + 2 * u
            grads = None
            for weights, ref, offset in ((a_send, own, 1), (a_recv, grad_recv, 0)):
                high, low = halves(
                    jnp.concatenate([ref[first + offset], ref[first + offset + 1]], axis=1)
                )
                product = mxu(weights, jnp.concatenate([high, low, high], axis=0))
                grads = product if grads is None else grads + product
            for j in range(2):
                part[first + j] += grads[:, j * LANES : (j + 1) * LANES]

    lax.fori_loop(0, rows // 4, finish, None)

    others = pl.ds(0, size - 1)
    waits(scattered.at[others], rs_recv)
    mine = scattered[0]
    for i in range(1, size):
        mine = mine + scattered[i]
    if n_groups > 1:
        across[own_group] = mine

        def cross(step, _):
            pltpu.make_async_remote_copy(
                src_ref=across.at[own_group],
                dst_ref=across.at[own_group],
                send_sem=x_send,
                recv_sem=x_recv,
                device_id=peer(step),
                device_id_type=MESH,
            ).start()

        lax.fori_loop(1, n_groups, cross, None)
        rest = pl.ds(0, n_groups - 1)
        waits(across.at[rest], x_recv)
        waits(across.at[rest], x_send)
        mine = across[0]
        for i in range(1, n_groups):
            mine = mine + across[i]
    gathered[me] = mine

    def gather(step, _):
        pltpu.make_async_remote_copy(
            src_ref=gathered.at[me],
            dst_ref=gathered.at[me],
            send_sem=ag_send,
            recv_sem=ag_recv,
            device_id=member(other(step)),
            device_id_type=MESH,
        ).start()

    lax.fori_loop(1, size, gather, None)
    for copy in copies:
        copy.wait()
    halo_in[0] = landing[1]
    halo_in[1] = landing[0]
    corner = lambda slot, at, to: jnp.where(
        lane == to, pltpu.roll(landing[slot], (to - at) % LANES, 1), 0.0
    )
    halo_in[2] = (
        pltpu.roll(jnp.where(lane < rows, landing[3], 0.0), 1, 1)
        + corner(7, rows, 1)
        + corner(5, LANES - 1, rows)
    )
    east_in = (
        jnp.where((lane >= 1) & (lane <= rows), landing[2], 0.0)
        + corner(6, rows + 1, 1)
        + corner(4, 0, rows)
    )
    west_in = halo_in[2]
    east_in = pltpu.roll(east_in, LANES - 1, 1)
    rim = (lane == 0) | (lane == LANES - 1)
    part[0] += halo_in[0]
    part[rows - 1] += halo_in[1]

    def add_columns(i, _):
        for u in range(4):
            r = 4 * i + u
            mix = pltpu.roll(
                jnp.where(lane == r + 1, west_in, east_in), LANES - 1 - r, 1
            )
            part[r] += jnp.where(rim, mix, 0.0)
        for u in range(4):
            r = 4 * i + u
            pltpu.make_async_copy(part.at[r], part_out.at[:, r, :], out_sem).start()

    lax.fori_loop(0, rows // 4, add_columns, None)
    waits(gathered.at[others], ag_recv)
    pltpu.make_async_copy(gathered, total_out, out_sem).start()
    waits(scattered.at[others], rs_send)
    waits(gathered.at[others], ag_send)
    for ref in (part, gathered):
        waits(ref, out_sem)


def sum_call(n_blk, n_lon, acc, placed, recv, part, state, cols, pack):
    rows = recv.shape[0]
    size = min(32, n_blk * n_lon)
    n_groups = n_blk * n_lon // size
    chunk = (4 * D // size, LANES)
    tile = (D, LANES)
    shape = lambda *dims: jax.ShapeDtypeStruct(dims, F32)
    vmem = lambda *dims: pltpu.VMEM(dims, F32)
    dma = pltpu.SemaphoreType.DMA
    return pl.pallas_call(
        functools.partial(sum_kernel, n_blk, n_lon),
        name="sums",
        out_shape=(shape(D, rows, LANES), shape(size, *chunk)),
        in_specs=[HBM] * 7,
        out_specs=[HBM] * 2,
        scratch_shapes=[
            vmem(4, *tile),
            vmem(rows + 2, 3, *tile),
            vmem(rows, *tile),
            vmem(rows, *tile),
            vmem(rows + 2, *tile),
            vmem(2, *tile),
            pltpu.VMEM((2 * D, P_LANES), BF16),
            vmem(rows + 2, *tile),
            vmem(4, *tile),
            vmem(2 * D, 2 * D),
            vmem(2 * D, 2 * D + 16),
            vmem(size, *chunk),
            vmem(size, *chunk),
            vmem(n_groups, *chunk),
            vmem(size, *chunk),
            vmem(8, *tile),
            vmem(3, *tile),
            dma((4,)),
            dma((2,)),
            dma,
            dma,
            dma,
            dma,
            dma,
            dma,
            dma((8,)),
            dma((8,)),
            dma,
        ],
        compiler_params=pltpu.CompilerParams(
            collective_id=1, has_side_effects=True, vmem_limit_bytes=ROOM
        ),
    )(acc, placed, recv, part, state, cols, pack)


def final_kernel(
    kl_weight,
    part_nodes,
    mean,
    logstd,
    noise,
    total_in,
    columns_in,
    *rest,
):
    grad_nodes, grad_mean, grad_logstd = rest[:3]
    small_outs = rest[3:16]
    grad, mean_v, logstd_v, noise_v, total, columns = rest[16:22]
    smalls = rest[22:35]
    in_sem, small_sem, out_sem = rest[35:]
    n_chunks = in_sem.shape[0]
    depth = D // n_chunks
    for i, (source, target) in enumerate(((columns_in, columns), (total_in, total))):
        pltpu.make_async_copy(source, target, small_sem.at[i]).start()
    spans = [pl.ds(i * depth, depth) for i in range(n_chunks)]
    pairs = ((part_nodes, grad), (mean, mean_v), (logstd, logstd_v), (noise, noise_v))
    for i, span in enumerate(spans):
        for source, target in pairs:
            pltpu.make_async_copy(source.at[span], target.at[span], in_sem.at[i]).start()

    waits(columns, small_sem.at[0])
    waits(total, small_sem.at[1])
    kl_value, g_w_ei, g_w_eo, g_w_ni, g_w_no = smalls[:5]
    chunk = total.shape[1]
    per_block = D // chunk
    blocks = [
        jnp.concatenate([total[i * per_block + j] for j in range(per_block)], axis=0)
        for i in range(4)
    ]
    g_w_ei[:, : 2 * D] = blocks[0]
    g_w_ei[:, 2 * D :] = blocks[1][:, :D]
    g_w_ni[...] = blocks[2]
    g_w_eo[...] = blocks[3][:, :D]
    g_w_no[...] = pltpu.roll(blocks[3], D, 1)[:, :D]
    for i in range(8):
        smalls[5 + i][...] = to_row(blocks[1][:, D + i : D + i + 1])
    diverged = jnp.sum(blocks[1][:, D + 8 : D + 9], axis=0, keepdims=True)
    kl_value[...] = diverged / columns[C_COUNT, 0:1, 0:1]
    for source, target in zip(smalls, small_outs):
        pltpu.make_async_copy(source, target, out_sem).start()

    inside = (kl_weight[0] * columns[C_VALID, 0:1, :]).reshape(1, 1, LANES)
    for i, span in enumerate(spans):
        for _, target in pairs:
            waits(target.at[span], in_sem.at[i])
        pltpu.make_async_copy(grad.at[span], grad_nodes.at[span], out_sem).start()
        for f in range(i * depth, (i + 1) * depth):
            one = pl.ds(f, 1)
            g = grad[one]
            spread = jnp.exp(logstd_v[one])
            mean_v[one] = g + inside * mean_v[one]
            logstd_v[one] = g * spread * noise_v[one] + inside * (spread * spread - 1.0)
        pltpu.make_async_copy(mean_v.at[span], grad_mean.at[span], out_sem).start()
        pltpu.make_async_copy(logstd_v.at[span], grad_logstd.at[span], out_sem).start()
    for ref in (grad, mean_v, logstd_v, *smalls):
        waits(ref, out_sem)


def final_call(kl_weight, part_nodes, mean, logstd, noise, total, columns):
    shape = lambda *dims: jax.ShapeDtypeStruct(dims, F32)
    vmem = lambda *dims: pltpu.VMEM(dims, F32)
    whole = mean.shape
    small = ((1, 1), (D, 3 * D), (D, D), (D, 2 * D), (D, D)) + ((1, D),) * 8
    return pl.pallas_call(
        final_kernel,
        name="final",
        out_shape=[shape(*dims) for dims in (whole,) * 3 + small],
        in_specs=[SMEM] + [HBM] * 6,
        out_specs=[HBM] * 16,
        scratch_shapes=[vmem(*whole) for _ in range(4)]
        + [vmem(*total.shape), vmem(C_TILES, D, LANES)]
        + [vmem(*dims) for dims in small]
        + [
            pltpu.SemaphoreType.DMA((8,)),
            pltpu.SemaphoreType.DMA((2,)),
            pltpu.SemaphoreType.DMA,
        ],
        compiler_params=pltpu.CompilerParams(vmem_limit_bytes=ROOM),
    )(kl_weight, part_nodes, mean, logstd, noise, total, columns)


def shards(
    nodes,
    edges,
    latent_mean,
    latent_logstd,
    latent_noise,
    kl_weight,
    band_counts,
    neighbors,
    edge_mask,
    w_edge_in,
    b_edge_in,
    w_edge_out,
    b_edge_out,
    edge_gain,
    edge_shift,
    w_node_in,
    b_node_in,
    w_node_out,
    b_node_out,
    node_gain,
    node_shift,
    cotangent,
):
    n_blk = lax.axis_size("blk")
    n_lon = lax.axis_size("lon")
    vectors = (
        b_edge_in,
        b_edge_out,
        edge_gain,
        edge_shift,
        b_node_in,
        b_node_out,
        node_gain,
        node_shift,
    )
    weights = (w_edge_in, w_edge_out, w_node_in, w_node_out)
    weights += tuple(vector.reshape(1, D) for vector in vectors)
    state, cols, projected, receiver, sides, codes, valid, pack, columns = start_call(
        n_blk,
        n_lon,
        band_counts,
        nodes,
        latent_mean,
        latent_logstd,
        latent_noise,
        neighbors,
        edge_mask,
        weights,
    )
    new_states, grad_edges, part, recv, placed, acc = layer_call(
        edges, cotangent, projected, receiver, sides, codes, valid, pack, columns, state
    )
    part, total = sum_call(n_blk, n_lon, acc, placed, recv, part, state, cols, pack)
    grad_nodes, grad_mean, grad_logstd, kl_value, g_w_ei, g_w_eo, g_w_ni, g_w_no, *g_vec = (
        final_call(
            kl_weight,
            part,
            latent_mean,
            latent_logstd,
            latent_noise,
            total,
            columns,
        )
    )
    g_vec = [vector.reshape(D) for vector in g_vec]
    return (
        new_states,
        kl_value.reshape(1),
        grad_nodes,
        grad_edges,
        grad_mean,
        grad_logstd,
        g_w_ei,
        g_vec[0],
        g_w_eo,
        g_vec[1],
        g_vec[2],
        g_vec[3],
        g_w_ni,
        g_vec[4],
        g_w_no,
        g_vec[5],
        g_vec[6],
        g_vec[7],
    )


def solution(mesh):
    node = P(None, "blk", "lon")
    slot = P(None, None, "blk", "lon")
    return jax.shard_map(
        shards,
        mesh=mesh,
        in_specs=(
            (node, slot, node, node, node, P(), P(), node, node) + (P(),) * 12 + (node,)
        ),
        out_specs=(node, P(), node, slot, node, node) + (P(),) * 12,
        check_vma=False,
    )
```

```python
import functools

import jax
import jax.numpy as jnp
from jax import lax
from jax.experimental import pallas as pl
from jax.experimental.pallas import tpu as pltpu
from jax.sharding import PartitionSpec as P

F32 = jnp.float32
BF16 = jnp.bfloat16
MESH = pl.DeviceIdType.MESH
D = 64
LANES = 128
NBR = 6
EPS = 1e-05
HBM = pl.BlockSpec(memory_space=pltpu.HBM)
VMEM = pl.BlockSpec(memory_space=pltpu.VMEM)
ROOM = 62 * 2**20
SMEM = pl.BlockSpec(memory_space=pltpu.SMEM)

WINDOWS = ((-1, -1), (-1, 0), (-1, 1), (0, -1), (0, 1), (1, -1), (1, 0), (1, 1))


def halves(value):
    high = value.astype(BF16)
    return high, (value - high.astype(F32)).astype(BF16)


def weight_pack(weight, *biases):
    high, low = halves(weight)
    if not biases:
        return jnp.concatenate([high, high, low], axis=1)
    place = lax.broadcasted_iota(jnp.int32, (weight.shape[0], 16), 1)
    wide = jnp.zeros((weight.shape[0], 16), F32)
    for i, bias in enumerate(biases):
        for j, part in enumerate(halves(bias)):
            wide = jnp.where(place == 2 * i + j, part.astype(F32), wide)
    return jnp.concatenate([high, high, wide.astype(BF16), low], axis=1)


def mxu(left, right):
    return jnp.dot(left, right, preferred_element_type=F32)


def outer(left, right):
    return lax.dot_general(
        left, right, (((1,), (1,)), ((), ())), preferred_element_type=F32
    )


def exact(left, right, dims):
    return lax.dot_general(
        left,
        right,
        (dims, ((), ())),
        precision=lax.Precision.HIGHEST,
        preferred_element_type=F32,
    )


def eye():
    return lax.broadcasted_iota(jnp.int32, (D, D), 0) == lax.broadcasted_iota(
        jnp.int32, (D, D), 1
    )


def to_column(row):
    return jnp.sum(jnp.where(eye(), row, 0.0), axis=1, keepdims=True)


def to_row(column):
    return jnp.sum(jnp.where(eye(), column, 0.0), axis=0, keepdims=True)


def waits(ref, sem):
    pltpu.make_async_copy(ref, ref, sem).wait()


def in_turn(*routines):
    waiting = list(routines)
    while waiting:
        for routine in list(waiting):
            if next(routine, routine) is routine:
                waiting.remove(routine)


def lane_ids(rows=D):
    return lax.broadcasted_iota(jnp.int32, (rows, LANES), 1)


P_HIDDEN, P_EDGE, P_EDGE_T, P_NODE_OUT = (0, 128), (128, 192), (192, 256), (256, 320)
P_NODE_OUT_T, P_NODE_IN_T, P_SEND_T, P_RECV_T = (320, 384), (384, 576), (576, 640), (640, 704)
P_NODE_IN, P_NODE_IN_END = (704, 768), (768, 832)
P_ROWS, P_LANES = 832, 256
C_GAIN_N, C_SHIFT_N, C_VALID, C_DIVERGED, C_COUNT, C_WEIGHT_N, C_ROWS = range(7)
C_TILES = 7


def packed_rows(ref, rows, lanes=3 * D):
    return ref[rows[0] : rows[1], :lanes]


def row_of(ref, row, step, count=D):
    flat = ref.reshape(count * step, LANES)
    return flat, pl.ds(row, count, stride=step)


def read_row(ref, row, step=8):
    flat, place = row_of(ref, row, step)
    return flat[place, :]


def write_row(ref, row, value, step=8):
    flat, place = row_of(ref, row, step)
    flat[place, :] = value


def pack_column(tile):
    return jnp.where(lane_ids(D // 2) < D, tile[: D // 2], pltpu.roll(tile[D // 2 :], D, 1))


def unpack_column(tile):
    return jnp.concatenate([tile, pltpu.roll(tile, D, 1)], axis=0)


def corner_rows(columns):
    rows = [to_row(column) for column in columns]
    wide = jnp.concatenate(rows + [jnp.zeros((4, D), F32)], axis=0)
    return jnp.concatenate([wide, jnp.zeros((8, D), F32)], axis=1)


def corner_at(ref, row, lane):
    return jnp.where(lane_ids() == lane, to_column(ref[row : row + 1, :D]), 0.0)


def rim_copies(around, rows, columns, corners, rows_in, columns_in, corners_in, send, recv):
    pairs = [(rows.at[0], rows_in.at[0]), (rows.at[1], rows_in.at[1])]
    pairs += [(columns.at[0], columns_in.at[0]), (columns.at[1], columns_in.at[1])]
    pairs += [(corners, corners_in.at[i]) for i in range(4)]
    return [
        pltpu.make_async_remote_copy(
            src_ref=source,
            dst_ref=target,
            send_sem=send.at[slot],
            recv_sem=recv.at[slot],
            device_id=place,
            device_id_type=MESH,
        )
        for slot, (place, (source, target)) in enumerate(zip(around, pairs))
    ]


def neighbours(n_blk, n_lon):
    blk = lax.axis_index("blk")
    lon = lax.axis_index("lon")
    up = lax.rem(blk + n_blk - 1, n_blk)
    down = lax.rem(blk + 1, n_blk)
    west = lax.rem(lon + n_lon - 1, n_lon)
    east = lax.rem(lon + 1, n_lon)
    around = (
        (up, lon),
        (down, lon),
        (blk, west),
        (blk, east),
        (up, west),
        (up, east),
        (down, west),
        (down, east),
    )
    return blk, lon, around


def start_kernel(
    n_blk,
    n_lon,
    counts,
    kl_weight,
    nodes,
    mean,
    logstd,
    noise,
    neighbors,
    edge_mask,
    w_ei,
    w_eo,
    w_ni,
    w_no,
    *rest,
):
    vectors = rest[:8]
    (
        state_out,
        cols_out,
        project_out,
        receive_out,
        sides_out,
        codes_out,
        valid_out,
        pack_out,
        columns_out,
        buf,
        state,
        projected,
        receiver,
        sides,
        nb,
        mk,
        codes,
        valid,
        v_ei,
        v_eo,
        v_ni,
        v_no,
        v_vec,
        pack,
        columns,
        cols,
        edge_rows,
        edge_cols,
        edge_corners,
        rows_in,
        cols_in,
        corners_in,
        in_sem,
        slot_sem,
        weight_sem,
        send_sem,
        recv_sem,
        out_sem,
    ) = rest[8:]
    rows = nodes.shape[1]
    blk, lon, around = neighbours(n_blk, n_lon)
    barrier = pltpu.get_barrier_semaphore()
    for place in around:
        pl.semaphore_signal(barrier, inc=1, device_id=place, device_id_type=MESH)

    n_groups = in_sem.shape[0]
    group = rows // n_groups
    for g in range(n_groups):
        for which, source in enumerate((nodes, mean, logstd, noise)):
            pltpu.make_async_copy(
                source.at[:, pl.ds(g * group, group), :], buf.at[g, which], in_sem.at[g]
            ).start()
    weights = [(w_ei, v_ei), (w_eo, v_eo), (w_ni, v_ni), (w_no, v_no)]
    weights += [(vectors[i], v_vec.at[i]) for i in range(8)]
    lane = lane_ids()
    count = counts[blk]
    inside = lane < count

    def state_row(g, j, carry):
        total, west_tile, east_tile = carry
        r = g * group + j
        node_r, mean_r, logstd_r, noise_r = [
            read_row(buf.at[g, which], j, group) for which in range(4)
        ]
        spread = jnp.exp(logstd_r)
        value = node_r + mean_r + spread * noise_r
        state[r + 1] = value
        total += jnp.where(inside, mean_r * mean_r + spread * spread - 2.0 * logstd_r, 0.0)
        moved = pltpu.roll(value, r + 1, 1)
        west_tile = jnp.where(lane == r + 1, moved, west_tile)
        east_tile = jnp.where(lane == r, moved, east_tile)
        return total, west_tile, east_tile

    carry = (jnp.zeros((D, LANES), F32),) * 3
    for source, target in weights:
        pltpu.make_async_copy(source, target, weight_sem).start()

    def state_group(g, carry):
        waits(buf.at[g], in_sem.at[g])
        for j in range(0, group, 2):
            carry = state_row(g, j + 1, state_row(g, j, carry))
        return carry

    carry = lax.fori_loop(0, n_groups, state_group, carry)
    total, west_tile, east_tile = carry
    edge_rows[0] = state[1]
    edge_rows[1] = state[rows]
    edge_cols[0] = pack_column(west_tile)
    edge_cols[1] = pack_column(east_tile)
    edge_corners[...] = corner_rows(
        [
            state[row][:, lane0 : lane0 + 1]
            for row in (1, rows)
            for lane0 in (0, LANES - 1)
        ]
    )

    pl.semaphore_wait(barrier, 8)
    copies = rim_copies(
        around,
        edge_rows,
        edge_cols,
        edge_corners,
        rows_in,
        cols_in,
        corners_in,
        send_sem,
        recv_sem,
    )
    for copy in copies:
        copy.start()
    pltpu.make_async_copy(neighbors, nb, slot_sem).start()
    pltpu.make_async_copy(edge_mask, mk, slot_sem).start()
    inner = pl.ds(1, rows)
    pltpu.make_async_copy(state.at[inner], state_out.at[inner], out_sem).start()

    for _, target in weights:
        waits(target, weight_sem)
    b_ei, b_eo, gain_e, shift_e, b_ni, b_no, gain_n, shift_n = [
        to_column(v_vec[i]) for i in range(8)
    ]
    n_valid = counts[0]
    for i in range(1, counts.shape[0]):
        n_valid += counts[i]
    for i, column in (
        (C_GAIN_N, gain_n),
        (C_SHIFT_N, shift_n),
        (C_VALID, jnp.where(inside, kl_weight[0], 0.0)),
        (C_COUNT, jnp.full((D, LANES), (D * rows * n_lon * n_valid).astype(F32))),
        (
            C_DIVERGED,
            0.5 * jnp.sum(total - rows * jnp.where(inside, 1.0, 0.0), axis=1, keepdims=True),
        ),
    ):
        columns[i] = jnp.broadcast_to(column, (D, LANES))
    w_in = v_ei[...]
    w_e, w_s, w_r = w_in[:, :D], w_in[:, D : 2 * D], w_in[:, 2 * D :]
    a_state = jnp.concatenate([weight_pack(0.5 * w_s), weight_pack(0.5 * w_r)], axis=0)
    w_o = v_eo[...]
    w_oc = w_o - jnp.mean(w_o, axis=0, keepdims=True)
    b_oc = b_eo - jnp.mean(b_eo, axis=0, keepdims=True)
    back = 0.5 * exact(w_o, w_oc, ((0,), (0,)))
    b_back = 0.5 * exact(w_o, b_oc, ((0,), (0,)))
    w_n = v_ni[...]
    w_nt = w_n.T
    gain_row, shift_row = v_vec[2], v_vec[3]
    one_row = jnp.ones_like(gain_row)
    scale_row = jnp.concatenate([one_row, gain_row], axis=1)
    add_row = jnp.concatenate([0.0 * one_row, shift_row], axis=1)
    columns[C_WEIGHT_N] = w_n
    row_id = lax.broadcasted_iota(jnp.int32, (D, LANES), 0)
    columns[C_ROWS] = jnp.where(row_id == 0, scale_row, jnp.where(row_id == 1, add_row, 0.0))
    w_shift = jnp.sum(w_n * add_row, axis=1, keepdims=True)
    w_out = v_no[...]
    scaled = gain_e * w_nt[D:]
    scaled = scaled - jnp.mean(scaled, axis=0, keepdims=True)

    def put(place, *parts):
        value = jnp.concatenate(parts, axis=0) if len(parts) > 1 else parts[0]
        pack[place[0] : place[1], : value.shape[1]] = value

    put(P_EDGE, weight_pack(0.5 * w_e))
    put(P_HIDDEN, weight_pack(w_oc, b_oc), weight_pack(back, b_back))
    put(P_EDGE_T, weight_pack(w_e.T))
    put(P_SEND_T, weight_pack(w_s.T))
    put(P_RECV_T, weight_pack(w_r.T))
    node_in = weight_pack(0.5 * w_n * scale_row, 0.5 * b_ni, 0.5 * w_shift)
    put(P_NODE_IN, node_in[:, :P_LANES])
    put(P_NODE_IN_END, node_in[:, P_LANES:])
    put(
        P_NODE_OUT,
        weight_pack(
            w_out - jnp.mean(w_out, axis=0, keepdims=True),
            b_no - jnp.mean(b_no, axis=0, keepdims=True),
        ),
    )
    put(P_NODE_OUT_T, weight_pack(0.5 * w_out.T))
    put(
        P_NODE_IN_T,
        weight_pack(w_nt[:D]),
        weight_pack(scaled),
        weight_pack(0.5 * exact(w_o, scaled, ((0,), (0,)))),
    )
    pltpu.make_async_copy(pack, pack_out, out_sem).start()
    pltpu.make_async_copy(columns, columns_out, out_sem).start()

    waits(nb, slot_sem)
    waits(mk, slot_sem)
    before = counts[lax.rem(blk + n_blk - 1, n_blk)]
    after = counts[lax.rem(blk + 1, n_blk)]
    row_id = lax.broadcasted_iota(jnp.int32, (rows, LANES), 0)
    col_id = lax.broadcasted_iota(jnp.int32, (rows, LANES), 1)
    above = jnp.where(row_id == 0, before, count)
    below = jnp.where(row_id == rows - 1, after, count)
    for k in range(NBR):
        delta = nb[k] - (row_id * (LANES + 2) + col_id)
        first = delta < LANES + 2
        middle = delta < 2 * (LANES + 2)
        step = jnp.where(
            first, delta, jnp.where(middle, delta - (LANES + 2), delta - 2 * (LANES + 2))
        )
        codes[k] = jnp.where(first, step, jnp.where(middle, 3 + (step >> 1), 5 + step))
        owner = col_id + step - 1
        owner = jnp.where(owner < 0, LANES - 1, jnp.where(owner >= LANES, 0, owner))
        limit = jnp.where(first, above, jnp.where(middle, count, below))
        valid[k] = jnp.where((col_id < count) & (owner < limit), mk[k].astype(F32), 0.0)
    for k in range(NBR, 8):
        codes[k] = jnp.zeros((rows, LANES), jnp.int32)
        valid[k] = jnp.zeros((rows, LANES), F32)
    for k in range(8):
        pltpu.make_async_copy(codes.at[k], codes_out.at[:, k, :], out_sem).start()
        pltpu.make_async_copy(valid.at[k], valid_out.at[:, k, :], out_sem).start()

    half_bias = 0.5 * b_ei

    def project(i, _):
        high, low = halves(
            jnp.concatenate([state[1 + 4 * i + u] for u in range(4)], axis=1)
        )
        both = mxu(a_state, jnp.concatenate([high, low, high], axis=0))
        for u in range(4):
            s = slice(u * LANES, (u + 1) * LANES)
            projected[1 + 4 * i + u] = both[:D, s]
            receiver[4 * i + u] = both[D:, s] + half_bias

    lax.fori_loop(0, rows // 4, project, None)
    pltpu.make_async_copy(projected.at[inner], project_out.at[inner], out_sem).start()
    pltpu.make_async_copy(receiver, receive_out, out_sem).start()

    for copy in copies:
        copy.wait()
    state[rows + 1] = rows_in[0]
    state[0] = rows_in[1]
    from_east = unpack_column(cols_in[0])
    from_west = unpack_column(cols_in[1])
    cols[1] = (
        pltpu.roll(jnp.where((lane >= 1) & (lane <= rows), from_east, 0.0), LANES - 1, 1)
        + corner_at(corners_in.at[0], 0, rows)
        + corner_at(corners_in.at[2], 2, LANES - 1)
    )
    cols[0] = (
        pltpu.roll(jnp.where(lane < rows, from_west, 0.0), 1, 1)
        + corner_at(corners_in.at[1], 1, rows + 1)
        + corner_at(corners_in.at[3], 3, 0)
    )
    high, low = halves(
        jnp.concatenate([rows_in[1], rows_in[0], cols[0], cols[1]], axis=1)
    )
    rim = mxu(a_state[:D], jnp.concatenate([high, low, high], axis=0))
    projected[0] = rim[:, :LANES]
    projected[rows + 1] = rim[:, LANES : 2 * LANES]
    sides[0] = rim[:, 2 * LANES : 3 * LANES]
    sides[1] = rim[:, 3 * LANES :]
    for t in (0, rows + 1):
        pltpu.make_async_copy(projected.at[t], project_out.at[t], out_sem).start()
        pltpu.make_async_copy(state.at[t], state_out.at[t], out_sem).start()
    pltpu.make_async_copy(sides, sides_out, out_sem).start()
    pltpu.make_async_copy(cols, cols_out, out_sem).start()
    for ref in (pack, columns, codes, valid, receiver, state, projected, cols, sides):
        waits(ref, out_sem)


def start_call(n_blk, n_lon, counts, kl_weight, nodes, mean, logstd, noise, neighbors, mask, weights):
    rows = nodes.shape[1]
    tile = (D, LANES)
    shapes = (
        ((rows + 2, *tile), F32),
        ((2, *tile), F32),
        ((rows + 2, *tile), F32),
        ((rows, *tile), F32),
        ((2, *tile), F32),
        ((rows, 8, LANES), jnp.int32),
        ((rows, 8, LANES), F32),
        ((P_ROWS, P_LANES), BF16),
        ((C_TILES, *tile), F32),
    )
    vmem = lambda *dims: pltpu.VMEM(dims, F32)
    ints = lambda *dims: pltpu.VMEM(dims, jnp.int32)
    dma = pltpu.SemaphoreType.DMA
    return pl.pallas_call(
        functools.partial(start_kernel, n_blk, n_lon),
        name="start",
        out_shape=[jax.ShapeDtypeStruct(*shape) for shape in shapes],
        in_specs=[SMEM, SMEM] + [HBM] * (6 + len(weights)),
        out_specs=[HBM] * len(shapes),
        scratch_shapes=[
            vmem(rows // 8, 4, D, 8, LANES),
            vmem(rows + 2, *tile),
            vmem(rows + 2, *tile),
            vmem(rows, *tile),
            vmem(2, *tile),
            ints(NBR, rows, LANES),
            ints(NBR, rows, LANES),
            ints(8, rows, LANES),
            vmem(8, rows, LANES),
            vmem(D, 3 * D),
            vmem(D, D),
            vmem(D, 2 * D),
            vmem(D, D),
            vmem(8, 1, D),
            pltpu.VMEM((P_ROWS, P_LANES), BF16),
            vmem(C_TILES, *tile),
            vmem(2, *tile),
            vmem(2, *tile),
            vmem(2, D // 2, LANES),
            vmem(8, LANES),
            vmem(2, *tile),
            vmem(2, D // 2, LANES),
            vmem(4, 8, LANES),
            dma((rows // 8,)),
            dma,
            dma,
            dma((8,)),
            dma((8,)),
            dma,
        ],
        compiler_params=pltpu.CompilerParams(
            collective_id=0, has_side_effects=True, vmem_limit_bytes=ROOM
        ),
    )(counts, kl_weight, nodes, mean, logstd, noise, neighbors, mask, *weights)


def layer_kernel(
    edges,
    cotangent,
    project_in,
    receive_in,
    sides_in,
    codes_in,
    valid_in,
    pack_in,
    columns_in,
    state_in,
    new_states,
    grad_edges,
    part_out,
    recv_out,
    own_out,
    cells_out,
    acc_out,
    slope,
    xs,
    hs,
    cb,
    db,
    staged,
    windows,
    projected,
    receiver,
    sides,
    codes,
    valid,
    pack,
    columns,
    state,
    inverse,
    summed,
    qc_ref,
    qo_ref,
    cot,
    fresh,
    part,
    placed,
    cells,
    grad_recv,
    gather_grads,
    acc_edge,
    acc_hidden,
    acc_nin,
    acc_nout,
    acc_vec,
    acc,
    row_sem,
    edge_sem,
    in_sem,
    out_sem,
):
    rows = cotangent.shape[1]
    wide = NBR * LANES
    two = 2 * LANES
    lane = lane_ids()

    halfway = 14
    ahead = 8

    def load_edges(r):
        for k in range(NBR):
            pltpu.make_async_copy(
                edges.at[:, k, r, :],
                staged.at[r, :, pl.ds(k * LANES, LANES)],
                edge_sem.at[r],
            ).start()

    first_weights = pl.ds(P_HIDDEN[0], P_EDGE[1])
    first_small = (
        (sides_in, sides),
        (pack_in.at[first_weights], pack.at[first_weights]),
        (codes_in, codes),
        (valid_in, valid),
    )
    parts = []
    for g, (first, last) in enumerate(((0, halfway), (halfway, rows + 2))):
        send, receive = pl.ds(first, last - first), pl.ds(first, min(last, rows) - first)
        part_g = ((project_in, projected, send), (receive_in, receiver, receive))
        for source, target, span in part_g:
            pltpu.make_async_copy(source.at[span], target.at[span], row_sem.at[g]).start()
        parts.append([target.at[span] for _, target, span in part_g])
        if g == 0:
            for source, target in first_small[:2]:
                pltpu.make_async_copy(source, target, in_sem.at[0]).start()
            for r in range(4):
                load_edges(r)
            for source, target in first_small[2:]:
                pltpu.make_async_copy(source, target, in_sem.at[0]).start()
    for r in range(4, ahead + 4):
        load_edges(r)

    def load_rest():
        rest = pl.ds(P_EDGE[1], P_ROWS - P_EDGE[1])
        pltpu.make_async_copy(pack_in.at[rest], pack.at[rest], in_sem.at[1]).start()
        pltpu.make_async_copy(columns_in, columns, in_sem.at[1]).start()
        pltpu.make_async_copy(state_in, state, in_sem.at[1]).start()

        for g in range(rows // 8):
            pltpu.make_async_copy(
                cotangent.at[:, pl.ds(8 * g, 8), :], cot.at[g], in_sem.at[1]
            ).start()
        return (cot, state, columns, pack.at[rest])

    ones16 = jnp.where(
        lax.broadcasted_iota(jnp.int32, (16, wide), 0) < 2, 1.0, 0.0
    ).astype(BF16)
    ones_two = ones16[:, :two]
    for _, target in first_small:
        waits(target, in_sem.at[0])

    def shift(t):
        centre = projected[t]
        mix = pltpu.roll(
            jnp.where(lane == t, sides[0], sides[1]), lax.rem(LANES - t, LANES), 1
        )
        windows[t, 1] = centre
        windows[t, 0] = jnp.where(lane == 0, mix, pltpu.roll(centre, 1, 1))
        windows[t, 2] = jnp.where(lane == LANES - 1, mix, pltpu.roll(centre, LANES - 1, 1))

    def edge_product(r, pair):
        own = receiver[r]
        s = pl.ds(pair * two, two)
        high, low = halves(staged[r, :, s])
        xs[r, :D, s] = high
        xs[r, D:, s] = low
        out = mxu(packed_rows(pack, P_EDGE), jnp.concatenate([high, low, high], axis=0))
        slope[r, :, s] = out + jnp.concatenate([own, own], axis=1)

    def hidden_values(r, pair):
        slots = (2 * pair, 2 * pair + 1)
        hidden = {k: [None] * 8 for k in slots}
        masks = {}
        for k in slots:
            code = jnp.broadcast_to(codes[r, pl.ds(k, 1), :], (8, LANES))
            masks[k] = ((code & 1) != 0, (code & 2) != 0, (code & 4) != 0)
        for f in range(8):
            rows_f = pl.ds(8 * f, 8)
            w = [windows[r + 1 + dr, 1 + dc, rows_f, :] for dr, dc in WINDOWS]
            for k in slots:
                s = pl.ds(k * LANES, LANES)
                b0, b1, b2 = masks[k]
                low = jnp.where(b1, jnp.where(b0, w[3], w[2]), jnp.where(b0, w[1], w[0]))
                top = jnp.where(b1, jnp.where(b0, w[7], w[6]), jnp.where(b0, w[5], w[4]))
                pre = slope[r, rows_f, s] + jnp.where(b2, top, low)
                t = jnp.tanh(pre)
                u = 1.0 + t
                h = pre * u
                slope[r, rows_f, s] = u + h * (1.0 - t)
                hidden[k][f] = h
        s = pl.ds(pair * two, two)
        high, low = halves(
            jnp.concatenate([jnp.concatenate(hidden[k], axis=0) for k in slots], axis=1)
        )
        hs[r, :D, s] = high
        hs[r, D : 2 * D, s] = low
        hs[r, 2 * D :, s] = ones_two

    def hidden_product(r, pair):
        s = pl.ds(pair * two, two)
        both = mxu(
            packed_rows(pack, P_HIDDEN, 3 * D + 16),
            jnp.concatenate([hs[r, :, s], hs[r, :D, s]], axis=0),
        )
        cb[r, :, s] = both[:D]
        db[r, :, s] = both[D:]
        return r, pair, both[:D]

    def norm(r, pair, pair_c, total):
        for j in range(2):
            k = 2 * pair + j
            c = pair_c[:, j * LANES : (j + 1) * LANES]
            variance = jnp.sum(c * c, axis=0, keepdims=True) * (1.0 / D)
            inv = lax.rsqrt(variance + EPS)
            inverse[r, pl.ds(k, 1), :] = inv
            term = (inv * valid[r, pl.ds(k, 1), :]) * c
            total = term if total is None else total + term
        if pair == NBR // 2 - 1:
            summed[r] = total
            total = None
        return total

    def forward(i, _, first=0, last=2, more=True):
        turn = [4 * i + u for u in range(4)]
        if first == 0:
            for r in turn:
                if more:
                    load_edges(r + 4 + ahead)
                waits(staged.at[r + 4], edge_sem.at[r + 4])
            for r in turn:
                shift(r + 6)
        units = [(r, pair) for r in turn for pair in range(NBR // 2)]
        products = []
        total = None
        if last >= 2:
            products.append(hidden_product(units[0][0] - 4, units[0][1]))
        for i_unit, (r, pair) in enumerate(units):
            if last >= 2 and i_unit + 1 < len(units):
                ahead_r, ahead_pair = units[i_unit + 1]
                products.append(hidden_product(ahead_r - 4, ahead_pair))
            if first <= 1 <= last:
                if pair == 0:
                    placed[r + 2] = jnp.zeros((3, D, LANES), F32)
                hidden_values(r, pair)
            if last >= 2:
                total = norm(*products[i_unit], total)
            if first == 0:
                edge_product(r + 4, pair)

    for ref in parts[0]:
        waits(ref, row_sem.at[0])
    for t in range(6):
        shift(t)
    for r in range(2):
        placed[r] = jnp.zeros((3, D, LANES), F32)
    for r in range(4):
        waits(staged.at[r], edge_sem.at[r])
        for pair in range(NBR // 2):
            edge_product(r, pair)
    for ref in parts[1]:
        waits(ref, row_sem.at[1])
    node_inputs = load_rest()
    forward(0, None, last=1)
    turns = rows // 4
    full = turns - 1 - ahead // 4
    lax.fori_loop(1, full, forward, None)
    lax.fori_loop(full, turns - 1, functools.partial(forward, more=False), None)
    forward(turns - 1, None, first=1)
    forward(turns, None, first=2)

    for ref in (acc_edge, acc_hidden, acc_nin, acc_nout, acc_vec):
        ref[...] = jnp.zeros_like(ref)
    for ref in node_inputs:
        waits(ref, in_sem.at[1])
    chunk = 4
    span = chunk * LANES

    def node_chunk(first):
        tile_cols = lambda i: jnp.concatenate([columns[i]] * chunk, axis=1)
        spread = lambda ref, offset: jnp.concatenate(
            [ref[first + offset + j] for j in range(chunk)], axis=1
        )
        degree = jnp.concatenate(
            [jnp.sum(valid[first + j], axis=0, keepdims=True) for j in range(chunk)], axis=1
        )
        st_high, st_low = halves(spread(state, 1))
        sum_high, sum_low = halves(spread(summed, 0))
        place = lax.broadcasted_iota(jnp.int32, (16, span), 0)
        extra = jnp.where(place < 2, 1.0, jnp.where(place < 4, degree, 0.0)).astype(BF16)
        tops = jnp.concatenate([st_high, sum_high], axis=0)
        ends = jnp.concatenate([st_low, sum_low], axis=0)
        pre = mxu(
            jnp.concatenate(
                [
                    packed_rows(pack, P_NODE_IN, P_LANES),
                    packed_rows(pack, P_NODE_IN_END, 6 * D + 16 - P_LANES),
                ],
                axis=1,
            ),
            jnp.concatenate([tops, ends, extra, tops], axis=0),
        )
        yield
        t = jnp.tanh(pre)
        u = 1.0 + t
        h = pre * u
        slope_n = u + h * (1.0 - t)
        h_high, h_low = halves(h)
        h_all = jnp.concatenate([h_high, h_low, ones16[:, :span]], axis=0)
        c = mxu(
            packed_rows(pack, P_NODE_OUT, 3 * D + 16),
            jnp.concatenate([h_all, h_high], axis=0),
        )
        yield
        cot_c = jnp.concatenate(
            [read_row(cot.at[(first + j) // 8], (first + j) % 8) for j in range(chunk)], axis=1
        )
        inv = lax.rsqrt(jnp.sum(c * c, axis=0, keepdims=True) * (1.0 / D) + EPS)
        n = c * inv
        new = spread(state, 1) + (tile_cols(C_GAIN_N) * n + tile_cols(C_SHIFT_N))
        q = cot_c * tile_cols(C_GAIN_N)
        q = q - jnp.sum(q, axis=0, keepdims=True) * (1.0 / D)
        grad = inv * (q - n * (jnp.sum(q * n, axis=0, keepdims=True) * (1.0 / D)))
        g_high, g_low = halves(grad)
        pre_grad = mxu(
            packed_rows(pack, P_NODE_OUT_T), jnp.concatenate([g_high, g_low, g_high], axis=0)
        )
        for j in range(chunk):
            s = slice(j * LANES, (j + 1) * LANES)
            write_row(fresh.at[(first + j) // 8], (first + j) % 8, new[:, s])
            acc_vec[0] += cot_c[:, s] * n[:, s]
            acc_vec[1] += cot_c[:, s]
        yield
        acc_nout[...] += outer(jnp.concatenate([g_high, g_low], axis=0), h_all)
        pre_grad = pre_grad * slope_n
        p_high, p_low = halves(pre_grad)
        back = mxu(
            packed_rows(pack, P_NODE_IN_T), jnp.concatenate([p_high, p_low, p_high], axis=0)
        )
        for j in range(chunk):
            s = slice(j * LANES, (j + 1) * LANES)
            acc_vec[2] += pre_grad[:, s]
            acc_vec[3] += pre_grad[:, s] * degree[:, s]
        yield
        acc_nin[...] += outer(
            jnp.concatenate([p_high, p_low], axis=0), jnp.concatenate([tops, ends], axis=0)
        )
        for j in range(chunk):
            s = slice(j * LANES, (j + 1) * LANES)
            part[first + j] = cot_c[:, s] + back[:D, s]
            qc_ref[first + j] = back[D : 2 * D, s]
            qo_ref[first + j] = back[2 * D :, s]

    in_flight = []
    for first in range(0, rows + 4 * chunk, chunk):
        if first < rows:
            in_flight.append(node_chunk(first))
        for routine in list(in_flight):
            if next(routine, routine) is routine:
                in_flight.remove(routine)

    for g in range(rows // 8):
        pltpu.make_async_copy(
            fresh.at[g], new_states.at[:, pl.ds(8 * g, 8), :], out_sem
        ).start()
    pltpu.make_async_copy(part, part_out, out_sem).start()

    def grad_unit(r, pair, u, received):
        qc = qc_ref[r]
        qo = qo_ref[r]
        hidden_grads, grads = [], []
        for k in (2 * pair, 2 * pair + 1):
            s = pl.ds(k * LANES, LANES)
            c = cb[r, :, s]
            inv = inverse[r, pl.ds(k, 1), :]
            alpha = inv * valid[r, pl.ds(k, 1), :]
            moment = jnp.sum(qc * c, axis=0, keepdims=True) * (1.0 / D)
            beta = alpha * inv * inv * moment
            hidden_grads.append(alpha * qc - beta * c)
            grad = (alpha * qo - beta * db[r, :, s]) * slope[r, :, s]
            grads.append(grad)
            received = grad if received is None else received + grad
        high, low = halves(jnp.concatenate(hidden_grads, axis=1))
        s = pl.ds(pair * two, two)
        gather_grads[u, :D, s] = high
        gather_grads[u, D : 2 * D, s] = low
        high, low = halves(jnp.concatenate(grads, axis=1))
        gather_grads[u, 2 * D : 3 * D, s] = high
        gather_grads[u, 3 * D :, s] = low
        ge = mxu(
            packed_rows(pack, P_EDGE_T), jnp.concatenate([high, low, high], axis=0)
        )
        return grads, received, ge

    def place_unit(r, pair, grads):
        code = [
            jnp.broadcast_to(codes[r, pl.ds(k, 1), :], (8, LANES))
            for k in (2 * pair, 2 * pair + 1)
        ]
        for which, (dr, dc) in enumerate(WINDOWS):
            masks = [c == which for c in code]
            for f in range(8):
                rows_f = pl.ds(8 * f, 8)
                value = placed[r + 1 + dr, 1 + dc, rows_f, :]
                for j in range(2):
                    value += jnp.where(masks[j], grads[j][8 * f : 8 * f + 8], 0.0)
                placed[r + 1 + dr, 1 + dc, rows_f, :] = value

    def store_unit(r, pair, ge):
        staged[r, :, pl.ds(pair * two, two)] = ge

    def products(r, u):
        r = jnp.maximum(r, 0)
        acc_hidden[...] += outer(gather_grads[u, : 2 * D], hs[r])
        acc_edge[...] += outer(gather_grads[u, 2 * D :], xs[r])

    own = projected

    def settle(t):
        to_west = placed[t, 0]
        to_east = placed[t, 2]
        own[t] = (
            placed[t, 1]
            + jnp.where(lane == 0, 0.0, pltpu.roll(to_east, 1, 1))
            + jnp.where(lane == LANES - 1, 0.0, pltpu.roll(to_west, LANES - 1, 1))
        )
        mix = pltpu.roll(jnp.where(lane == 0, to_west, to_east), t, 1)
        cells[0] = jnp.where(lane == t, mix, cells[0])
        cells[1] = jnp.where(lane == lax.rem(t + LANES - 1, LANES), mix, cells[1])

    def send_rows(i, unroll=4):
        span = pl.ds(unroll * i, unroll)
        pltpu.make_async_copy(grad_recv.at[span], recv_out.at[span], out_sem).start()
        for u in range(unroll):
            r = unroll * i + u
            for k in range(NBR):
                pltpu.make_async_copy(
                    staged.at[r, :, pl.ds(k * LANES, LANES)],
                    grad_edges.at[:, k, r, :],
                    out_sem,
                ).start()

    def backward(i, _, unroll=4):
        if not isinstance(i, int):
            send_rows(i - 1)
            for u in range(unroll):
                settle(unroll * (i - 1) + u)
        pending = None
        for u in range(unroll):
            r = unroll * i + u
            products(r - unroll, u)
            received = None
            for pair in range(NBR // 2):
                grads, received, ge = grad_unit(r, pair, u, received)
                place_unit(r, pair, grads)
                if pending is not None:
                    store_unit(*pending)
                pending = (r, pair, ge)
            grad_recv[r] = received
        store_unit(*pending)
        if not isinstance(i, int):
            span = pl.ds(unroll * (i - 1), unroll)
            pltpu.make_async_copy(own.at[span], own_out.at[span], out_sem).start()

    cells[...] = jnp.zeros_like(cells)
    gather_grads[...] = jnp.zeros_like(gather_grads)
    backward(0, None)
    lax.fori_loop(1, rows // 4, backward, None)
    send_rows(rows // 4 - 1)
    for t in range(rows - 4, rows + 2):
        settle(t)
    tail = pl.ds(rows - 4, 6)
    pltpu.make_async_copy(own.at[tail], own_out.at[tail], out_sem).start()
    pltpu.make_async_copy(cells, cells_out, out_sem).start()
    for u in range(4):
        products(rows - 4 + u, u)

    def folded(ref):
        half = ref[:D, : 2 * D] + ref[D:, : 2 * D]
        return half + pltpu.roll(half, D, 1)

    left = lane < D
    acc[0] = folded(acc_edge)
    plain = (
        acc_nin[:D, : 2 * D]
        + acc_nin[D:, : 2 * D]
        + acc_nin[:D, 2 * D :]
        + acc_nin[D:, 2 * D :]
    )
    pick = lambda ref, start, i: jnp.sum(
        jnp.where(lane[:, :16] == i, ref[:D, start:] + ref[D:, start:], 0.0),
        axis=1,
        keepdims=True,
    )
    lane_sum = lambda i: jnp.sum(acc_vec[i], axis=1, keepdims=True)
    by_degree = lane_sum(3)
    acc[2] = plain * columns[C_ROWS, 0:1, :] + by_degree * columns[C_ROWS, 1:2, :]
    acc[3] = jnp.where(left, folded(acc_hidden), folded(acc_nout))
    weight_n = columns[C_WEIGHT_N]
    gain_row = jnp.sum(weight_n * plain, axis=0, keepdims=True)[:, D:]
    shift_row = jnp.sum(weight_n * by_degree, axis=0, keepdims=True)[:, D:]
    block = jnp.zeros((D, LANES), F32)
    for i, vector in (
        (1, pick(acc_hidden, 2 * D, 0)),
        (2, to_column(gain_row)),
        (3, to_column(shift_row)),
        (4, lane_sum(2)),
        (5, pick(acc_nout, 2 * D, 0)),
        (6, lane_sum(0)),
        (7, lane_sum(1)),
        (8, columns[C_DIVERGED]),
    ):
        block = jnp.where(lane == D + i, vector, block)
    acc[1] = block
    pltpu.make_async_copy(acc, acc_out, out_sem).start()
    for ref in (fresh, part, grad_recv, own.at[pl.ds(0, rows + 2)], cells, staged, acc):
        waits(ref, out_sem)


def layer_call(edges, cotangent, projected, receiver, sides, codes, valid, pack, columns, state):
    rows = cotangent.shape[1]
    wide = NBR * LANES
    tile = (D, LANES)
    shape = lambda *dims: jax.ShapeDtypeStruct(dims, F32)
    vmem = lambda *dims: pltpu.VMEM(dims, F32)
    return pl.pallas_call(
        layer_kernel,
        name="layer",
        out_shape=(
            shape(D, rows, LANES),
            shape(D, NBR, rows, LANES),
            shape(rows, *tile),
            shape(rows, *tile),
            shape(rows + 2, *tile),
            shape(2, *tile),
            shape(4, *tile),
        ),
        in_specs=[HBM] * 10,
        out_specs=[HBM] * 7,
        scratch_shapes=[
            vmem(rows, D, wide),
            pltpu.VMEM((rows, 2 * D, wide), BF16),
            pltpu.VMEM((rows, 2 * D + 16, wide), BF16),
            vmem(rows, D, wide),
            vmem(rows, D, wide),
            vmem(rows, D, wide),
            vmem(rows + 6, 3, *tile),
            vmem(rows + 6, *tile),
            vmem(rows, *tile),
            vmem(2, *tile),
            pltpu.VMEM((rows, 8, LANES), jnp.int32),
            vmem(rows, 8, LANES),
            pltpu.VMEM((P_ROWS, P_LANES), BF16),
            vmem(C_TILES, *tile),
            vmem(rows + 2, *tile),
            vmem(rows, 8, LANES),
            vmem(rows, *tile),
            vmem(rows, *tile),
            vmem(rows, *tile),
            vmem(rows // 8, D, 8, LANES),
            vmem(rows // 8, D, 8, LANES),
            vmem(rows, *tile),
            vmem(rows + 2, 3, *tile),
            vmem(2, *tile),
            vmem(rows, *tile),
            pltpu.VMEM((4, 4 * D, wide), BF16),
            vmem(2 * D, 2 * D),
            vmem(2 * D, 2 * D + 16),
            vmem(2 * D, 4 * D),
            vmem(2 * D, 2 * D + 16),
            vmem(4, *tile),
            vmem(4, *tile),
            pltpu.SemaphoreType.DMA((2,)),
            pltpu.SemaphoreType.DMA((rows,)),
            pltpu.SemaphoreType.DMA((2,)),
            pltpu.SemaphoreType.DMA,
        ],
        compiler_params=pltpu.CompilerParams(vmem_limit_bytes=ROOM),
    )(edges, cotangent, projected, receiver, sides, codes, valid, pack, columns, state)


def sum_kernel(
    n_blk,
    n_lon,
    acc_in,
    own_in,
    cells_in,
    recv_in,
    part_in,
    state_in,
    cols_all,
    pack_in,
    part_out,
    total_out,
    acc,
    own,
    cells,
    grad_recv,
    part,
    natural,
    state,
    cols,
    pack,
    edge_rows,
    edge_cols,
    edge_corners,
    rows_in,
    cols_in,
    corners_in,
    acc_send,
    acc_recv,
    packed,
    scattered,
    across,
    gathered,
    in_sem,
    row_sem,
    rs_send,
    rs_recv,
    x_send,
    x_recv,
    ag_send,
    ag_recv,
    halo_send,
    halo_recv,
    out_sem,
):
    rows = recv_in.shape[0]
    blk, lon, around = neighbours(n_blk, n_lon)
    size = scattered.shape[0]
    n_groups = across.shape[0]
    per = size // n_lon
    me = lax.rem(blk, per) * n_lon + lon
    own_group = blk // per
    lane = lane_ids()

    def member(index):
        return (own_group * per + index // n_lon, lax.rem(index, n_lon))

    def other(step):
        return lax.rem(me + step, size)

    def peer(step):
        return (lax.rem(own_group + step, n_groups) * per + lax.rem(blk, per), lon)

    half = rows // 2
    for h in range(2):
        span = pl.ds(h * half, half)
        span3 = pl.ds(0, half + 1) if h == 0 else pl.ds(half + 1, half + 1)
        for source, target in (
            (own_in.at[span3], own.at[span3]),
            (state_in.at[span3], state.at[span3]),
            (recv_in.at[span], grad_recv.at[span]),
        ):
            pltpu.make_async_copy(source, target, row_sem.at[h]).start()
    small = (
        (pack_in.at[pl.ds(P_SEND_T[0], 2 * D)], pack),
        (cols_all, cols),
        (acc_in, acc),
        (part_in, part),
        (cells_in, cells),
    )
    for i, (source, target) in enumerate(small):
        pltpu.make_async_copy(source, target, in_sem.at[i]).start()

    barrier = pltpu.get_barrier_semaphore()

    def greet(step, _):
        pl.semaphore_signal(
            barrier, inc=1, device_id=member(other(step)), device_id_type=MESH
        )

    lax.fori_loop(1, size, greet, None)
    expected = size - 1
    if n_groups > 1:
        for place in around:
            pl.semaphore_signal(barrier, inc=1, device_id=place, device_id_type=MESH)

        def greet_group(step, _):
            pl.semaphore_signal(barrier, inc=1, device_id=peer(step), device_id_type=MESH)

        lax.fori_loop(1, n_groups, greet_group, None)
        expected += 8 + n_groups - 1

    acc_send[...] = jnp.zeros_like(acc_send)
    acc_recv[...] = jnp.zeros_like(acc_recv)

    def both_halves(value):
        return jnp.concatenate(halves(value), axis=0)

    ones_row = jnp.where(
        lax.broadcasted_iota(jnp.int32, (16, 4 * LANES), 0) < 1, 1.0, 0.0
    ).astype(BF16)

    def collect(i, _):
        wide = lambda ref, first: both_halves(
            jnp.concatenate([ref[first + u] for u in range(4)], axis=1)
        )
        there = wide(state, 1 + 4 * i)
        acc_send[...] += outer(wide(own, 1 + 4 * i), there)
        acc_recv[...] += outer(
            wide(grad_recv, 4 * i), jnp.concatenate([there, ones_row], axis=0)
        )

    for h in range(2):
        waits(own.at[pl.ds(h * (half + 1), half + 1)], row_sem.at[h])
        waits(state.at[pl.ds(h * (half + 1), half + 1)], row_sem.at[h])
        waits(grad_recv.at[pl.ds(h * half, half)], row_sem.at[h])
        lax.fori_loop(h * half // 4, (h + 1) * half // 4, collect, None)
    waits(cells, in_sem.at[4])
    waits(cols, in_sem.at[1])
    edge_values = jnp.concatenate([own[0], own[rows + 1], cells[0], cells[1]], axis=1)
    edge_states = jnp.concatenate([state[0], state[rows + 1], cols[0], cols[1]], axis=1)
    acc_send[...] += outer(both_halves(edge_values), both_halves(edge_states))

    def folded(ref):
        part_sum = ref[:D, : 2 * D] + ref[D:, : 2 * D]
        return part_sum + pltpu.roll(part_sum, D, 1)

    left = lane < D
    waits(acc, in_sem.at[2])
    ones_sum = jnp.sum(
        jnp.where(lane[:, :16] == 0, acc_recv[:D, 2 * D :] + acc_recv[D:, 2 * D :], 0.0),
        axis=1,
        keepdims=True,
    )
    chunk = packed.shape[1]
    blocks = (
        jnp.where(left, acc[0], folded(acc_send)),
        jnp.where(left, folded(acc_recv), jnp.where(lane == D, ones_sum, acc[1])),
        acc[2],
        acc[3],
    )
    per_block = D // chunk
    for i, block in enumerate(blocks):
        for j in range(per_block):
            packed[i * per_block + j] = block[j * chunk : (j + 1) * chunk]
    pl.semaphore_wait(barrier, expected)

    def scatter(step, _):
        target = other(step)
        pltpu.make_async_remote_copy(
            src_ref=packed.at[target],
            dst_ref=scattered.at[me],
            send_sem=rs_send,
            recv_sem=rs_recv,
            device_id=member(target),
            device_id_type=MESH,
        ).start()

    lax.fori_loop(1, size, scatter, None)
    scattered[me] = packed[me]

    waits(pack, in_sem.at[0])
    a_send = pack[:D, : 3 * D]
    a_recv = pack[D : 2 * D, : 3 * D]
    high, low = halves(edge_values)
    edge_grads = mxu(a_send, jnp.concatenate([high, low, high], axis=0))
    edge_grad = [edge_grads[:, i * LANES : (i + 1) * LANES] for i in range(4)]
    edge_rows[0], edge_rows[1] = edge_grad[0], edge_grad[1]
    west_cells, east_cells = edge_grad[2], edge_grad[3]
    edge_cols[0], edge_cols[1] = pack_column(west_cells), pack_column(east_cells)
    edge_corners[...] = corner_rows(
        [
            west_cells[:, :1],
            east_cells[:, LANES - 1 :],
            west_cells[:, rows + 1 : rows + 2],
            east_cells[:, rows : rows + 1],
        ]
    )
    copies = rim_copies(
        around,
        edge_rows,
        edge_cols,
        edge_corners,
        rows_in,
        cols_in,
        corners_in,
        halo_send,
        halo_recv,
    )
    for copy in copies:
        copy.start()
    waits(part, in_sem.at[3])

    def finish(i, _):
        for u in range(2):
            first = 4 * i + 2 * u
            grads = None
            for weights, ref, offset in ((a_send, own, 1), (a_recv, grad_recv, 0)):
                high, low = halves(
                    jnp.concatenate([ref[first + offset], ref[first + offset + 1]], axis=1)
                )
                product = mxu(weights, jnp.concatenate([high, low, high], axis=0))
                grads = product if grads is None else grads + product
            for j in range(2):
                part[first + j] += grads[:, j * LANES : (j + 1) * LANES]

    lax.fori_loop(0, rows // 4, finish, None)

    others = pl.ds(0, size - 1)
    waits(scattered.at[others], rs_recv)
    mine = scattered[0]
    for i in range(1, size):
        mine = mine + scattered[i]
    if n_groups > 1:
        across[own_group] = mine

        def cross(step, _):
            pltpu.make_async_remote_copy(
                src_ref=across.at[own_group],
                dst_ref=across.at[own_group],
                send_sem=x_send,
                recv_sem=x_recv,
                device_id=peer(step),
                device_id_type=MESH,
            ).start()

        lax.fori_loop(1, n_groups, cross, None)
        rest = pl.ds(0, n_groups - 1)
        waits(across.at[rest], x_recv)
        waits(across.at[rest], x_send)
        mine = across[0]
        for i in range(1, n_groups):
            mine = mine + across[i]
    gathered[me] = mine

    def gather(step, _):
        pltpu.make_async_remote_copy(
            src_ref=gathered.at[me],
            dst_ref=gathered.at[me],
            send_sem=ag_send,
            recv_sem=ag_recv,
            device_id=member(other(step)),
            device_id_type=MESH,
        ).start()

    lax.fori_loop(1, size, gather, None)
    for copy in copies:
        copy.wait()
    west_in = (
        pltpu.roll(jnp.where(lane < rows, unpack_column(cols_in[1]), 0.0), 1, 1)
        + corner_at(corners_in.at[3], 3, 1)
        + corner_at(corners_in.at[1], 1, rows)
    )
    east_in = unpack_column(cols_in[0])
    east_in = (
        pltpu.roll(jnp.where((lane >= 1) & (lane <= rows), east_in, 0.0), LANES - 1, 1)
        + corner_at(corners_in.at[2], 2, 0)
        + corner_at(corners_in.at[0], 0, rows - 1)
    )
    rim = (lane == 0) | (lane == LANES - 1)
    part[0] += rows_in[1]
    part[rows - 1] += rows_in[0]

    def add_columns(i, _):
        for u in range(4):
            r = 4 * i + u
            mix = pltpu.roll(
                jnp.where(lane == r + 1, west_in, east_in), LANES - 1 - r, 1
            )
            write_row(natural.at[r // 8], lax.rem(r, 8), part[r] + jnp.where(rim, mix, 0.0))

    lax.fori_loop(0, rows // 4, add_columns, None)
    for g in range(rows // 8):
        pltpu.make_async_copy(
            natural.at[g], part_out.at[:, pl.ds(8 * g, 8), :], out_sem
        ).start()
    waits(gathered.at[others], ag_recv)
    pltpu.make_async_copy(gathered, total_out, out_sem).start()
    waits(scattered.at[others], rs_send)
    waits(gathered.at[others], ag_send)
    for ref in (part, gathered):
        waits(ref, out_sem)


def sum_call(n_blk, n_lon, acc, own, cells, recv, part, state, cols, pack):
    rows = recv.shape[0]
    size = min(32, n_blk * n_lon)
    n_groups = n_blk * n_lon // size
    chunk = (4 * D // size, LANES)
    tile = (D, LANES)
    shape = lambda *dims: jax.ShapeDtypeStruct(dims, F32)
    vmem = lambda *dims: pltpu.VMEM(dims, F32)
    dma = pltpu.SemaphoreType.DMA
    return pl.pallas_call(
        functools.partial(sum_kernel, n_blk, n_lon),
        name="sums",
        out_shape=(shape(D, rows, LANES), shape(size, *chunk)),
        in_specs=[HBM] * 8,
        out_specs=[HBM] * 2,
        scratch_shapes=[
            vmem(4, *tile),
            vmem(rows + 2, *tile),
            vmem(2, *tile),
            vmem(rows, *tile),
            vmem(rows, *tile),
            vmem(rows // 8, D, 8, LANES),
            vmem(rows + 2, *tile),
            vmem(2, *tile),
            pltpu.VMEM((2 * D, P_LANES), BF16),
            vmem(2, *tile),
            vmem(2, D // 2, LANES),
            vmem(8, LANES),
            vmem(2, *tile),
            vmem(2, D // 2, LANES),
            vmem(4, 8, LANES),
            vmem(2 * D, 2 * D),
            vmem(2 * D, 2 * D + 16),
            vmem(size, *chunk),
            vmem(size, *chunk),
            vmem(n_groups, *chunk),
            vmem(size, *chunk),
            dma((5,)),
            dma((2,)),
            dma,
            dma,
            dma,
            dma,
            dma,
            dma,
            dma((8,)),
            dma((8,)),
            dma,
        ],
        compiler_params=pltpu.CompilerParams(
            collective_id=1, has_side_effects=True, vmem_limit_bytes=ROOM
        ),
    )(acc, own, cells, recv, part, state, cols, pack)


def final_kernel(
    part_nodes,
    mean,
    logstd,
    noise,
    total_in,
    columns_in,
    *rest,
):
    grad_nodes, grad_mean, grad_logstd = rest[:3]
    small_outs = rest[3:16]
    grad, mean_v, logstd_v, noise_v, total, columns = rest[16:22]
    smalls = rest[22:35]
    in_sem, small_sem, out_sem = rest[35:]
    n_chunks = in_sem.shape[0]
    depth = D // n_chunks
    for i, (source, target) in enumerate(((columns_in, columns), (total_in, total))):
        pltpu.make_async_copy(source, target, small_sem.at[i]).start()
    spans = [pl.ds(i * depth, depth) for i in range(n_chunks)]
    pairs = ((part_nodes, grad), (mean, mean_v), (logstd, logstd_v), (noise, noise_v))
    for i, span in enumerate(spans):
        for source, target in pairs:
            pltpu.make_async_copy(source.at[span], target.at[span], in_sem.at[i]).start()

    waits(columns, small_sem.at[0])
    waits(total, small_sem.at[1])
    kl_value, g_w_ei, g_w_eo, g_w_ni, g_w_no = smalls[:5]
    chunk = total.shape[1]
    per_block = D // chunk
    blocks = [
        jnp.concatenate([total[i * per_block + j] for j in range(per_block)], axis=0)
        for i in range(4)
    ]
    g_w_ei[:, : 2 * D] = blocks[0]
    g_w_ei[:, 2 * D :] = blocks[1][:, :D]
    g_w_ni[...] = blocks[2]
    g_w_eo[...] = blocks[3][:, :D]
    g_w_no[...] = pltpu.roll(blocks[3], D, 1)[:, :D]
    for i in range(8):
        smalls[5 + i][...] = to_row(blocks[1][:, D + i : D + i + 1])
    diverged = jnp.sum(blocks[1][:, D + 8 : D + 9], axis=0, keepdims=True)
    kl_value[...] = diverged / columns[C_COUNT, 0:1, 0:1]
    for source, target in zip(smalls, small_outs):
        pltpu.make_async_copy(source, target, out_sem).start()

    inside = columns[C_VALID, 0:1, :].reshape(1, 1, LANES)
    for i, span in enumerate(spans):
        for _, target in pairs:
            waits(target.at[span], in_sem.at[i])
        pltpu.make_async_copy(grad.at[span], grad_nodes.at[span], out_sem).start()
        for f in range(i * depth, (i + 1) * depth):
            one = pl.ds(f, 1)
            g = grad[one]
            spread = jnp.exp(logstd_v[one])
            mean_v[one] = g + inside * mean_v[one]
            logstd_v[one] = g * spread * noise_v[one] + inside * (spread * spread - 1.0)
        pltpu.make_async_copy(mean_v.at[span], grad_mean.at[span], out_sem).start()
        pltpu.make_async_copy(logstd_v.at[span], grad_logstd.at[span], out_sem).start()
    for ref in (grad, mean_v, logstd_v, *smalls):
        waits(ref, out_sem)


def final_call(part_nodes, mean, logstd, noise, total, columns):
    shape = lambda *dims: jax.ShapeDtypeStruct(dims, F32)
    vmem = lambda *dims: pltpu.VMEM(dims, F32)
    whole = mean.shape
    small = ((1, 1), (D, 3 * D), (D, D), (D, 2 * D), (D, D)) + ((1, D),) * 8
    return pl.pallas_call(
        final_kernel,
        name="final",
        out_shape=[shape(*dims) for dims in (whole,) * 3 + small],
        in_specs=[HBM] * 6,
        out_specs=[HBM] * 16,
        scratch_shapes=[vmem(*whole) for _ in range(4)]
        + [vmem(*total.shape), vmem(C_TILES, D, LANES)]
        + [vmem(*dims) for dims in small]
        + [
            pltpu.SemaphoreType.DMA((8,)),
            pltpu.SemaphoreType.DMA((2,)),
            pltpu.SemaphoreType.DMA,
        ],
        compiler_params=pltpu.CompilerParams(vmem_limit_bytes=ROOM),
    )(part_nodes, mean, logstd, noise, total, columns)


def shards(
    nodes,
    edges,
    latent_mean,
    latent_logstd,
    latent_noise,
    kl_weight,
    band_counts,
    neighbors,
    edge_mask,
    w_edge_in,
    b_edge_in,
    w_edge_out,
    b_edge_out,
    edge_gain,
    edge_shift,
    w_node_in,
    b_node_in,
    w_node_out,
    b_node_out,
    node_gain,
    node_shift,
    cotangent,
):
    n_blk = lax.axis_size("blk")
    n_lon = lax.axis_size("lon")
    vectors = (
        b_edge_in,
        b_edge_out,
        edge_gain,
        edge_shift,
        b_node_in,
        b_node_out,
        node_gain,
        node_shift,
    )
    weights = (w_edge_in, w_edge_out, w_node_in, w_node_out)
    weights += tuple(vector.reshape(1, D) for vector in vectors)
    state, cols, projected, receiver, sides, codes, valid, pack, columns = start_call(
        n_blk,
        n_lon,
        band_counts,
        kl_weight,
        nodes,
        latent_mean,
        latent_logstd,
        latent_noise,
        neighbors,
        edge_mask,
        weights,
    )
    new_states, grad_edges, part, recv, own, cells, acc = layer_call(
        edges, cotangent, projected, receiver, sides, codes, valid, pack, columns, state
    )
    part, total = sum_call(n_blk, n_lon, acc, own, cells, recv, part, state, cols, pack)
    grad_nodes, grad_mean, grad_logstd, kl_value, g_w_ei, g_w_eo, g_w_ni, g_w_no, *g_vec = (
        final_call(
            part,
            latent_mean,
            latent_logstd,
            latent_noise,
            total,
            columns,
        )
    )
    g_vec = [vector.reshape(D) for vector in g_vec]
    return (
        new_states,
        kl_value.reshape(1),
        grad_nodes,
        grad_edges,
        grad_mean,
        grad_logstd,
        g_w_ei,
        g_vec[0],
        g_w_eo,
        g_vec[1],
        g_vec[2],
        g_vec[3],
        g_w_ni,
        g_vec[4],
        g_w_no,
        g_vec[5],
        g_vec[6],
        g_vec[7],
    )


def solution(mesh):
    node = P(None, "blk", "lon")
    slot = P(None, None, "blk", "lon")
    return jax.shard_map(
        shards,
        mesh=mesh,
        in_specs=(
            (node, slot, node, node, node, P(), P(), node, node) + (P(),) * 12 + (node,)
        ),
        out_specs=(node, P(), node, slot, node, node) + (P(),) * 12,
        check_vma=False,
    )
```

```python
import functools

import jax
import jax.numpy as jnp
from jax import lax
from jax.experimental import pallas as pl
from jax.experimental.pallas import tpu as pltpu
from jax.sharding import PartitionSpec as P

F32 = jnp.float32
BF16 = jnp.bfloat16
MESH = pl.DeviceIdType.MESH
D = 64
LANES = 128
NBR = 6
EPS = 1e-05
HBM = pl.BlockSpec(memory_space=pltpu.HBM)
VMEM = pl.BlockSpec(memory_space=pltpu.VMEM)
ROOM = 62 * 2**20
SMEM = pl.BlockSpec(memory_space=pltpu.SMEM)

WINDOWS = ((-1, -1), (-1, 0), (-1, 1), (0, -1), (0, 1), (1, -1), (1, 0), (1, 1))


def halves(value):
    high = value.astype(BF16)
    return high, (value - high.astype(F32)).astype(BF16)


def weight_pack(weight, *biases):
    high, low = halves(weight)
    if not biases:
        return jnp.concatenate([high, high, low], axis=1)
    place = lax.broadcasted_iota(jnp.int32, (weight.shape[0], 16), 1)
    wide = jnp.zeros((weight.shape[0], 16), F32)
    for i, bias in enumerate(biases):
        for j, part in enumerate(halves(bias)):
            wide = jnp.where(place == 2 * i + j, part.astype(F32), wide)
    return jnp.concatenate([high, high, wide.astype(BF16), low], axis=1)


def mxu(left, right):
    return jnp.dot(left, right, preferred_element_type=F32)


def outer(left, right):
    return lax.dot_general(
        left, right, (((1,), (1,)), ((), ())), preferred_element_type=F32
    )


def exact(left, right, dims):
    return lax.dot_general(
        left,
        right,
        (dims, ((), ())),
        precision=lax.Precision.HIGHEST,
        preferred_element_type=F32,
    )


def eye():
    return lax.broadcasted_iota(jnp.int32, (D, D), 0) == lax.broadcasted_iota(
        jnp.int32, (D, D), 1
    )


def to_column(row):
    return jnp.sum(jnp.where(eye(), row, 0.0), axis=1, keepdims=True)


def to_row(column):
    return jnp.sum(jnp.where(eye(), column, 0.0), axis=0, keepdims=True)


def waits(ref, sem):
    pltpu.make_async_copy(ref, ref, sem).wait()


def in_turn(*routines):
    waiting = list(routines)
    while waiting:
        for routine in list(waiting):
            if next(routine, routine) is routine:
                waiting.remove(routine)


def lane_ids(rows=D):
    return lax.broadcasted_iota(jnp.int32, (rows, LANES), 1)


P_HIDDEN, P_EDGE, P_EDGE_T, P_NODE_OUT = (0, 128), (128, 192), (192, 256), (256, 320)
P_NODE_OUT_T, P_NODE_IN_T, P_SEND_T, P_RECV_T = (320, 384), (384, 576), (576, 640), (640, 704)
P_NODE_IN, P_NODE_IN_END = (704, 768), (768, 832)
P_ROWS, P_LANES = 832, 256
C_GAIN_N, C_SHIFT_N, C_VALID, C_DIVERGED, C_COUNT, C_WEIGHT_N, C_ROWS = range(7)
C_TILES = 7


def packed_rows(ref, rows, lanes=3 * D):
    return ref[rows[0] : rows[1], :lanes]


def row_of(ref, row, step, count=D):
    flat = ref.reshape(count * step, LANES)
    return flat, pl.ds(row, count, stride=step)


def read_row(ref, row, step=8):
    flat, place = row_of(ref, row, step)
    return flat[place, :]


def write_row(ref, row, value, step=8):
    flat, place = row_of(ref, row, step)
    flat[place, :] = value


def pack_column(tile):
    return jnp.where(lane_ids(D // 2) < D, tile[: D // 2], pltpu.roll(tile[D // 2 :], D, 1))


def unpack_column(tile):
    return jnp.concatenate([tile, pltpu.roll(tile, D, 1)], axis=0)


def corner_rows(columns):
    rows = [to_row(column) for column in columns]
    wide = jnp.concatenate(rows + [jnp.zeros((4, D), F32)], axis=0)
    return jnp.concatenate([wide, jnp.zeros((8, D), F32)], axis=1)


def corner_at(ref, row, lane):
    return jnp.where(lane_ids() == lane, to_column(ref[row : row + 1, :D]), 0.0)


def rim_copies(around, rows, columns, corners, rows_in, columns_in, corners_in, send, recv):
    pairs = [(rows.at[0], rows_in.at[0]), (rows.at[1], rows_in.at[1])]
    pairs += [(columns.at[0], columns_in.at[0]), (columns.at[1], columns_in.at[1])]
    pairs += [(corners, corners_in.at[i]) for i in range(4)]
    return [
        pltpu.make_async_remote_copy(
            src_ref=source,
            dst_ref=target,
            send_sem=send.at[slot],
            recv_sem=recv.at[slot],
            device_id=place,
            device_id_type=MESH,
        )
        for slot, (place, (source, target)) in enumerate(zip(around, pairs))
    ]


def neighbours(n_blk, n_lon):
    blk = lax.axis_index("blk")
    lon = lax.axis_index("lon")
    up = lax.rem(blk + n_blk - 1, n_blk)
    down = lax.rem(blk + 1, n_blk)
    west = lax.rem(lon + n_lon - 1, n_lon)
    east = lax.rem(lon + 1, n_lon)
    around = (
        (up, lon),
        (down, lon),
        (blk, west),
        (blk, east),
        (up, west),
        (up, east),
        (down, west),
        (down, east),
    )
    return blk, lon, around


def start_kernel(
    n_blk,
    n_lon,
    counts,
    kl_weight,
    nodes,
    mean,
    logstd,
    noise,
    neighbors,
    edge_mask,
    w_ei,
    w_eo,
    w_ni,
    w_no,
    *rest,
):
    vectors = rest[:8]
    (
        state_out,
        cols_out,
        project_out,
        receive_out,
        sides_out,
        codes_out,
        valid_out,
        pack_out,
        columns_out,
        buf,
        state,
        projected,
        receiver,
        sides,
        nb,
        mk,
        codes,
        valid,
        v_ei,
        v_eo,
        v_ni,
        v_no,
        v_vec,
        pack,
        columns,
        cols,
        edge_rows,
        edge_cols,
        edge_corners,
        rows_in,
        cols_in,
        corners_in,
        in_sem,
        slot_sem,
        weight_sem,
        send_sem,
        recv_sem,
        out_sem,
    ) = rest[8:]
    rows = nodes.shape[1]
    blk, lon, around = neighbours(n_blk, n_lon)
    barrier = pltpu.get_barrier_semaphore()
    for place in around:
        pl.semaphore_signal(barrier, inc=1, device_id=place, device_id_type=MESH)

    n_groups = in_sem.shape[0]
    group = rows // n_groups
    for g in range(n_groups):
        for which, source in enumerate((nodes, mean, logstd, noise)):
            pltpu.make_async_copy(
                source.at[:, pl.ds(g * group, group), :], buf.at[g, which], in_sem.at[g]
            ).start()
    weights = [(w_ei, v_ei), (w_eo, v_eo), (w_ni, v_ni), (w_no, v_no)]
    weights += [(vectors[i], v_vec.at[i]) for i in range(8)]
    lane = lane_ids()
    count = counts[blk]
    inside = lane < count

    def state_row(g, j, carry):
        total, west_tile, east_tile = carry
        r = g * group + j
        node_r, mean_r, logstd_r, noise_r = [
            read_row(buf.at[g, which], j, group) for which in range(4)
        ]
        spread = jnp.exp(logstd_r)
        value = node_r + mean_r + spread * noise_r
        state[r + 1] = value
        total += jnp.where(inside, mean_r * mean_r + spread * spread - 2.0 * logstd_r, 0.0)
        moved = pltpu.roll(value, r + 1, 1)
        west_tile = jnp.where(lane == r + 1, moved, west_tile)
        east_tile = jnp.where(lane == r, moved, east_tile)
        return total, west_tile, east_tile

    carry = (jnp.zeros((D, LANES), F32),) * 3
    for source, target in weights:
        pltpu.make_async_copy(source, target, weight_sem).start()

    def state_group(g, carry):
        waits(buf.at[g], in_sem.at[g])
        for j in range(0, group, 2):
            carry = state_row(g, j + 1, state_row(g, j, carry))
        return carry

    carry = lax.fori_loop(0, n_groups, state_group, carry)
    total, west_tile, east_tile = carry
    edge_rows[0] = state[1]
    edge_rows[1] = state[rows]
    edge_cols[0] = pack_column(west_tile)
    edge_cols[1] = pack_column(east_tile)
    edge_corners[...] = corner_rows(
        [
            state[row][:, lane0 : lane0 + 1]
            for row in (1, rows)
            for lane0 in (0, LANES - 1)
        ]
    )

    pl.semaphore_wait(barrier, 8)
    copies = rim_copies(
        around,
        edge_rows,
        edge_cols,
        edge_corners,
        rows_in,
        cols_in,
        corners_in,
        send_sem,
        recv_sem,
    )
    for copy in copies:
        copy.start()
    pltpu.make_async_copy(neighbors, nb, slot_sem).start()
    pltpu.make_async_copy(edge_mask, mk, slot_sem).start()
    inner = pl.ds(1, rows)
    pltpu.make_async_copy(state.at[inner], state_out.at[inner], out_sem).start()

    for _, target in weights:
        waits(target, weight_sem)
    b_ei, b_eo, gain_e, shift_e, b_ni, b_no, gain_n, shift_n = [
        to_column(v_vec[i]) for i in range(8)
    ]
    n_valid = counts[0]
    for i in range(1, counts.shape[0]):
        n_valid += counts[i]
    for i, column in (
        (C_GAIN_N, gain_n),
        (C_SHIFT_N, shift_n),
        (C_VALID, jnp.where(inside, kl_weight[0], 0.0)),
        (C_COUNT, jnp.full((D, LANES), (D * rows * n_lon * n_valid).astype(F32))),
        (
            C_DIVERGED,
            0.5 * jnp.sum(total - rows * jnp.where(inside, 1.0, 0.0), axis=1, keepdims=True),
        ),
    ):
        columns[i] = jnp.broadcast_to(column, (D, LANES))
    w_in = v_ei[...]
    w_e, w_s, w_r = w_in[:, :D], w_in[:, D : 2 * D], w_in[:, 2 * D :]
    a_state = jnp.concatenate([weight_pack(0.5 * w_s), weight_pack(0.5 * w_r)], axis=0)
    w_o = v_eo[...]
    w_oc = w_o - jnp.mean(w_o, axis=0, keepdims=True)
    b_oc = b_eo - jnp.mean(b_eo, axis=0, keepdims=True)
    back = 0.5 * exact(w_o, w_oc, ((0,), (0,)))
    b_back = 0.5 * exact(w_o, b_oc, ((0,), (0,)))
    w_n = v_ni[...]
    w_nt = w_n.T
    gain_row, shift_row = v_vec[2], v_vec[3]
    one_row = jnp.ones_like(gain_row)
    scale_row = jnp.concatenate([one_row, gain_row], axis=1)
    add_row = jnp.concatenate([0.0 * one_row, shift_row], axis=1)
    columns[C_WEIGHT_N] = w_n
    row_id = lax.broadcasted_iota(jnp.int32, (D, LANES), 0)
    columns[C_ROWS] = jnp.where(row_id == 0, scale_row, jnp.where(row_id == 1, add_row, 0.0))
    w_shift = jnp.sum(w_n * add_row, axis=1, keepdims=True)
    w_out = v_no[...]
    scaled = gain_e * w_nt[D:]
    scaled = scaled - jnp.mean(scaled, axis=0, keepdims=True)

    def put(place, *parts):
        value = jnp.concatenate(parts, axis=0) if len(parts) > 1 else parts[0]
        pack[place[0] : place[1], : value.shape[1]] = value

    put(P_EDGE, weight_pack(0.5 * w_e))
    put(P_HIDDEN, weight_pack(w_oc, b_oc), weight_pack(back, b_back))
    put(P_EDGE_T, weight_pack(w_e.T))
    put(P_SEND_T, weight_pack(w_s.T))
    put(P_RECV_T, weight_pack(w_r.T))
    node_in = weight_pack(0.5 * w_n * scale_row, 0.5 * b_ni, 0.5 * w_shift)
    put(P_NODE_IN, node_in[:, :P_LANES])
    put(P_NODE_IN_END, node_in[:, P_LANES:])
    put(
        P_NODE_OUT,
        weight_pack(
            w_out - jnp.mean(w_out, axis=0, keepdims=True),
            b_no - jnp.mean(b_no, axis=0, keepdims=True),
        ),
    )
    put(P_NODE_OUT_T, weight_pack(0.5 * w_out.T))
    put(
        P_NODE_IN_T,
        weight_pack(w_nt[:D]),
        weight_pack(scaled),
        weight_pack(0.5 * exact(w_o, scaled, ((0,), (0,)))),
    )
    pltpu.make_async_copy(pack, pack_out, out_sem).start()
    pltpu.make_async_copy(columns, columns_out, out_sem).start()

    waits(nb, slot_sem)
    waits(mk, slot_sem)
    before = counts[lax.rem(blk + n_blk - 1, n_blk)]
    after = counts[lax.rem(blk + 1, n_blk)]
    row_id = lax.broadcasted_iota(jnp.int32, (rows, LANES), 0)
    col_id = lax.broadcasted_iota(jnp.int32, (rows, LANES), 1)
    above = jnp.where(row_id == 0, before, count)
    below = jnp.where(row_id == rows - 1, after, count)
    for k in range(NBR):
        delta = nb[k] - (row_id * (LANES + 2) + col_id)
        first = delta < LANES + 2
        middle = delta < 2 * (LANES + 2)
        step = jnp.where(
            first, delta, jnp.where(middle, delta - (LANES + 2), delta - 2 * (LANES + 2))
        )
        codes[k] = jnp.where(first, step, jnp.where(middle, 3 + (step >> 1), 5 + step))
        owner = col_id + step - 1
        owner = jnp.where(owner < 0, LANES - 1, jnp.where(owner >= LANES, 0, owner))
        limit = jnp.where(first, above, jnp.where(middle, count, below))
        valid[k] = jnp.where((col_id < count) & (owner < limit), mk[k].astype(F32), 0.0)
    for k in range(NBR, 8):
        codes[k] = jnp.zeros((rows, LANES), jnp.int32)
        valid[k] = jnp.zeros((rows, LANES), F32)
    for k in range(8):
        pltpu.make_async_copy(codes.at[k], codes_out.at[:, k, :], out_sem).start()
        pltpu.make_async_copy(valid.at[k], valid_out.at[:, k, :], out_sem).start()

    half_bias = 0.5 * b_ei

    def project(i, _):
        high, low = halves(
            jnp.concatenate([state[1 + 4 * i + u] for u in range(4)], axis=1)
        )
        both = mxu(a_state, jnp.concatenate([high, low, high], axis=0))
        for u in range(4):
            s = slice(u * LANES, (u + 1) * LANES)
            projected[1 + 4 * i + u] = both[:D, s]
            receiver[4 * i + u] = both[D:, s] + half_bias

    lax.fori_loop(0, rows // 4, project, None)
    pltpu.make_async_copy(projected.at[inner], project_out.at[inner], out_sem).start()
    pltpu.make_async_copy(receiver, receive_out, out_sem).start()

    for copy in copies:
        copy.wait()
    state[rows + 1] = rows_in[0]
    state[0] = rows_in[1]
    from_east = unpack_column(cols_in[0])
    from_west = unpack_column(cols_in[1])
    cols[1] = (
        pltpu.roll(jnp.where((lane >= 1) & (lane <= rows), from_east, 0.0), LANES - 1, 1)
        + corner_at(corners_in.at[0], 0, rows)
        + corner_at(corners_in.at[2], 2, LANES - 1)
    )
    cols[0] = (
        pltpu.roll(jnp.where(lane < rows, from_west, 0.0), 1, 1)
        + corner_at(corners_in.at[1], 1, rows + 1)
        + corner_at(corners_in.at[3], 3, 0)
    )
    high, low = halves(
        jnp.concatenate([rows_in[1], rows_in[0], cols[0], cols[1]], axis=1)
    )
    rim = mxu(a_state[:D], jnp.concatenate([high, low, high], axis=0))
    projected[0] = rim[:, :LANES]
    projected[rows + 1] = rim[:, LANES : 2 * LANES]
    sides[0] = rim[:, 2 * LANES : 3 * LANES]
    sides[1] = rim[:, 3 * LANES :]
    for t in (0, rows + 1):
        pltpu.make_async_copy(projected.at[t], project_out.at[t], out_sem).start()
        pltpu.make_async_copy(state.at[t], state_out.at[t], out_sem).start()
    pltpu.make_async_copy(sides, sides_out, out_sem).start()
    pltpu.make_async_copy(cols, cols_out, out_sem).start()
    for ref in (pack, columns, codes, valid, receiver, state, projected, cols, sides):
        waits(ref, out_sem)


def start_call(n_blk, n_lon, counts, kl_weight, nodes, mean, logstd, noise, neighbors, mask, weights):
    rows = nodes.shape[1]
    tile = (D, LANES)
    shapes = (
        ((rows + 2, *tile), F32),
        ((2, *tile), F32),
        ((rows + 2, *tile), F32),
        ((rows, *tile), F32),
        ((2, *tile), F32),
        ((rows, 8, LANES), jnp.int32),
        ((rows, 8, LANES), F32),
        ((P_ROWS, P_LANES), BF16),
        ((C_TILES, *tile), F32),
    )
    vmem = lambda *dims: pltpu.VMEM(dims, F32)
    ints = lambda *dims: pltpu.VMEM(dims, jnp.int32)
    dma = pltpu.SemaphoreType.DMA
    return pl.pallas_call(
        functools.partial(start_kernel, n_blk, n_lon),
        name="start",
        out_shape=[jax.ShapeDtypeStruct(*shape) for shape in shapes],
        in_specs=[SMEM, SMEM] + [HBM] * (6 + len(weights)),
        out_specs=[HBM] * len(shapes),
        scratch_shapes=[
            vmem(rows // 8, 4, D, 8, LANES),
            vmem(rows + 2, *tile),
            vmem(rows + 2, *tile),
            vmem(rows, *tile),
            vmem(2, *tile),
            ints(NBR, rows, LANES),
            ints(NBR, rows, LANES),
            ints(8, rows, LANES),
            vmem(8, rows, LANES),
            vmem(D, 3 * D),
            vmem(D, D),
            vmem(D, 2 * D),
            vmem(D, D),
            vmem(8, 1, D),
            pltpu.VMEM((P_ROWS, P_LANES), BF16),
            vmem(C_TILES, *tile),
            vmem(2, *tile),
            vmem(2, *tile),
            vmem(2, D // 2, LANES),
            vmem(8, LANES),
            vmem(2, *tile),
            vmem(2, D // 2, LANES),
            vmem(4, 8, LANES),
            dma((rows // 8,)),
            dma,
            dma,
            dma((8,)),
            dma((8,)),
            dma,
        ],
        compiler_params=pltpu.CompilerParams(
            collective_id=0, has_side_effects=True, vmem_limit_bytes=ROOM
        ),
    )(counts, kl_weight, nodes, mean, logstd, noise, neighbors, mask, *weights)


def layer_kernel(
    edges,
    cotangent,
    project_in,
    receive_in,
    sides_in,
    codes_in,
    valid_in,
    pack_in,
    columns_in,
    state_in,
    new_states,
    grad_edges,
    part_out,
    recv_out,
    own_out,
    cells_out,
    acc_out,
    slope,
    xs,
    hs,
    cb,
    db,
    staged,
    windows,
    projected,
    receiver,
    sides,
    codes,
    valid,
    pack,
    columns,
    state,
    inverse,
    summed,
    qc_ref,
    qo_ref,
    cot,
    fresh,
    placed,
    cells,
    gather_grads,
    acc_edge,
    acc_hidden,
    acc_nin,
    acc_nout,
    acc_vec,
    acc,
    row_sem,
    edge_sem,
    in_sem,
    out_sem,
):
    rows = cotangent.shape[1]
    wide = NBR * LANES
    two = 2 * LANES
    part, grad_recv, own = receiver, summed, projected
    lane = lane_ids()

    halfway = 10

    def load_edges(r):
        for k in range(NBR):
            pltpu.make_async_copy(
                edges.at[:, k, r, :],
                staged.at[r, :, pl.ds(k * LANES, LANES)],
                edge_sem.at[r],
            ).start()

    first_weights = pl.ds(P_HIDDEN[0], P_EDGE[1])
    first_small = (
        (sides_in, sides),
        (pack_in.at[first_weights], pack.at[first_weights]),
        (codes_in, codes),
        (valid_in, valid),
    )
    parts = []
    for g, (first, last) in enumerate(((0, halfway), (halfway, rows + 2))):
        send, receive = pl.ds(first, last - first), pl.ds(first, min(last, rows) - first)
        part_g = ((project_in, projected, send), (receive_in, receiver, receive))
        for source, target, span in part_g:
            pltpu.make_async_copy(source.at[span], target.at[span], row_sem.at[g]).start()
        parts.append([target.at[span] for _, target, span in part_g])
        if g == 0:
            for source, target in first_small[:2]:
                pltpu.make_async_copy(source, target, in_sem.at[0]).start()
            for r in range(4):
                load_edges(r)
            for source, target in first_small[2:]:
                pltpu.make_async_copy(source, target, in_sem.at[0]).start()
    lax.fori_loop(4, 12, lambda r, _: load_edges(r), None)

    def load_rest():
        rest = pl.ds(P_EDGE[1], P_ROWS - P_EDGE[1])
        pltpu.make_async_copy(pack_in.at[rest], pack.at[rest], in_sem.at[1]).start()
        pltpu.make_async_copy(columns_in, columns, in_sem.at[1]).start()
        pltpu.make_async_copy(state_in, state, in_sem.at[1]).start()

        for g in range(rows // 8):
            pltpu.make_async_copy(
                cotangent.at[:, pl.ds(8 * g, 8), :], cot.at[g], in_sem.at[1]
            ).start()
        lax.fori_loop(12, rows, lambda r, _: load_edges(r), None)
        return (cot, state, columns, pack.at[rest])

    ones16 = jnp.where(
        lax.broadcasted_iota(jnp.int32, (16, wide), 0) < 2, 1.0, 0.0
    ).astype(BF16)
    ones_two = ones16[:, :two]
    for _, target in first_small:
        waits(target, in_sem.at[0])

    def shift(t):
        centre = projected[t]
        mix = pltpu.roll(
            jnp.where(lane == t, sides[0], sides[1]), lax.rem(LANES - t, LANES), 1
        )
        windows[t, 1] = centre
        windows[t, 0] = jnp.where(lane == 0, mix, pltpu.roll(centre, 1, 1))
        windows[t, 2] = jnp.where(lane == LANES - 1, mix, pltpu.roll(centre, LANES - 1, 1))

    def edge_product(r, pair):
        own = receiver[r]
        s = pl.ds(pair * two, two)
        high, low = halves(staged[r, :, s])
        xs[r, :D, s] = high
        xs[r, D:, s] = low
        out = mxu(packed_rows(pack, P_EDGE), jnp.concatenate([high, low, high], axis=0))
        slope[r, :, s] = out + jnp.concatenate([own, own], axis=1)

    def hidden_values(r, pair):
        slots = (2 * pair, 2 * pair + 1)
        hidden = {k: [None] * 8 for k in slots}
        masks = {}
        for k in slots:
            code = jnp.broadcast_to(codes[r, pl.ds(k, 1), :], (8, LANES))
            masks[k] = ((code & 1) != 0, (code & 2) != 0, (code & 4) != 0)
        for f in range(8):
            rows_f = pl.ds(8 * f, 8)
            w = [windows[r + 1 + dr, 1 + dc, rows_f, :] for dr, dc in WINDOWS]
            for k in slots:
                s = pl.ds(k * LANES, LANES)
                b0, b1, b2 = masks[k]
                low = jnp.where(b1, jnp.where(b0, w[3], w[2]), jnp.where(b0, w[1], w[0]))
                top = jnp.where(b1, jnp.where(b0, w[7], w[6]), jnp.where(b0, w[5], w[4]))
                pre = slope[r, rows_f, s] + jnp.where(b2, top, low)
                t = jnp.tanh(pre)
                u = 1.0 + t
                h = pre * u
                slope[r, rows_f, s] = u + h * (1.0 - t)
                hidden[k][f] = h
        s = pl.ds(pair * two, two)
        high, low = halves(
            jnp.concatenate([jnp.concatenate(hidden[k], axis=0) for k in slots], axis=1)
        )
        hs[r, :D, s] = high
        hs[r, D : 2 * D, s] = low
        hs[r, 2 * D :, s] = ones_two

    def hidden_product(r, pair):
        s = pl.ds(pair * two, two)
        both = mxu(
            packed_rows(pack, P_HIDDEN, 3 * D + 16),
            jnp.concatenate([hs[r, :, s], hs[r, :D, s]], axis=0),
        )
        cb[r, :, s] = both[:D]
        db[r, :, s] = both[D:]
        return r, pair, both[:D]

    def norm(r, pair, pair_c, total):
        for j in range(2):
            k = 2 * pair + j
            c = pair_c[:, j * LANES : (j + 1) * LANES]
            variance = jnp.sum(c * c, axis=0, keepdims=True) * (1.0 / D)
            inv = lax.rsqrt(variance + EPS)
            inverse[r, pl.ds(k, 1), :] = inv
            term = (inv * valid[r, pl.ds(k, 1), :]) * c
            total = term if total is None else total + term
        if pair == NBR // 2 - 1:
            summed[r] = total
            total = None
        return total

    def forward(i, _, first=0, last=2):
        turn = [4 * i + u for u in range(4)]
        if first == 0:
            for r in turn:
                waits(staged.at[r + 4], edge_sem.at[r + 4])
            for r in turn:
                shift(r + 6)
        units = [(r, pair) for r in turn for pair in range(NBR // 2)]
        products = []
        total = None
        if last >= 2:
            products.append(hidden_product(units[0][0] - 4, units[0][1]))
        for i_unit, (r, pair) in enumerate(units):
            if last >= 2 and i_unit + 1 < len(units):
                ahead_r, ahead_pair = units[i_unit + 1]
                products.append(hidden_product(ahead_r - 4, ahead_pair))
            if first <= 1 <= last:
                if pair == 0:
                    placed[r + 2] = jnp.zeros((3, D, LANES), F32)
                hidden_values(r, pair)
            if last >= 2:
                total = norm(*products[i_unit], total)
            if first == 0:
                edge_product(r + 4, pair)

    for ref in parts[0]:
        waits(ref, row_sem.at[0])
    for t in range(6):
        shift(t)
    for r in range(2):
        placed[r] = jnp.zeros((3, D, LANES), F32)
    for r in range(4):
        waits(staged.at[r], edge_sem.at[r])
        for pair in range(NBR // 2):
            edge_product(r, pair)
    node_inputs = load_rest()
    forward(0, None, last=1)
    for ref in parts[1]:
        waits(ref, row_sem.at[1])
    turns = rows // 4
    lax.fori_loop(1, turns - 1, forward, None)
    forward(turns - 1, None, first=1)
    forward(turns, None, first=2)

    for ref in (acc_edge, acc_hidden, acc_nin, acc_nout, acc_vec):
        ref[...] = jnp.zeros_like(ref)
    for ref in node_inputs:
        waits(ref, in_sem.at[1])
    chunk = 4
    span = chunk * LANES

    def node_chunk(first):
        tile_cols = lambda i: jnp.concatenate([columns[i]] * chunk, axis=1)
        spread = lambda ref, offset: jnp.concatenate(
            [ref[first + offset + j] for j in range(chunk)], axis=1
        )
        degree = jnp.concatenate(
            [jnp.sum(valid[first + j], axis=0, keepdims=True) for j in range(chunk)], axis=1
        )
        st_high, st_low = halves(spread(state, 1))
        sum_high, sum_low = halves(spread(summed, 0))
        place = lax.broadcasted_iota(jnp.int32, (16, span), 0)
        extra = jnp.where(place < 2, 1.0, jnp.where(place < 4, degree, 0.0)).astype(BF16)
        tops = jnp.concatenate([st_high, sum_high], axis=0)
        ends = jnp.concatenate([st_low, sum_low], axis=0)
        pre = mxu(
            jnp.concatenate(
                [
                    packed_rows(pack, P_NODE_IN, P_LANES),
                    packed_rows(pack, P_NODE_IN_END, 6 * D + 16 - P_LANES),
                ],
                axis=1,
            ),
            jnp.concatenate([tops, ends, extra, tops], axis=0),
        )
        yield
        t = jnp.tanh(pre)
        u = 1.0 + t
        h = pre * u
        slope_n = u + h * (1.0 - t)
        h_high, h_low = halves(h)
        h_all = jnp.concatenate([h_high, h_low, ones16[:, :span]], axis=0)
        c = mxu(
            packed_rows(pack, P_NODE_OUT, 3 * D + 16),
            jnp.concatenate([h_all, h_high], axis=0),
        )
        yield
        cot_c = jnp.concatenate(
            [read_row(cot.at[(first + j) // 8], (first + j) % 8) for j in range(chunk)], axis=1
        )
        inv = lax.rsqrt(jnp.sum(c * c, axis=0, keepdims=True) * (1.0 / D) + EPS)
        n = c * inv
        new = spread(state, 1) + (tile_cols(C_GAIN_N) * n + tile_cols(C_SHIFT_N))
        q = cot_c * tile_cols(C_GAIN_N)
        q = q - jnp.sum(q, axis=0, keepdims=True) * (1.0 / D)
        grad = inv * (q - n * (jnp.sum(q * n, axis=0, keepdims=True) * (1.0 / D)))
        g_high, g_low = halves(grad)
        pre_grad = mxu(
            packed_rows(pack, P_NODE_OUT_T), jnp.concatenate([g_high, g_low, g_high], axis=0)
        )
        for j in range(chunk):
            s = slice(j * LANES, (j + 1) * LANES)
            write_row(fresh.at[(first + j) // 8], (first + j) % 8, new[:, s])
            acc_vec[0] += cot_c[:, s] * n[:, s]
            acc_vec[1] += cot_c[:, s]
        yield
        acc_nout[...] += outer(jnp.concatenate([g_high, g_low], axis=0), h_all)
        pre_grad = pre_grad * slope_n
        p_high, p_low = halves(pre_grad)
        back = mxu(
            packed_rows(pack, P_NODE_IN_T), jnp.concatenate([p_high, p_low, p_high], axis=0)
        )
        for j in range(chunk):
            s = slice(j * LANES, (j + 1) * LANES)
            acc_vec[2] += pre_grad[:, s]
            acc_vec[3] += pre_grad[:, s] * degree[:, s]
        yield
        acc_nin[...] += outer(
            jnp.concatenate([p_high, p_low], axis=0), jnp.concatenate([tops, ends], axis=0)
        )
        for j in range(chunk):
            s = slice(j * LANES, (j + 1) * LANES)
            part[first + j] = cot_c[:, s] + back[:D, s]
            qc_ref[first + j] = back[D : 2 * D, s]
            qo_ref[first + j] = back[2 * D :, s]

    in_flight = []
    for first in range(0, rows + 4 * chunk, chunk):
        if first < rows:
            in_flight.append(node_chunk(first))
        for routine in list(in_flight):
            if next(routine, routine) is routine:
                in_flight.remove(routine)

    for g in range(rows // 8):
        pltpu.make_async_copy(
            fresh.at[g], new_states.at[:, pl.ds(8 * g, 8), :], out_sem
        ).start()
    pltpu.make_async_copy(part, part_out, out_sem).start()

    def grad_unit(r, pair, u, received):
        qc = qc_ref[r]
        qo = qo_ref[r]
        hidden_grads, grads = [], []
        for k in (2 * pair, 2 * pair + 1):
            s = pl.ds(k * LANES, LANES)
            c = cb[r, :, s]
            inv = inverse[r, pl.ds(k, 1), :]
            alpha = inv * valid[r, pl.ds(k, 1), :]
            moment = jnp.sum(qc * c, axis=0, keepdims=True) * (1.0 / D)
            beta = alpha * inv * inv * moment
            hidden_grads.append(alpha * qc - beta * c)
            grad = (alpha * qo - beta * db[r, :, s]) * slope[r, :, s]
            grads.append(grad)
            received = grad if received is None else received + grad
        high, low = halves(jnp.concatenate(hidden_grads, axis=1))
        s = pl.ds(pair * two, two)
        gather_grads[u, :D, s] = high
        gather_grads[u, D : 2 * D, s] = low
        high, low = halves(jnp.concatenate(grads, axis=1))
        gather_grads[u, 2 * D : 3 * D, s] = high
        gather_grads[u, 3 * D :, s] = low
        ge = mxu(
            packed_rows(pack, P_EDGE_T), jnp.concatenate([high, low, high], axis=0)
        )
        return grads, received, ge

    def place_unit(r, pair, grads):
        code = [
            jnp.broadcast_to(codes[r, pl.ds(k, 1), :], (8, LANES))
            for k in (2 * pair, 2 * pair + 1)
        ]
        for which, (dr, dc) in enumerate(WINDOWS):
            masks = [c == which for c in code]
            for f in range(8):
                rows_f = pl.ds(8 * f, 8)
                value = placed[r + 1 + dr, 1 + dc, rows_f, :]
                for j in range(2):
                    value += jnp.where(masks[j], grads[j][8 * f : 8 * f + 8], 0.0)
                placed[r + 1 + dr, 1 + dc, rows_f, :] = value

    def store_unit(r, pair, ge):
        staged[r, :, pl.ds(pair * two, two)] = ge

    def products(r, u):
        r = jnp.maximum(r, 0)
        acc_hidden[...] += outer(gather_grads[u, : 2 * D], hs[r])
        acc_edge[...] += outer(gather_grads[u, 2 * D :], xs[r])

    def settle(t):
        to_west = placed[t, 0]
        to_east = placed[t, 2]
        own[t] = (
            placed[t, 1]
            + jnp.where(lane == 0, 0.0, pltpu.roll(to_east, 1, 1))
            + jnp.where(lane == LANES - 1, 0.0, pltpu.roll(to_west, LANES - 1, 1))
        )
        mix = pltpu.roll(jnp.where(lane == 0, to_west, to_east), t, 1)
        cells[0] = jnp.where(lane == t, mix, cells[0])
        cells[1] = jnp.where(lane == lax.rem(t + LANES - 1, LANES), mix, cells[1])

    def send_rows(i, unroll=4):
        span = pl.ds(unroll * i, unroll)
        pltpu.make_async_copy(grad_recv.at[span], recv_out.at[span], out_sem).start()
        for u in range(unroll):
            r = unroll * i + u
            for k in range(NBR):
                pltpu.make_async_copy(
                    staged.at[r, :, pl.ds(k * LANES, LANES)],
                    grad_edges.at[:, k, r, :],
                    out_sem,
                ).start()

    def backward(i, _, unroll=4):
        if not isinstance(i, int):
            send_rows(i - 1)
            for u in range(unroll):
                settle(unroll * (i - 1) + u)
        pending = None
        for u in range(unroll):
            r = unroll * i + u
            products(r - unroll, u)
            received = None
            for pair in range(NBR // 2):
                grads, received, ge = grad_unit(r, pair, u, received)
                place_unit(r, pair, grads)
                if pending is not None:
                    store_unit(*pending)
                pending = (r, pair, ge)
            grad_recv[r] = received
        store_unit(*pending)
        if not isinstance(i, int):
            span = pl.ds(unroll * (i - 1), unroll)
            pltpu.make_async_copy(own.at[span], own_out.at[span], out_sem).start()

    cells[...] = jnp.zeros_like(cells)
    gather_grads[...] = jnp.zeros_like(gather_grads)
    backward(0, None)
    lax.fori_loop(1, rows // 4, backward, None)
    send_rows(rows // 4 - 1)
    for t in range(rows - 4, rows + 2):
        settle(t)
    tail = pl.ds(rows - 4, 6)
    pltpu.make_async_copy(own.at[tail], own_out.at[tail], out_sem).start()
    pltpu.make_async_copy(cells, cells_out, out_sem).start()
    for u in range(4):
        products(rows - 4 + u, u)

    def folded(ref):
        half = ref[:D, : 2 * D] + ref[D:, : 2 * D]
        return half + pltpu.roll(half, D, 1)

    left = lane < D
    acc[0] = folded(acc_edge)
    plain = (
        acc_nin[:D, : 2 * D]
        + acc_nin[D:, : 2 * D]
        + acc_nin[:D, 2 * D :]
        + acc_nin[D:, 2 * D :]
    )
    pick = lambda ref, start, i: jnp.sum(
        jnp.where(lane[:, :16] == i, ref[:D, start:] + ref[D:, start:], 0.0),
        axis=1,
        keepdims=True,
    )
    lane_sum = lambda i: jnp.sum(acc_vec[i], axis=1, keepdims=True)
    by_degree = lane_sum(3)
    acc[2] = plain * columns[C_ROWS, 0:1, :] + by_degree * columns[C_ROWS, 1:2, :]
    acc[3] = jnp.where(left, folded(acc_hidden), folded(acc_nout))
    weight_n = columns[C_WEIGHT_N]
    gain_row = jnp.sum(weight_n * plain, axis=0, keepdims=True)[:, D:]
    shift_row = jnp.sum(weight_n * by_degree, axis=0, keepdims=True)[:, D:]
    block = jnp.zeros((D, LANES), F32)
    for i, vector in (
        (1, pick(acc_hidden, 2 * D, 0)),
        (2, to_column(gain_row)),
        (3, to_column(shift_row)),
        (4, lane_sum(2)),
        (5, pick(acc_nout, 2 * D, 0)),
        (6, lane_sum(0)),
        (7, lane_sum(1)),
        (8, columns[C_DIVERGED]),
    ):
        block = jnp.where(lane == D + i, vector, block)
    acc[1] = block
    pltpu.make_async_copy(acc, acc_out, out_sem).start()
    for ref in (fresh, part, grad_recv, own.at[pl.ds(0, rows + 2)], cells, staged, acc):
        waits(ref, out_sem)


def layer_call(edges, cotangent, projected, receiver, sides, codes, valid, pack, columns, state):
    rows = cotangent.shape[1]
    wide = NBR * LANES
    tile = (D, LANES)
    shape = lambda *dims: jax.ShapeDtypeStruct(dims, F32)
    vmem = lambda *dims: pltpu.VMEM(dims, F32)
    return pl.pallas_call(
        layer_kernel,
        name="layer",
        out_shape=(
            shape(D, rows, LANES),
            shape(D, NBR, rows, LANES),
            shape(rows, *tile),
            shape(rows, *tile),
            shape(rows + 2, *tile),
            shape(2, *tile),
            shape(4, *tile),
        ),
        in_specs=[HBM] * 10,
        out_specs=[HBM] * 7,
        scratch_shapes=[
            vmem(rows, D, wide),
            pltpu.VMEM((rows, 2 * D, wide), BF16),
            pltpu.VMEM((rows, 2 * D + 16, wide), BF16),
            vmem(rows, D, wide),
            vmem(rows, D, wide),
            vmem(rows, D, wide),
            vmem(rows + 6, 3, *tile),
            vmem(rows + 6, *tile),
            vmem(rows, *tile),
            vmem(2, *tile),
            pltpu.VMEM((rows, 8, LANES), jnp.int32),
            vmem(rows, 8, LANES),
            pltpu.VMEM((P_ROWS, P_LANES), BF16),
            vmem(C_TILES, *tile),
            vmem(rows + 2, *tile),
            vmem(rows, 8, LANES),
            vmem(rows, *tile),
            vmem(rows, *tile),
            vmem(rows, *tile),
            vmem(rows // 8, D, 8, LANES),
            vmem(rows // 8, D, 8, LANES),
            vmem(rows + 2, 3, *tile),
            vmem(2, *tile),
            pltpu.VMEM((4, 4 * D, wide), BF16),
            vmem(2 * D, 2 * D),
            vmem(2 * D, 2 * D + 16),
            vmem(2 * D, 4 * D),
            vmem(2 * D, 2 * D + 16),
            vmem(4, *tile),
            vmem(4, *tile),
            pltpu.SemaphoreType.DMA((2,)),
            pltpu.SemaphoreType.DMA((rows,)),
            pltpu.SemaphoreType.DMA((2,)),
            pltpu.SemaphoreType.DMA,
        ],
        compiler_params=pltpu.CompilerParams(vmem_limit_bytes=ROOM),
    )(edges, cotangent, projected, receiver, sides, codes, valid, pack, columns, state)


def sum_kernel(
    n_blk,
    n_lon,
    acc_in,
    own_in,
    cells_in,
    recv_in,
    part_in,
    state_in,
    cols_all,
    pack_in,
    columns_in,
    mean,
    logstd,
    noise,
    nodes_out,
    mean_out,
    logstd_out,
    total_out,
    acc,
    own,
    cells,
    grad_recv,
    part,
    natural,
    mean_v,
    logstd_v,
    noise_v,
    inside,
    state,
    cols,
    pack,
    edge_rows,
    edge_cols,
    edge_corners,
    rows_in,
    cols_in,
    corners_in,
    acc_send,
    acc_recv,
    packed,
    scattered,
    across,
    gathered,
    in_sem,
    row_sem,
    rs_send,
    rs_recv,
    x_send,
    x_recv,
    ag_send,
    ag_recv,
    halo_send,
    halo_recv,
    latent_sem,
    out_sem,
):
    rows = recv_in.shape[0]
    blk, lon, around = neighbours(n_blk, n_lon)
    size = scattered.shape[0]
    n_groups = across.shape[0]
    per = size // n_lon
    me = lax.rem(blk, per) * n_lon + lon
    own_group = blk // per
    lane = lane_ids()

    def member(index):
        if n_lon & (n_lon - 1):
            return (own_group * per + index // n_lon, lax.rem(index, n_lon))
        return (own_group * per + (index >> (n_lon.bit_length() - 1)), index & (n_lon - 1))

    def other(step):
        if size & (size - 1):
            return lax.rem(me + step, size)
        return (me + step) & (size - 1)

    def peer(step):
        return (lax.rem(own_group + step, n_groups) * per + lax.rem(blk, per), lon)

    half = rows // 2
    for h in range(2):
        span = pl.ds(h * half, half)
        span3 = pl.ds(0, half + 1) if h == 0 else pl.ds(half + 1, half + 1)
        for source, target in (
            (own_in.at[span3], own.at[span3]),
            (state_in.at[span3], state.at[span3]),
            (recv_in.at[span], grad_recv.at[span]),
        ):
            pltpu.make_async_copy(source, target, row_sem.at[h]).start()
    small = (
        (pack_in.at[pl.ds(P_SEND_T[0], 2 * D)], pack),
        (cols_all, cols),
        (acc_in, acc),
        (part_in, part),
        (cells_in, cells),
        (columns_in.at[C_VALID], inside),
    )
    for i, (source, target) in enumerate(small):
        pltpu.make_async_copy(source, target, in_sem.at[i]).start()

    groups = [pl.ds(8 * g, 8) for g in range(rows // 8)]
    latent = ((mean, mean_v), (logstd, logstd_v), (noise, noise_v))
    barrier = pltpu.get_barrier_semaphore()

    def greet(step, _):
        pl.semaphore_signal(
            barrier, inc=1, device_id=member(other(step)), device_id_type=MESH
        )

    lax.fori_loop(1, size, greet, None)
    expected = size - 1
    if n_groups > 1:
        for place in around:
            pl.semaphore_signal(barrier, inc=1, device_id=place, device_id_type=MESH)

        def greet_group(step, _):
            pl.semaphore_signal(barrier, inc=1, device_id=peer(step), device_id_type=MESH)

        lax.fori_loop(1, n_groups, greet_group, None)
        expected += 8 + n_groups - 1

    acc_send[...] = jnp.zeros_like(acc_send)
    acc_recv[...] = jnp.zeros_like(acc_recv)

    def both_halves(value):
        return jnp.concatenate(halves(value), axis=0)

    ones_row = jnp.where(
        lax.broadcasted_iota(jnp.int32, (16, 4 * LANES), 0) < 1, 1.0, 0.0
    ).astype(BF16)

    def collect(i, _):
        wide = lambda ref, first: both_halves(
            jnp.concatenate([ref[first + u] for u in range(4)], axis=1)
        )
        there = wide(state, 1 + 4 * i)
        acc_send[...] += outer(wide(own, 1 + 4 * i), there)
        acc_recv[...] += outer(
            wide(grad_recv, 4 * i), jnp.concatenate([there, ones_row], axis=0)
        )

    for h in range(2):
        waits(own.at[pl.ds(h * (half + 1), half + 1)], row_sem.at[h])
        waits(state.at[pl.ds(h * (half + 1), half + 1)], row_sem.at[h])
        waits(grad_recv.at[pl.ds(h * half, half)], row_sem.at[h])
        lax.fori_loop(h * half // 4, (h + 1) * half // 4, collect, None)
    waits(cells, in_sem.at[4])
    waits(cols, in_sem.at[1])
    edge_values = jnp.concatenate([own[0], own[rows + 1], cells[0], cells[1]], axis=1)
    edge_states = jnp.concatenate([state[0], state[rows + 1], cols[0], cols[1]], axis=1)
    acc_send[...] += outer(both_halves(edge_values), both_halves(edge_states))

    def folded(ref):
        part_sum = ref[:D, : 2 * D] + ref[D:, : 2 * D]
        return part_sum + pltpu.roll(part_sum, D, 1)

    left = lane < D
    waits(acc, in_sem.at[2])
    ones_sum = jnp.sum(
        jnp.where(lane[:, :16] == 0, acc_recv[:D, 2 * D :] + acc_recv[D:, 2 * D :], 0.0),
        axis=1,
        keepdims=True,
    )
    columns_t = jnp.where(lane == D, ones_sum, acc[1]).T[D:]
    vector_rows = jnp.concatenate([jnp.zeros((D, D), F32), columns_t], axis=1)
    chunk = packed.shape[1]
    blocks = (
        jnp.where(left, acc[0], folded(acc_send)),
        jnp.where(left, folded(acc_recv), vector_rows),
        acc[2],
        acc[3],
    )
    per_block = D // chunk
    for i, block in enumerate(blocks):
        for j in range(per_block):
            packed[i * per_block + j] = block[j * chunk : (j + 1) * chunk]
    for g, span in enumerate(groups):
        for source, target in latent:
            pltpu.make_async_copy(source.at[:, span, :], target.at[g], latent_sem).start()

    pl.semaphore_wait(barrier, expected)

    def scatter(step, _):
        target = other(step)
        pltpu.make_async_remote_copy(
            src_ref=packed.at[target],
            dst_ref=scattered.at[me],
            send_sem=rs_send,
            recv_sem=rs_recv,
            device_id=member(target),
            device_id_type=MESH,
        ).start()

    lax.fori_loop(1, size, scatter, None)
    scattered[me] = packed[me]

    waits(pack, in_sem.at[0])
    a_send = pack[:D, : 3 * D]
    a_recv = pack[D : 2 * D, : 3 * D]
    high, low = halves(edge_values)
    edge_grads = mxu(a_send, jnp.concatenate([high, low, high], axis=0))
    edge_grad = [edge_grads[:, i * LANES : (i + 1) * LANES] for i in range(4)]
    edge_rows[0], edge_rows[1] = edge_grad[0], edge_grad[1]
    west_cells, east_cells = edge_grad[2], edge_grad[3]
    edge_cols[0], edge_cols[1] = pack_column(west_cells), pack_column(east_cells)
    edge_corners[...] = corner_rows(
        [
            west_cells[:, :1],
            east_cells[:, LANES - 1 :],
            west_cells[:, rows + 1 : rows + 2],
            east_cells[:, rows : rows + 1],
        ]
    )
    copies = rim_copies(
        around,
        edge_rows,
        edge_cols,
        edge_corners,
        rows_in,
        cols_in,
        corners_in,
        halo_send,
        halo_recv,
    )
    for copy in copies:
        copy.start()
    waits(part, in_sem.at[3])

    def finish(i, _):
        for u in range(2):
            first = 4 * i + 2 * u
            grads = None
            for weights, ref, offset in ((a_send, own, 1), (a_recv, grad_recv, 0)):
                high, low = halves(
                    jnp.concatenate([ref[first + offset], ref[first + offset + 1]], axis=1)
                )
                product = mxu(weights, jnp.concatenate([high, low, high], axis=0))
                grads = product if grads is None else grads + product
            for j in range(2):
                part[first + j] += grads[:, j * LANES : (j + 1) * LANES]

    lax.fori_loop(0, rows // 4, finish, None)

    waits(inside, in_sem.at[5])
    for _, target in latent:
        waits(target, latent_sem)
    weight = inside[0:1, :].reshape(1, 1, LANES)

    def blocks(i):
        return i // 8, pl.ds(8 * (i % 8), 8)

    def latent_terms(i, _):
        at = blocks(i)
        spread = jnp.exp(logstd_v[at])
        mean_v[at] = weight * mean_v[at]
        noise_v[at] = spread * noise_v[at]
        logstd_v[at] = weight * (spread * spread - 1.0)

    lax.fori_loop(0, rows, latent_terms, None)

    others = pl.ds(0, size - 1)
    waits(scattered.at[others], rs_recv)
    mine = scattered[0]
    for i in range(1, size):
        mine = mine + scattered[i]
    if n_groups > 1:
        across[own_group] = mine

        def cross(step, _):
            pltpu.make_async_remote_copy(
                src_ref=across.at[own_group],
                dst_ref=across.at[own_group],
                send_sem=x_send,
                recv_sem=x_recv,
                device_id=peer(step),
                device_id_type=MESH,
            ).start()

        lax.fori_loop(1, n_groups, cross, None)
        rest = pl.ds(0, n_groups - 1)
        waits(across.at[rest], x_recv)
        waits(across.at[rest], x_send)
        mine = across[0]
        for i in range(1, n_groups):
            mine = mine + across[i]
    gathered[me] = mine

    def gather(step, _):
        pltpu.make_async_remote_copy(
            src_ref=gathered.at[me],
            dst_ref=gathered.at[me],
            send_sem=ag_send,
            recv_sem=ag_recv,
            device_id=member(other(step)),
            device_id_type=MESH,
        ).start()

    lax.fori_loop(1, size, gather, None)
    for copy in copies:
        copy.wait()
    west_in = (
        pltpu.roll(jnp.where(lane < rows, unpack_column(cols_in[1]), 0.0), 1, 1)
        + corner_at(corners_in.at[3], 3, 1)
        + corner_at(corners_in.at[1], 1, rows)
    )
    east_in = unpack_column(cols_in[0])
    east_in = (
        pltpu.roll(jnp.where((lane >= 1) & (lane <= rows), east_in, 0.0), LANES - 1, 1)
        + corner_at(corners_in.at[2], 2, 0)
        + corner_at(corners_in.at[0], 0, rows - 1)
    )
    rim = (lane == 0) | (lane == LANES - 1)
    part[0] += rows_in[1]
    part[rows - 1] += rows_in[0]

    def add_columns(i, _):
        for u in range(4):
            r = 4 * i + u
            mix = pltpu.roll(
                jnp.where(lane == r + 1, west_in, east_in), LANES - 1 - r, 1
            )
            write_row(natural.at[r // 8], lax.rem(r, 8), part[r] + jnp.where(rim, mix, 0.0))

    lax.fori_loop(0, rows // 4, add_columns, None)

    def latent_grads(i, _):
        at = blocks(i)
        grad = natural[at]
        mean_v[at] = grad + mean_v[at]
        logstd_v[at] = grad * noise_v[at] + logstd_v[at]

    lax.fori_loop(0, rows, latent_grads, None)
    results = ((natural, nodes_out), (mean_v, mean_out), (logstd_v, logstd_out))
    for g, span in enumerate(groups):
        for source, target in results:
            pltpu.make_async_copy(source.at[g], target.at[:, span, :], out_sem).start()
    waits(gathered.at[others], ag_recv)
    pltpu.make_async_copy(gathered, total_out, out_sem).start()
    waits(scattered.at[others], rs_send)
    waits(gathered.at[others], ag_send)
    for ref in (natural, mean_v, logstd_v, gathered):
        waits(ref, out_sem)


def sum_call(n_blk, n_lon, *operands):
    recv = operands[3]
    rows = recv.shape[0]
    size = min(32, n_blk * n_lon)
    n_groups = n_blk * n_lon // size
    chunk = (4 * D // size, LANES)
    tile = (D, LANES)
    shape = lambda *dims: jax.ShapeDtypeStruct(dims, F32)
    vmem = lambda *dims: pltpu.VMEM(dims, F32)
    dma = pltpu.SemaphoreType.DMA
    return pl.pallas_call(
        functools.partial(sum_kernel, n_blk, n_lon),
        name="sums",
        out_shape=(shape(D, rows, LANES),) * 3 + (shape(size, *chunk),),
        in_specs=[HBM] * 12,
        out_specs=[HBM] * 4,
        scratch_shapes=[
            vmem(4, *tile),
            vmem(rows + 2, *tile),
            vmem(2, *tile),
            vmem(rows, *tile),
            vmem(rows, *tile),
            vmem(rows // 8, D, 8, LANES),
            vmem(rows // 8, D, 8, LANES),
            vmem(rows // 8, D, 8, LANES),
            vmem(rows // 8, D, 8, LANES),
            vmem(*tile),
            vmem(rows + 2, *tile),
            vmem(2, *tile),
            pltpu.VMEM((2 * D, P_LANES), BF16),
            vmem(2, *tile),
            vmem(2, D // 2, LANES),
            vmem(8, LANES),
            vmem(2, *tile),
            vmem(2, D // 2, LANES),
            vmem(4, 8, LANES),
            vmem(2 * D, 2 * D),
            vmem(2 * D, 2 * D + 16),
            vmem(size, *chunk),
            vmem(size, *chunk),
            vmem(n_groups, *chunk),
            vmem(size, *chunk),
            dma((6,)),
            dma((2,)),
            dma,
            dma,
            dma,
            dma,
            dma,
            dma,
            dma((8,)),
            dma((8,)),
            dma,
            dma,
        ],
        compiler_params=pltpu.CompilerParams(
            collective_id=1, has_side_effects=True, vmem_limit_bytes=ROOM
        ),
    )(*operands)


def final_kernel(*refs):
    large_in, (total_in, columns_in), refs = refs[:3], refs[3:5], refs[5:]
    large_outs, small_outs, refs = refs[:3], refs[3:16], refs[16:]
    large, (total, columns), smalls, refs = refs[:3], refs[3:5], refs[5:18], refs[18:]
    in_sem, small_sem, out_sem = refs
    n_chunks = in_sem.shape[0]
    depth = D // n_chunks
    for i, (source, target) in enumerate(((columns_in, columns), (total_in, total))):
        pltpu.make_async_copy(source, target, small_sem.at[i]).start()
    spans = [pl.ds(i * depth, depth) for i in range(n_chunks)]
    for i, span in enumerate(spans):
        for source, target in zip(large_in, large):
            pltpu.make_async_copy(source.at[span], target.at[span], in_sem.at[i]).start()

    def forward_block(i):
        for ref in large:
            waits(ref.at[spans[i]], in_sem.at[i])
        for source, target in zip(large, large_outs):
            pltpu.make_async_copy(source.at[spans[i]], target.at[spans[i]], out_sem).start()

    for i in range(2):
        forward_block(i)

    waits(columns, small_sem.at[0])
    waits(total, small_sem.at[1])
    kl_value, g_w_ei, g_w_eo, g_w_ni, g_w_no = smalls[:5]
    chunk = total.shape[1]
    per_block = D // chunk
    blocks = [
        jnp.concatenate([total[i * per_block + j] for j in range(per_block)], axis=0)
        for i in range(4)
    ]
    g_w_ei[:, : 2 * D] = blocks[0]
    g_w_ei[:, 2 * D :] = blocks[1][:, :D]
    g_w_ni[...] = blocks[2]
    g_w_eo[...] = blocks[3][:, :D]
    g_w_no[...] = pltpu.roll(blocks[3], D, 1)[:, :D]
    vector_rows = pltpu.roll(blocks[1][:16], D, 1)
    for i in range(8):
        smalls[5 + i][...] = vector_rows[i : i + 1, :D]
    diverged = jnp.sum(vector_rows[8:9, :D], axis=1, keepdims=True)
    kl_value[...] = diverged / columns[C_COUNT, 0:1, 0:1]
    for source, target in zip(smalls, small_outs):
        pltpu.make_async_copy(source, target, out_sem).start()

    for i in range(2, n_chunks):
        forward_block(i)
    for ref in (*large, *smalls):
        waits(ref, out_sem)


def final_call(*operands):
    shape = lambda *dims: jax.ShapeDtypeStruct(dims, F32)
    vmem = lambda *dims: pltpu.VMEM(dims, F32)
    whole, total = operands[0].shape, operands[3].shape
    small = ((1, 1), (D, 3 * D), (D, D), (D, 2 * D), (D, D)) + ((1, D),) * 8
    return pl.pallas_call(
        final_kernel,
        name="final",
        out_shape=[shape(*dims) for dims in (whole,) * 3 + small],
        in_specs=[HBM] * 5,
        out_specs=[HBM] * 16,
        scratch_shapes=[vmem(*whole) for _ in range(3)]
        + [vmem(*total), vmem(C_TILES, D, LANES)]
        + [vmem(*dims) for dims in small]
        + [
            pltpu.SemaphoreType.DMA((8,)),
            pltpu.SemaphoreType.DMA((2,)),
            pltpu.SemaphoreType.DMA,
        ],
        compiler_params=pltpu.CompilerParams(vmem_limit_bytes=ROOM),
    )(*operands)


def shards(
    nodes,
    edges,
    latent_mean,
    latent_logstd,
    latent_noise,
    kl_weight,
    band_counts,
    neighbors,
    edge_mask,
    w_edge_in,
    b_edge_in,
    w_edge_out,
    b_edge_out,
    edge_gain,
    edge_shift,
    w_node_in,
    b_node_in,
    w_node_out,
    b_node_out,
    node_gain,
    node_shift,
    cotangent,
):
    n_blk = lax.axis_size("blk")
    n_lon = lax.axis_size("lon")
    vectors = (
        b_edge_in,
        b_edge_out,
        edge_gain,
        edge_shift,
        b_node_in,
        b_node_out,
        node_gain,
        node_shift,
    )
    weights = (w_edge_in, w_edge_out, w_node_in, w_node_out)
    weights += tuple(vector.reshape(1, D) for vector in vectors)
    state, cols, projected, receiver, sides, codes, valid, pack, columns = start_call(
        n_blk,
        n_lon,
        band_counts,
        kl_weight,
        nodes,
        latent_mean,
        latent_logstd,
        latent_noise,
        neighbors,
        edge_mask,
        weights,
    )
    new_states, grad_edges, part, recv, own, cells, acc = layer_call(
        edges, cotangent, projected, receiver, sides, codes, valid, pack, columns, state
    )
    grads = sum_call(
        n_blk,
        n_lon,
        acc,
        own,
        cells,
        recv,
        part,
        state,
        cols,
        pack,
        columns,
        latent_mean,
        latent_logstd,
        latent_noise,
    )
    grad_nodes, grad_mean, grad_logstd, kl_value, g_w_ei, g_w_eo, g_w_ni, g_w_no, *g_vec = (
        final_call(*grads, columns)
    )
    g_vec = [vector.reshape(D) for vector in g_vec]
    return (
        new_states,
        kl_value.reshape(1),
        grad_nodes,
        grad_edges,
        grad_mean,
        grad_logstd,
        g_w_ei,
        g_vec[0],
        g_w_eo,
        g_vec[1],
        g_vec[2],
        g_vec[3],
        g_w_ni,
        g_vec[4],
        g_w_no,
        g_vec[5],
        g_vec[6],
        g_vec[7],
    )


def solution(mesh):
    node = P(None, "blk", "lon")
    slot = P(None, None, "blk", "lon")
    return jax.shard_map(
        shards,
        mesh=mesh,
        in_specs=(
            (node, slot, node, node, node, P(), P(), node, node) + (P(),) * 12 + (node,)
        ),
        out_specs=(node, P(), node, slot, node, node) + (P(),) * 12,
        check_vma=False,
    )
```

```python
import functools

import jax
import jax.numpy as jnp
from jax import lax
from jax.experimental import pallas as pl
from jax.experimental.pallas import tpu as pltpu
from jax.sharding import PartitionSpec as P

F32 = jnp.float32
BF16 = jnp.bfloat16
MESH = pl.DeviceIdType.MESH
D = 64
LANES = 128
NBR = 6
EPS = 1e-05
HBM = pl.BlockSpec(memory_space=pltpu.HBM)
VMEM = pl.BlockSpec(memory_space=pltpu.VMEM)
ROOM = 62 * 2**20
SMEM = pl.BlockSpec(memory_space=pltpu.SMEM)

WINDOWS = ((-1, -1), (-1, 0), (-1, 1), (0, -1), (0, 1), (1, -1), (1, 0), (1, 1))


def halves(value):
    high = value.astype(BF16)
    return high, (value - high.astype(F32)).astype(BF16)


def weight_pack(weight, *biases):
    high, low = halves(weight)
    if not biases:
        return jnp.concatenate([high, high, low], axis=1)
    place = lax.broadcasted_iota(jnp.int32, (weight.shape[0], 16), 1)
    wide = jnp.zeros((weight.shape[0], 16), F32)
    for i, bias in enumerate(biases):
        for j, part in enumerate(halves(bias)):
            wide = jnp.where(place == 2 * i + j, part.astype(F32), wide)
    return jnp.concatenate([high, high, wide.astype(BF16), low], axis=1)


def mxu(left, right):
    return jnp.dot(left, right, preferred_element_type=F32)


def outer(left, right):
    return lax.dot_general(
        left, right, (((1,), (1,)), ((), ())), preferred_element_type=F32
    )


def exact(left, right, dims):
    return lax.dot_general(
        left,
        right,
        (dims, ((), ())),
        precision=lax.Precision.HIGHEST,
        preferred_element_type=F32,
    )


def eye():
    return lax.broadcasted_iota(jnp.int32, (D, D), 0) == lax.broadcasted_iota(
        jnp.int32, (D, D), 1
    )


def to_column(row):
    return jnp.sum(jnp.where(eye(), row, 0.0), axis=1, keepdims=True)


def to_row(column):
    return jnp.sum(jnp.where(eye(), column, 0.0), axis=0, keepdims=True)


def waits(ref, sem):
    pltpu.make_async_copy(ref, ref, sem).wait()


def in_turn(*routines):
    waiting = list(routines)
    while waiting:
        for routine in list(waiting):
            if next(routine, routine) is routine:
                waiting.remove(routine)


def lane_ids(rows=D):
    return lax.broadcasted_iota(jnp.int32, (rows, LANES), 1)


P_HIDDEN, P_EDGE, P_EDGE_T, P_NODE_OUT = (0, 128), (128, 192), (192, 256), (256, 320)
P_NODE_OUT_T, P_NODE_IN_T, P_SEND_T, P_RECV_T = (320, 384), (384, 576), (576, 640), (640, 704)
P_NODE_IN, P_NODE_IN_END = (704, 768), (768, 832)
P_ROWS, P_LANES = 832, 256
C_GAIN_N, C_SHIFT_N, C_VALID, C_DIVERGED, C_COUNT, C_WEIGHT_N, C_ROWS = range(7)
C_TILES = 7


def packed_rows(ref, rows, lanes=3 * D):
    return ref[rows[0] : rows[1], :lanes]


def row_of(ref, row, step, count=D):
    flat = ref.reshape(count * step, LANES)
    return flat, pl.ds(row, count, stride=step)


def read_row(ref, row, step=8):
    flat, place = row_of(ref, row, step)
    return flat[place, :]


def write_row(ref, row, value, step=8):
    flat, place = row_of(ref, row, step)
    flat[place, :] = value


def pack_column(tile):
    return jnp.where(lane_ids(D // 2) < D, tile[: D // 2], pltpu.roll(tile[D // 2 :], D, 1))


def unpack_column(tile):
    return jnp.concatenate([tile, pltpu.roll(tile, D, 1)], axis=0)


def corner_rows(columns):
    rows = [to_row(column) for column in columns]
    wide = jnp.concatenate(rows + [jnp.zeros((4, D), F32)], axis=0)
    return jnp.concatenate([wide, jnp.zeros((8, D), F32)], axis=1)


def corner_at(ref, row, lane):
    return jnp.where(lane_ids() == lane, to_column(ref[row : row + 1, :D]), 0.0)


def rim_copies(around, rows, columns, corners, rows_in, columns_in, corners_in, send, recv):
    pairs = [(rows.at[0], rows_in.at[0]), (rows.at[1], rows_in.at[1])]
    pairs += [(columns.at[0], columns_in.at[0]), (columns.at[1], columns_in.at[1])]
    pairs += [(corners, corners_in.at[i]) for i in range(4)]
    return [
        pltpu.make_async_remote_copy(
            src_ref=source,
            dst_ref=target,
            send_sem=send.at[slot],
            recv_sem=recv.at[slot],
            device_id=place,
            device_id_type=MESH,
        )
        for slot, (place, (source, target)) in enumerate(zip(around, pairs))
    ]


def neighbours(n_blk, n_lon):
    blk = lax.axis_index("blk")
    lon = lax.axis_index("lon")
    up = lax.rem(blk + n_blk - 1, n_blk)
    down = lax.rem(blk + 1, n_blk)
    west = lax.rem(lon + n_lon - 1, n_lon)
    east = lax.rem(lon + 1, n_lon)
    around = (
        (up, lon),
        (down, lon),
        (blk, west),
        (blk, east),
        (up, west),
        (up, east),
        (down, west),
        (down, east),
    )
    return blk, lon, around


def start_kernel(
    n_blk,
    n_lon,
    counts,
    kl_weight,
    nodes,
    mean,
    logstd,
    noise,
    neighbors,
    edge_mask,
    w_ei,
    w_eo,
    w_ni,
    w_no,
    *rest,
):
    vectors = rest[:8]
    (
        state_out,
        cols_out,
        project_out,
        receive_out,
        sides_out,
        codes_out,
        valid_out,
        pack_out,
        columns_out,
        buf,
        state,
        projected,
        receiver,
        sides,
        nb,
        mk,
        codes,
        valid,
        v_ei,
        v_eo,
        v_ni,
        v_no,
        v_vec,
        pack,
        columns,
        cols,
        edge_rows,
        edge_cols,
        edge_corners,
        rows_in,
        cols_in,
        corners_in,
        in_sem,
        slot_sem,
        weight_sem,
        send_sem,
        recv_sem,
        out_sem,
    ) = rest[8:]
    rows = nodes.shape[1]
    blk, lon, around = neighbours(n_blk, n_lon)
    barrier = pltpu.get_barrier_semaphore()
    for place in around:
        pl.semaphore_signal(barrier, inc=1, device_id=place, device_id_type=MESH)

    n_groups = in_sem.shape[0]
    group = rows // n_groups
    for g in range(n_groups):
        for which, source in enumerate((nodes, mean, logstd, noise)):
            pltpu.make_async_copy(
                source.at[:, pl.ds(g * group, group), :], buf.at[g, which], in_sem.at[g]
            ).start()
    weights = [(w_ei, v_ei), (w_eo, v_eo), (w_ni, v_ni), (w_no, v_no)]
    weights += [(vectors[i], v_vec.at[i]) for i in range(8)]
    lane = lane_ids()
    count = counts[blk]
    inside = lane < count

    def state_row(g, j, carry):
        total, west_tile, east_tile = carry
        r = g * group + j
        node_r, mean_r, logstd_r, noise_r = [
            read_row(buf.at[g, which], j, group) for which in range(4)
        ]
        spread = jnp.exp(logstd_r)
        value = node_r + mean_r + spread * noise_r
        state[r + 1] = value
        total += jnp.where(inside, mean_r * mean_r + spread * spread - 2.0 * logstd_r, 0.0)
        moved = pltpu.roll(value, r + 1, 1)
        west_tile = jnp.where(lane == r + 1, moved, west_tile)
        east_tile = jnp.where(lane == r, moved, east_tile)
        return total, west_tile, east_tile

    carry = (jnp.zeros((D, LANES), F32),) * 3
    for source, target in weights:
        pltpu.make_async_copy(source, target, weight_sem).start()

    def state_group(g, carry):
        waits(buf.at[g], in_sem.at[g])
        for j in range(0, group, 2):
            carry = state_row(g, j + 1, state_row(g, j, carry))
        return carry

    carry = lax.fori_loop(0, n_groups, state_group, carry)
    total, west_tile, east_tile = carry
    edge_rows[0] = state[1]
    edge_rows[1] = state[rows]
    edge_cols[0] = pack_column(west_tile)
    edge_cols[1] = pack_column(east_tile)
    edge_corners[...] = corner_rows(
        [
            state[row][:, lane0 : lane0 + 1]
            for row in (1, rows)
            for lane0 in (0, LANES - 1)
        ]
    )

    pl.semaphore_wait(barrier, 8)
    copies = rim_copies(
        around,
        edge_rows,
        edge_cols,
        edge_corners,
        rows_in,
        cols_in,
        corners_in,
        send_sem,
        recv_sem,
    )
    for copy in copies:
        copy.start()
    pltpu.make_async_copy(neighbors, nb, slot_sem).start()
    pltpu.make_async_copy(edge_mask, mk, slot_sem).start()
    inner = pl.ds(1, rows)
    pltpu.make_async_copy(state.at[inner], state_out.at[inner], out_sem).start()

    for _, target in weights:
        waits(target, weight_sem)
    b_ei, b_eo, gain_e, shift_e, b_ni, b_no, gain_n, shift_n = [
        to_column(v_vec[i]) for i in range(8)
    ]
    n_valid = counts[0]
    for i in range(1, counts.shape[0]):
        n_valid += counts[i]
    for i, column in (
        (C_GAIN_N, gain_n),
        (C_SHIFT_N, shift_n),
        (C_VALID, jnp.where(inside, kl_weight[0], 0.0)),
        (C_COUNT, jnp.full((D, LANES), (D * rows * n_lon * n_valid).astype(F32))),
        (
            C_DIVERGED,
            0.5 * jnp.sum(total - rows * jnp.where(inside, 1.0, 0.0), axis=1, keepdims=True),
        ),
    ):
        columns[i] = jnp.broadcast_to(column, (D, LANES))
    w_in = v_ei[...]
    w_e, w_s, w_r = w_in[:, :D], w_in[:, D : 2 * D], w_in[:, 2 * D :]
    a_state = jnp.concatenate([weight_pack(0.5 * w_s), weight_pack(0.5 * w_r)], axis=0)
    w_o = v_eo[...]
    w_oc = w_o - jnp.mean(w_o, axis=0, keepdims=True)
    b_oc = b_eo - jnp.mean(b_eo, axis=0, keepdims=True)
    back = 0.5 * exact(w_o, w_oc, ((0,), (0,)))
    b_back = 0.5 * exact(w_o, b_oc, ((0,), (0,)))
    w_n = v_ni[...]
    w_nt = w_n.T
    gain_row, shift_row = v_vec[2], v_vec[3]
    one_row = jnp.ones_like(gain_row)
    scale_row = jnp.concatenate([one_row, gain_row], axis=1)
    add_row = jnp.concatenate([0.0 * one_row, shift_row], axis=1)
    columns[C_WEIGHT_N] = w_n
    row_id = lax.broadcasted_iota(jnp.int32, (D, LANES), 0)
    columns[C_ROWS] = jnp.where(row_id == 0, scale_row, jnp.where(row_id == 1, add_row, 0.0))
    w_shift = jnp.sum(w_n * add_row, axis=1, keepdims=True)
    w_out = v_no[...]
    scaled = gain_e * w_nt[D:]
    scaled = scaled - jnp.mean(scaled, axis=0, keepdims=True)

    def put(place, *parts):
        value = jnp.concatenate(parts, axis=0) if len(parts) > 1 else parts[0]
        pack[place[0] : place[1], : value.shape[1]] = value

    put(P_EDGE, weight_pack(0.5 * w_e))
    put(P_HIDDEN, weight_pack(w_oc, b_oc), weight_pack(back, b_back))
    put(P_EDGE_T, weight_pack(w_e.T))
    put(P_SEND_T, weight_pack(w_s.T))
    put(P_RECV_T, weight_pack(w_r.T))
    node_in = weight_pack(0.5 * w_n * scale_row, 0.5 * b_ni, 0.5 * w_shift)
    put(P_NODE_IN, node_in[:, :P_LANES])
    put(P_NODE_IN_END, node_in[:, P_LANES:])
    put(
        P_NODE_OUT,
        weight_pack(
            w_out - jnp.mean(w_out, axis=0, keepdims=True),
            b_no - jnp.mean(b_no, axis=0, keepdims=True),
        ),
    )
    put(P_NODE_OUT_T, weight_pack(0.5 * w_out.T))
    put(
        P_NODE_IN_T,
        weight_pack(w_nt[:D]),
        weight_pack(scaled),
        weight_pack(0.5 * exact(w_o, scaled, ((0,), (0,)))),
    )
    pltpu.make_async_copy(pack, pack_out, out_sem).start()
    pltpu.make_async_copy(columns, columns_out, out_sem).start()

    waits(nb, slot_sem)
    waits(mk, slot_sem)
    before = counts[lax.rem(blk + n_blk - 1, n_blk)]
    after = counts[lax.rem(blk + 1, n_blk)]
    row_id = lax.broadcasted_iota(jnp.int32, (rows, LANES), 0)
    col_id = lax.broadcasted_iota(jnp.int32, (rows, LANES), 1)
    above = jnp.where(row_id == 0, before, count)
    below = jnp.where(row_id == rows - 1, after, count)
    for k in range(NBR):
        delta = nb[k] - (row_id * (LANES + 2) + col_id)
        first = delta < LANES + 2
        middle = delta < 2 * (LANES + 2)
        step = jnp.where(
            first, delta, jnp.where(middle, delta - (LANES + 2), delta - 2 * (LANES + 2))
        )
        codes[k] = jnp.where(first, step, jnp.where(middle, 3 + (step >> 1), 5 + step))
        owner = col_id + step - 1
        owner = jnp.where(owner < 0, LANES - 1, jnp.where(owner >= LANES, 0, owner))
        limit = jnp.where(first, above, jnp.where(middle, count, below))
        valid[k] = jnp.where((col_id < count) & (owner < limit), mk[k].astype(F32), 0.0)
    for k in range(NBR, 8):
        codes[k] = jnp.zeros((rows, LANES), jnp.int32)
        valid[k] = jnp.zeros((rows, LANES), F32)
    for k in range(8):
        pltpu.make_async_copy(codes.at[k], codes_out.at[:, k, :], out_sem).start()
        pltpu.make_async_copy(valid.at[k], valid_out.at[:, k, :], out_sem).start()

    half_bias = 0.5 * b_ei

    def project(i, _):
        high, low = halves(
            jnp.concatenate([state[1 + 4 * i + u] for u in range(4)], axis=1)
        )
        both = mxu(a_state, jnp.concatenate([high, low, high], axis=0))
        for u in range(4):
            s = slice(u * LANES, (u + 1) * LANES)
            projected[1 + 4 * i + u] = both[:D, s]
            receiver[4 * i + u] = both[D:, s] + half_bias

    lax.fori_loop(0, rows // 4, project, None)
    pltpu.make_async_copy(projected.at[inner], project_out.at[inner], out_sem).start()
    pltpu.make_async_copy(receiver, receive_out, out_sem).start()

    for copy in copies:
        copy.wait()
    state[rows + 1] = rows_in[0]
    state[0] = rows_in[1]
    from_east = unpack_column(cols_in[0])
    from_west = unpack_column(cols_in[1])
    cols[1] = (
        pltpu.roll(jnp.where((lane >= 1) & (lane <= rows), from_east, 0.0), LANES - 1, 1)
        + corner_at(corners_in.at[0], 0, rows)
        + corner_at(corners_in.at[2], 2, LANES - 1)
    )
    cols[0] = (
        pltpu.roll(jnp.where(lane < rows, from_west, 0.0), 1, 1)
        + corner_at(corners_in.at[1], 1, rows + 1)
        + corner_at(corners_in.at[3], 3, 0)
    )
    high, low = halves(
        jnp.concatenate([rows_in[1], rows_in[0], cols[0], cols[1]], axis=1)
    )
    rim = mxu(a_state[:D], jnp.concatenate([high, low, high], axis=0))
    projected[0] = rim[:, :LANES]
    projected[rows + 1] = rim[:, LANES : 2 * LANES]
    sides[0] = rim[:, 2 * LANES : 3 * LANES]
    sides[1] = rim[:, 3 * LANES :]
    for t in (0, rows + 1):
        pltpu.make_async_copy(projected.at[t], project_out.at[t], out_sem).start()
        pltpu.make_async_copy(state.at[t], state_out.at[t], out_sem).start()
    pltpu.make_async_copy(sides, sides_out, out_sem).start()
    pltpu.make_async_copy(cols, cols_out, out_sem).start()
    for ref in (pack, columns, codes, valid, receiver, state, projected, cols, sides):
        waits(ref, out_sem)


def start_call(n_blk, n_lon, counts, kl_weight, nodes, mean, logstd, noise, neighbors, mask, weights):
    rows = nodes.shape[1]
    tile = (D, LANES)
    shapes = (
        ((rows + 2, *tile), F32),
        ((2, *tile), F32),
        ((rows + 2, *tile), F32),
        ((rows, *tile), F32),
        ((2, *tile), F32),
        ((rows, 8, LANES), jnp.int32),
        ((rows, 8, LANES), F32),
        ((P_ROWS, P_LANES), BF16),
        ((C_TILES, *tile), F32),
    )
    vmem = lambda *dims: pltpu.VMEM(dims, F32)
    ints = lambda *dims: pltpu.VMEM(dims, jnp.int32)
    dma = pltpu.SemaphoreType.DMA
    return pl.pallas_call(
        functools.partial(start_kernel, n_blk, n_lon),
        name="start",
        out_shape=[jax.ShapeDtypeStruct(*shape) for shape in shapes],
        in_specs=[SMEM, SMEM] + [HBM] * (6 + len(weights)),
        out_specs=[HBM] * len(shapes),
        scratch_shapes=[
            vmem(rows // 8, 4, D, 8, LANES),
            vmem(rows + 2, *tile),
            vmem(rows + 2, *tile),
            vmem(rows, *tile),
            vmem(2, *tile),
            ints(NBR, rows, LANES),
            ints(NBR, rows, LANES),
            ints(8, rows, LANES),
            vmem(8, rows, LANES),
            vmem(D, 3 * D),
            vmem(D, D),
            vmem(D, 2 * D),
            vmem(D, D),
            vmem(8, 1, D),
            pltpu.VMEM((P_ROWS, P_LANES), BF16),
            vmem(C_TILES, *tile),
            vmem(2, *tile),
            vmem(2, *tile),
            vmem(2, D // 2, LANES),
            vmem(8, LANES),
            vmem(2, *tile),
            vmem(2, D // 2, LANES),
            vmem(4, 8, LANES),
            dma((rows // 8,)),
            dma,
            dma,
            dma((8,)),
            dma((8,)),
            dma,
        ],
        compiler_params=pltpu.CompilerParams(
            collective_id=0, has_side_effects=True, vmem_limit_bytes=ROOM
        ),
    )(counts, kl_weight, nodes, mean, logstd, noise, neighbors, mask, *weights)


def layer_kernel(
    edges,
    cotangent,
    project_in,
    receive_in,
    sides_in,
    codes_in,
    valid_in,
    pack_in,
    columns_in,
    state_in,
    new_states,
    grad_edges,
    part_out,
    recv_out,
    own_out,
    cells_out,
    acc_out,
    slope,
    xs,
    hs,
    cb,
    db,
    staged,
    windows,
    projected,
    receiver,
    sides,
    codes,
    valid,
    pack,
    columns,
    state,
    inverse,
    summed,
    qc_ref,
    qo_ref,
    cot,
    fresh,
    placed,
    cells,
    gather_grads,
    acc_edge,
    acc_hidden,
    acc_nin,
    acc_nout,
    acc_vec,
    acc,
    row_sem,
    edge_sem,
    in_sem,
    out_sem,
):
    rows = cotangent.shape[1]
    wide = NBR * LANES
    two = 2 * LANES
    part, grad_recv, own = receiver, summed, projected
    lane = lane_ids()

    halfway = 10

    def load_edges(r):
        for k in range(NBR):
            pltpu.make_async_copy(
                edges.at[:, k, r, :],
                staged.at[r, :, pl.ds(k * LANES, LANES)],
                edge_sem.at[r],
            ).start()

    first_weights = pl.ds(P_HIDDEN[0], P_EDGE[1])
    first_small = (
        (sides_in, sides),
        (pack_in.at[first_weights], pack.at[first_weights]),
        (codes_in, codes),
        (valid_in, valid),
    )
    parts = []
    for g, (first, last) in enumerate(((0, halfway), (halfway, rows + 2))):
        send, receive = pl.ds(first, last - first), pl.ds(first, min(last, rows) - first)
        part_g = ((project_in, projected, send), (receive_in, receiver, receive))
        for source, target, span in part_g:
            pltpu.make_async_copy(source.at[span], target.at[span], row_sem.at[g]).start()
        parts.append([target.at[span] for _, target, span in part_g])
        if g == 0:
            for source, target in first_small[:2]:
                pltpu.make_async_copy(source, target, in_sem.at[0]).start()
            for r in range(4):
                load_edges(r)
            for source, target in first_small[2:]:
                pltpu.make_async_copy(source, target, in_sem.at[0]).start()
    lax.fori_loop(4, 12, lambda r, _: load_edges(r), None)

    def load_rest():
        rest = pl.ds(P_EDGE[1], P_ROWS - P_EDGE[1])
        pltpu.make_async_copy(pack_in.at[rest], pack.at[rest], in_sem.at[1]).start()
        pltpu.make_async_copy(columns_in, columns, in_sem.at[1]).start()
        pltpu.make_async_copy(state_in, state, in_sem.at[1]).start()

        for g in range(rows // 8):
            pltpu.make_async_copy(
                cotangent.at[:, pl.ds(8 * g, 8), :], cot.at[g], in_sem.at[1]
            ).start()
        lax.fori_loop(12, rows, lambda r, _: load_edges(r), None)
        return (cot, state, columns, pack.at[rest])

    ones16 = jnp.where(
        lax.broadcasted_iota(jnp.int32, (16, wide), 0) < 2, 1.0, 0.0
    ).astype(BF16)
    ones_two = ones16[:, :two]
    for _, target in first_small:
        waits(target, in_sem.at[0])

    def shift(t):
        centre = projected[t]
        mix = pltpu.roll(
            jnp.where(lane == t, sides[0], sides[1]), lax.rem(LANES - t, LANES), 1
        )
        windows[t, 1] = centre
        windows[t, 0] = jnp.where(lane == 0, mix, pltpu.roll(centre, 1, 1))
        windows[t, 2] = jnp.where(lane == LANES - 1, mix, pltpu.roll(centre, LANES - 1, 1))

    def edge_product(r, pair):
        own = receiver[r]
        s = pl.ds(pair * two, two)
        high, low = halves(staged[r, :, s])
        xs[r, :D, s] = high
        xs[r, D:, s] = low
        out = mxu(packed_rows(pack, P_EDGE), jnp.concatenate([high, low, high], axis=0))
        slope[r, :, s] = out + jnp.concatenate([own, own], axis=1)

    def hidden_values(r, pair):
        slots = (2 * pair, 2 * pair + 1)
        hidden = {k: [None] * 8 for k in slots}
        masks = {}
        for k in slots:
            code = jnp.broadcast_to(codes[r, pl.ds(k, 1), :], (8, LANES))
            masks[k] = ((code & 1) != 0, (code & 2) != 0, (code & 4) != 0)
        for f in range(8):
            rows_f = pl.ds(8 * f, 8)
            w = [windows[r + 1 + dr, 1 + dc, rows_f, :] for dr, dc in WINDOWS]
            for k in slots:
                s = pl.ds(k * LANES, LANES)
                b0, b1, b2 = masks[k]
                low = jnp.where(b1, jnp.where(b0, w[3], w[2]), jnp.where(b0, w[1], w[0]))
                top = jnp.where(b1, jnp.where(b0, w[7], w[6]), jnp.where(b0, w[5], w[4]))
                pre = slope[r, rows_f, s] + jnp.where(b2, top, low)
                t = jnp.tanh(pre)
                u = 1.0 + t
                h = pre * u
                slope[r, rows_f, s] = u + h * (1.0 - t)
                hidden[k][f] = h
        s = pl.ds(pair * two, two)
        high, low = halves(
            jnp.concatenate([jnp.concatenate(hidden[k], axis=0) for k in slots], axis=1)
        )
        hs[r, :D, s] = high
        hs[r, D : 2 * D, s] = low
        hs[r, 2 * D :, s] = ones_two

    def hidden_product(r, pair):
        s = pl.ds(pair * two, two)
        both = mxu(
            packed_rows(pack, P_HIDDEN, 3 * D + 16),
            jnp.concatenate([hs[r, :, s], hs[r, :D, s]], axis=0),
        )
        cb[r, :, s] = both[:D]
        db[r, :, s] = both[D:]
        return r, pair, both[:D]

    def norm(r, pair, pair_c, total):
        for j in range(2):
            k = 2 * pair + j
            c = pair_c[:, j * LANES : (j + 1) * LANES]
            variance = jnp.sum(c * c, axis=0, keepdims=True) * (1.0 / D)
            inv = lax.rsqrt(variance + EPS)
            inverse[r, pl.ds(k, 1), :] = inv
            term = (inv * valid[r, pl.ds(k, 1), :]) * c
            total = term if total is None else total + term
        if pair == NBR // 2 - 1:
            summed[r] = total
            total = None
        return total

    def forward(i, _, first=0, last=2):
        turn = [4 * i + u for u in range(4)]
        if first == 0:
            for r in turn:
                waits(staged.at[r + 4], edge_sem.at[r + 4])
            for r in turn:
                shift(r + 6)
        units = [(r, pair) for r in turn for pair in range(NBR // 2)]
        products = []
        total = None
        if last >= 2:
            products.append(hidden_product(units[0][0] - 4, units[0][1]))
        for i_unit, (r, pair) in enumerate(units):
            if last >= 2 and i_unit + 1 < len(units):
                ahead_r, ahead_pair = units[i_unit + 1]
                products.append(hidden_product(ahead_r - 4, ahead_pair))
            if first <= 1 <= last:
                if pair == 0:
                    placed[r + 2] = jnp.zeros((3, D, LANES), F32)
                hidden_values(r, pair)
            if last >= 2:
                total = norm(*products[i_unit], total)
            if first == 0:
                edge_product(r + 4, pair)

    for ref in parts[0]:
        waits(ref, row_sem.at[0])
    for t in range(6):
        shift(t)
    for r in range(2):
        placed[r] = jnp.zeros((3, D, LANES), F32)
    for r in range(4):
        waits(staged.at[r], edge_sem.at[r])
        for pair in range(NBR // 2):
            edge_product(r, pair)
    node_inputs = load_rest()
    forward(0, None, last=1)
    for ref in parts[1]:
        waits(ref, row_sem.at[1])
    turns = rows // 4
    lax.fori_loop(1, turns - 1, forward, None)
    forward(turns - 1, None, first=1)
    forward(turns, None, first=2)

    for ref in (acc_edge, acc_hidden, acc_nin, acc_nout, acc_vec):
        ref[...] = jnp.zeros_like(ref)
    for ref in node_inputs:
        waits(ref, in_sem.at[1])
    chunk = 4
    span = chunk * LANES

    def node_chunk(first):
        tile_cols = lambda i: jnp.concatenate([columns[i]] * chunk, axis=1)
        spread = lambda ref, offset: jnp.concatenate(
            [ref[first + offset + j] for j in range(chunk)], axis=1
        )
        degree = jnp.concatenate(
            [jnp.sum(valid[first + j], axis=0, keepdims=True) for j in range(chunk)], axis=1
        )
        st_high, st_low = halves(spread(state, 1))
        sum_high, sum_low = halves(spread(summed, 0))
        place = lax.broadcasted_iota(jnp.int32, (16, span), 0)
        extra = jnp.where(place < 2, 1.0, jnp.where(place < 4, degree, 0.0)).astype(BF16)
        tops = jnp.concatenate([st_high, sum_high], axis=0)
        ends = jnp.concatenate([st_low, sum_low], axis=0)
        pre = mxu(
            jnp.concatenate(
                [
                    packed_rows(pack, P_NODE_IN, P_LANES),
                    packed_rows(pack, P_NODE_IN_END, 6 * D + 16 - P_LANES),
                ],
                axis=1,
            ),
            jnp.concatenate([tops, ends, extra, tops], axis=0),
        )
        yield
        t = jnp.tanh(pre)
        u = 1.0 + t
        h = pre * u
        slope_n = u + h * (1.0 - t)
        h_high, h_low = halves(h)
        h_all = jnp.concatenate([h_high, h_low, ones16[:, :span]], axis=0)
        c = mxu(
            packed_rows(pack, P_NODE_OUT, 3 * D + 16),
            jnp.concatenate([h_all, h_high], axis=0),
        )
        yield
        cot_c = jnp.concatenate(
            [read_row(cot.at[(first + j) // 8], (first + j) % 8) for j in range(chunk)], axis=1
        )
        inv = lax.rsqrt(jnp.sum(c * c, axis=0, keepdims=True) * (1.0 / D) + EPS)
        n = c * inv
        new = spread(state, 1) + (tile_cols(C_GAIN_N) * n + tile_cols(C_SHIFT_N))
        q = cot_c * tile_cols(C_GAIN_N)
        q = q - jnp.sum(q, axis=0, keepdims=True) * (1.0 / D)
        grad = inv * (q - n * (jnp.sum(q * n, axis=0, keepdims=True) * (1.0 / D)))
        g_high, g_low = halves(grad)
        pre_grad = mxu(
            packed_rows(pack, P_NODE_OUT_T), jnp.concatenate([g_high, g_low, g_high], axis=0)
        )
        for j in range(chunk):
            s = slice(j * LANES, (j + 1) * LANES)
            write_row(fresh.at[(first + j) // 8], (first + j) % 8, new[:, s])
            acc_vec[0] += cot_c[:, s] * n[:, s]
            acc_vec[1] += cot_c[:, s]
        yield
        acc_nout[...] += outer(jnp.concatenate([g_high, g_low], axis=0), h_all)
        pre_grad = pre_grad * slope_n
        p_high, p_low = halves(pre_grad)
        back = mxu(
            packed_rows(pack, P_NODE_IN_T), jnp.concatenate([p_high, p_low, p_high], axis=0)
        )
        for j in range(chunk):
            s = slice(j * LANES, (j + 1) * LANES)
            acc_vec[2] += pre_grad[:, s]
            acc_vec[3] += pre_grad[:, s] * degree[:, s]
        yield
        acc_nin[...] += outer(
            jnp.concatenate([p_high, p_low], axis=0), jnp.concatenate([tops, ends], axis=0)
        )
        for j in range(chunk):
            s = slice(j * LANES, (j + 1) * LANES)
            part[first + j] = cot_c[:, s] + back[:D, s]
            qc_ref[first + j] = back[D : 2 * D, s]
            qo_ref[first + j] = back[2 * D :, s]

    in_flight = []
    for first in range(0, rows + 4 * chunk, chunk):
        if first < rows:
            in_flight.append(node_chunk(first))
        for routine in list(in_flight):
            if next(routine, routine) is routine:
                in_flight.remove(routine)

    for g in range(rows // 8):
        pltpu.make_async_copy(
            fresh.at[g], new_states.at[:, pl.ds(8 * g, 8), :], out_sem
        ).start()
    pltpu.make_async_copy(part, part_out, out_sem).start()

    def grad_unit(r, pair, u, received):
        qc = qc_ref[r]
        qo = qo_ref[r]
        hidden_grads, grads = [], []
        for k in (2 * pair, 2 * pair + 1):
            s = pl.ds(k * LANES, LANES)
            c = cb[r, :, s]
            inv = inverse[r, pl.ds(k, 1), :]
            alpha = inv * valid[r, pl.ds(k, 1), :]
            moment = jnp.sum(qc * c, axis=0, keepdims=True) * (1.0 / D)
            beta = alpha * inv * inv * moment
            hidden_grads.append(alpha * qc - beta * c)
            grad = (alpha * qo - beta * db[r, :, s]) * slope[r, :, s]
            grads.append(grad)
            received = grad if received is None else received + grad
        high, low = halves(jnp.concatenate(hidden_grads, axis=1))
        s = pl.ds(pair * two, two)
        gather_grads[u, :D, s] = high
        gather_grads[u, D : 2 * D, s] = low
        high, low = halves(jnp.concatenate(grads, axis=1))
        gather_grads[u, 2 * D : 3 * D, s] = high
        gather_grads[u, 3 * D :, s] = low
        ge = mxu(
            packed_rows(pack, P_EDGE_T), jnp.concatenate([high, low, high], axis=0)
        )
        return grads, received, ge

    def place_unit(r, pair, grads):
        code = [
            jnp.broadcast_to(codes[r, pl.ds(k, 1), :], (8, LANES))
            for k in (2 * pair, 2 * pair + 1)
        ]
        for which, (dr, dc) in enumerate(WINDOWS):
            masks = [c == which for c in code]
            for f in range(8):
                rows_f = pl.ds(8 * f, 8)
                value = placed[r + 1 + dr, 1 + dc, rows_f, :]
                for j in range(2):
                    value += jnp.where(masks[j], grads[j][8 * f : 8 * f + 8], 0.0)
                placed[r + 1 + dr, 1 + dc, rows_f, :] = value

    def store_unit(r, pair, ge):
        staged[r, :, pl.ds(pair * two, two)] = ge

    def products(r, u):
        r = jnp.maximum(r, 0)
        acc_hidden[...] += outer(gather_grads[u, : 2 * D], hs[r])
        acc_edge[...] += outer(gather_grads[u, 2 * D :], xs[r])

    def settle(t):
        to_west = placed[t, 0]
        to_east = placed[t, 2]
        own[t] = (
            placed[t, 1]
            + jnp.where(lane == 0, 0.0, pltpu.roll(to_east, 1, 1))
            + jnp.where(lane == LANES - 1, 0.0, pltpu.roll(to_west, LANES - 1, 1))
        )
        mix = pltpu.roll(jnp.where(lane == 0, to_west, to_east), t, 1)
        cells[0] = jnp.where(lane == t, mix, cells[0])
        cells[1] = jnp.where(lane == lax.rem(t + LANES - 1, LANES), mix, cells[1])

    def send_rows(i, unroll=4):
        span = pl.ds(unroll * i, unroll)
        pltpu.make_async_copy(grad_recv.at[span], recv_out.at[span], out_sem).start()
        for u in range(unroll):
            r = unroll * i + u
            for k in range(NBR):
                pltpu.make_async_copy(
                    staged.at[r, :, pl.ds(k * LANES, LANES)],
                    grad_edges.at[:, k, r, :],
                    out_sem,
                ).start()

    def backward(i, _, unroll=4):
        if not isinstance(i, int):
            send_rows(i - 1)
            for u in range(unroll):
                settle(unroll * (i - 1) + u)
        pending = None
        for u in range(unroll):
            r = unroll * i + u
            products(r - unroll, u)
            received = None
            for pair in range(NBR // 2):
                grads, received, ge = grad_unit(r, pair, u, received)
                place_unit(r, pair, grads)
                if pending is not None:
                    store_unit(*pending)
                pending = (r, pair, ge)
            grad_recv[r] = received
        store_unit(*pending)
        if not isinstance(i, int):
            span = pl.ds(unroll * (i - 1), unroll)
            pltpu.make_async_copy(own.at[span], own_out.at[span], out_sem).start()

    cells[...] = jnp.zeros_like(cells)
    gather_grads[...] = jnp.zeros_like(gather_grads)
    backward(0, None)
    lax.fori_loop(1, rows // 4, backward, None)
    send_rows(rows // 4 - 1)
    for t in range(rows - 4, rows + 2):
        settle(t)
    tail = pl.ds(rows - 4, 6)
    pltpu.make_async_copy(own.at[tail], own_out.at[tail], out_sem).start()
    pltpu.make_async_copy(cells, cells_out, out_sem).start()
    for u in range(4):
        products(rows - 4 + u, u)

    def folded(ref):
        half = ref[:D, : 2 * D] + ref[D:, : 2 * D]
        return half + pltpu.roll(half, D, 1)

    left = lane < D
    acc[0] = folded(acc_edge)
    plain = (
        acc_nin[:D, : 2 * D]
        + acc_nin[D:, : 2 * D]
        + acc_nin[:D, 2 * D :]
        + acc_nin[D:, 2 * D :]
    )
    pick = lambda ref, start, i: jnp.sum(
        jnp.where(lane[:, :16] == i, ref[:D, start:] + ref[D:, start:], 0.0),
        axis=1,
        keepdims=True,
    )
    lane_sum = lambda i: jnp.sum(acc_vec[i], axis=1, keepdims=True)
    by_degree = lane_sum(3)
    acc[2] = plain * columns[C_ROWS, 0:1, :] + by_degree * columns[C_ROWS, 1:2, :]
    acc[3] = jnp.where(left, folded(acc_hidden), folded(acc_nout))
    weight_n = columns[C_WEIGHT_N]
    gain_row = jnp.sum(weight_n * plain, axis=0, keepdims=True)[:, D:]
    shift_row = jnp.sum(weight_n * by_degree, axis=0, keepdims=True)[:, D:]
    block = jnp.zeros((D, LANES), F32)
    for i, vector in (
        (1, pick(acc_hidden, 2 * D, 0)),
        (2, to_column(gain_row)),
        (3, to_column(shift_row)),
        (4, lane_sum(2)),
        (5, pick(acc_nout, 2 * D, 0)),
        (6, lane_sum(0)),
        (7, lane_sum(1)),
        (8, columns[C_DIVERGED]),
    ):
        block = jnp.where(lane == D + i, vector, block)
    acc[1] = block
    pltpu.make_async_copy(acc, acc_out, out_sem).start()
    for ref in (fresh, part, grad_recv, own.at[pl.ds(0, rows + 2)], cells, staged, acc):
        waits(ref, out_sem)


def layer_call(edges, cotangent, projected, receiver, sides, codes, valid, pack, columns, state):
    rows = cotangent.shape[1]
    wide = NBR * LANES
    tile = (D, LANES)
    shape = lambda *dims: jax.ShapeDtypeStruct(dims, F32)
    vmem = lambda *dims: pltpu.VMEM(dims, F32)
    return pl.pallas_call(
        layer_kernel,
        name="layer",
        out_shape=(
            shape(D, rows, LANES),
            shape(D, NBR, rows, LANES),
            shape(rows, *tile),
            shape(rows, *tile),
            shape(rows + 2, *tile),
            shape(2, *tile),
            shape(4, *tile),
        ),
        in_specs=[HBM] * 10,
        out_specs=[HBM] * 7,
        scratch_shapes=[
            vmem(rows, D, wide),
            pltpu.VMEM((rows, 2 * D, wide), BF16),
            pltpu.VMEM((rows, 2 * D + 16, wide), BF16),
            vmem(rows, D, wide),
            vmem(rows, D, wide),
            vmem(rows, D, wide),
            vmem(rows + 6, 3, *tile),
            vmem(rows + 6, *tile),
            vmem(rows, *tile),
            vmem(2, *tile),
            pltpu.VMEM((rows, 8, LANES), jnp.int32),
            vmem(rows, 8, LANES),
            pltpu.VMEM((P_ROWS, P_LANES), BF16),
            vmem(C_TILES, *tile),
            vmem(rows + 2, *tile),
            vmem(rows, 8, LANES),
            vmem(rows, *tile),
            vmem(rows, *tile),
            vmem(rows, *tile),
            vmem(rows // 8, D, 8, LANES),
            vmem(rows // 8, D, 8, LANES),
            vmem(rows + 2, 3, *tile),
            vmem(2, *tile),
            pltpu.VMEM((4, 4 * D, wide), BF16),
            vmem(2 * D, 2 * D),
            vmem(2 * D, 2 * D + 16),
            vmem(2 * D, 4 * D),
            vmem(2 * D, 2 * D + 16),
            vmem(4, *tile),
            vmem(4, *tile),
            pltpu.SemaphoreType.DMA((2,)),
            pltpu.SemaphoreType.DMA((rows,)),
            pltpu.SemaphoreType.DMA((2,)),
            pltpu.SemaphoreType.DMA,
        ],
        compiler_params=pltpu.CompilerParams(vmem_limit_bytes=ROOM),
    )(edges, cotangent, projected, receiver, sides, codes, valid, pack, columns, state)


def sum_kernel(
    n_blk,
    n_lon,
    acc_in,
    own_in,
    cells_in,
    recv_in,
    part_in,
    state_in,
    cols_all,
    pack_in,
    columns_in,
    mean,
    logstd,
    noise,
    nodes_out,
    mean_out,
    logstd_out,
    total_out,
    acc,
    own,
    cells,
    grad_recv,
    part,
    natural,
    mean_v,
    logstd_v,
    noise_v,
    inside,
    state,
    cols,
    pack,
    edge_rows,
    edge_cols,
    edge_corners,
    rows_in,
    cols_in,
    corners_in,
    acc_send,
    acc_recv,
    packed,
    scattered,
    across,
    gathered,
    in_sem,
    row_sem,
    rs_send,
    rs_recv,
    x_send,
    x_recv,
    ag_send,
    ag_recv,
    halo_send,
    halo_recv,
    latent_sem,
    out_sem,
):
    rows = recv_in.shape[0]
    blk, lon, around = neighbours(n_blk, n_lon)
    size = scattered.shape[0]
    n_groups = across.shape[0]
    per = size // n_lon
    me = lax.rem(blk, per) * n_lon + lon
    own_group = blk // per
    lane = lane_ids()

    def member(index):
        if n_lon & (n_lon - 1):
            return (own_group * per + index // n_lon, lax.rem(index, n_lon))
        return (own_group * per + (index >> (n_lon.bit_length() - 1)), index & (n_lon - 1))

    def other(step):
        if size & (size - 1):
            return lax.rem(me + step, size)
        return (me + step) & (size - 1)

    def peer(step):
        return (lax.rem(own_group + step, n_groups) * per + lax.rem(blk, per), lon)

    half = rows // 2
    for h in range(2):
        span = pl.ds(h * half, half)
        span3 = pl.ds(0, half + 1) if h == 0 else pl.ds(half + 1, half + 1)
        for source, target in (
            (own_in.at[span3], own.at[span3]),
            (state_in.at[span3], state.at[span3]),
            (recv_in.at[span], grad_recv.at[span]),
        ):
            pltpu.make_async_copy(source, target, row_sem.at[h]).start()
    small = (
        (pack_in.at[pl.ds(P_SEND_T[0], 2 * D)], pack),
        (cols_all, cols),
        (acc_in, acc),
        (part_in, part),
        (cells_in, cells),
        (columns_in.at[C_VALID], inside),
    )
    for i, (source, target) in enumerate(small):
        pltpu.make_async_copy(source, target, in_sem.at[i]).start()

    groups = [pl.ds(8 * g, 8) for g in range(rows // 8)]
    latent = ((mean, mean_v), (logstd, logstd_v), (noise, noise_v))
    barrier = pltpu.get_barrier_semaphore()

    def greet(step, _):
        pl.semaphore_signal(
            barrier, inc=1, device_id=member(other(step)), device_id_type=MESH
        )

    lax.fori_loop(1, size, greet, None)
    expected = size - 1
    if n_groups > 1:
        for place in around:
            pl.semaphore_signal(barrier, inc=1, device_id=place, device_id_type=MESH)

        def greet_group(step, _):
            pl.semaphore_signal(barrier, inc=1, device_id=peer(step), device_id_type=MESH)

        lax.fori_loop(1, n_groups, greet_group, None)
        expected += 8 + n_groups - 1

    acc_send[...] = jnp.zeros_like(acc_send)
    acc_recv[...] = jnp.zeros_like(acc_recv)

    def both_halves(value):
        return jnp.concatenate(halves(value), axis=0)

    ones_row = jnp.where(
        lax.broadcasted_iota(jnp.int32, (16, 4 * LANES), 0) < 1, 1.0, 0.0
    ).astype(BF16)

    def collect(i, _):
        wide = lambda ref, first: both_halves(
            jnp.concatenate([ref[first + u] for u in range(4)], axis=1)
        )
        there = wide(state, 1 + 4 * i)
        acc_send[...] += outer(wide(own, 1 + 4 * i), there)
        acc_recv[...] += outer(
            wide(grad_recv, 4 * i), jnp.concatenate([there, ones_row], axis=0)
        )

    for h in range(2):
        waits(own.at[pl.ds(h * (half + 1), half + 1)], row_sem.at[h])
        waits(state.at[pl.ds(h * (half + 1), half + 1)], row_sem.at[h])
        waits(grad_recv.at[pl.ds(h * half, half)], row_sem.at[h])
        lax.fori_loop(h * half // 4, (h + 1) * half // 4, collect, None)
    waits(cells, in_sem.at[4])
    waits(cols, in_sem.at[1])
    edge_values = jnp.concatenate([own[0], own[rows + 1], cells[0], cells[1]], axis=1)
    edge_states = jnp.concatenate([state[0], state[rows + 1], cols[0], cols[1]], axis=1)
    acc_send[...] += outer(both_halves(edge_values), both_halves(edge_states))

    def folded(ref):
        part_sum = ref[:D, : 2 * D] + ref[D:, : 2 * D]
        return part_sum + pltpu.roll(part_sum, D, 1)

    left = lane < D
    waits(acc, in_sem.at[2])
    ones_sum = jnp.sum(
        jnp.where(lane[:, :16] == 0, acc_recv[:D, 2 * D :] + acc_recv[D:, 2 * D :], 0.0),
        axis=1,
        keepdims=True,
    )
    columns_t = jnp.where(lane == D, ones_sum, acc[1]).T[D:]
    vector_rows = jnp.concatenate([jnp.zeros((D, D), F32), columns_t], axis=1)
    chunk = packed.shape[1]
    blocks = (
        jnp.where(left, acc[0], folded(acc_send)),
        jnp.where(left, folded(acc_recv), vector_rows),
        acc[2],
        acc[3],
    )
    per_block = D // chunk
    for i, block in enumerate(blocks):
        for j in range(per_block):
            packed[i * per_block + j] = block[j * chunk : (j + 1) * chunk]
    for g, span in enumerate(groups):
        for source, target in latent:
            pltpu.make_async_copy(source.at[:, span, :], target.at[g], latent_sem).start()

    pl.semaphore_wait(barrier, expected)

    def scatter(step, _):
        target = other(step)
        pltpu.make_async_remote_copy(
            src_ref=packed.at[target],
            dst_ref=scattered.at[me],
            send_sem=rs_send,
            recv_sem=rs_recv,
            device_id=member(target),
            device_id_type=MESH,
        ).start()

    lax.fori_loop(1, size, scatter, None)
    scattered[me] = packed[me]

    waits(pack, in_sem.at[0])
    a_send = pack[:D, : 3 * D]
    a_recv = pack[D : 2 * D, : 3 * D]
    high, low = halves(edge_values)
    edge_grads = mxu(a_send, jnp.concatenate([high, low, high], axis=0))
    edge_grad = [edge_grads[:, i * LANES : (i + 1) * LANES] for i in range(4)]
    edge_rows[0], edge_rows[1] = edge_grad[0], edge_grad[1]
    west_cells, east_cells = edge_grad[2], edge_grad[3]
    edge_cols[0], edge_cols[1] = pack_column(west_cells), pack_column(east_cells)
    edge_corners[...] = corner_rows(
        [
            west_cells[:, :1],
            east_cells[:, LANES - 1 :],
            west_cells[:, rows + 1 : rows + 2],
            east_cells[:, rows : rows + 1],
        ]
    )
    copies = rim_copies(
        around,
        edge_rows,
        edge_cols,
        edge_corners,
        rows_in,
        cols_in,
        corners_in,
        halo_send,
        halo_recv,
    )
    for copy in copies:
        copy.start()
    waits(part, in_sem.at[3])

    def finish(i, _):
        for u in range(2):
            first = 4 * i + 2 * u
            grads = None
            for weights, ref, offset in ((a_send, own, 1), (a_recv, grad_recv, 0)):
                high, low = halves(
                    jnp.concatenate([ref[first + offset], ref[first + offset + 1]], axis=1)
                )
                product = mxu(weights, jnp.concatenate([high, low, high], axis=0))
                grads = product if grads is None else grads + product
            for j in range(2):
                part[first + j] += grads[:, j * LANES : (j + 1) * LANES]

    lax.fori_loop(0, rows // 4, finish, None)

    waits(inside, in_sem.at[5])
    for _, target in latent:
        waits(target, latent_sem)
    weight = inside[0:1, :].reshape(1, 1, LANES)

    def blocks(i):
        return i // 8, pl.ds(8 * (i % 8), 8)

    def latent_terms(i, _):
        at = blocks(i)
        spread = jnp.exp(logstd_v[at])
        mean_v[at] = weight * mean_v[at]
        noise_v[at] = spread * noise_v[at]
        logstd_v[at] = weight * (spread * spread - 1.0)

    lax.fori_loop(0, rows, latent_terms, None)

    others = pl.ds(0, size - 1)
    waits(scattered.at[others], rs_recv)
    mine = scattered[0]
    for i in range(1, size):
        mine = mine + scattered[i]
    if n_groups > 1:
        across[own_group] = mine

        def cross(step, _):
            pltpu.make_async_remote_copy(
                src_ref=across.at[own_group],
                dst_ref=across.at[own_group],
                send_sem=x_send,
                recv_sem=x_recv,
                device_id=peer(step),
                device_id_type=MESH,
            ).start()

        lax.fori_loop(1, n_groups, cross, None)
        rest = pl.ds(0, n_groups - 1)
        waits(across.at[rest], x_recv)
        waits(across.at[rest], x_send)
        mine = across[0]
        for i in range(1, n_groups):
            mine = mine + across[i]
    gathered[me] = mine

    def gather(step, _):
        pltpu.make_async_remote_copy(
            src_ref=gathered.at[me],
            dst_ref=gathered.at[me],
            send_sem=ag_send,
            recv_sem=ag_recv,
            device_id=member(other(step)),
            device_id_type=MESH,
        ).start()

    lax.fori_loop(1, size, gather, None)
    for copy in copies:
        copy.wait()
    west_in = (
        pltpu.roll(jnp.where(lane < rows, unpack_column(cols_in[1]), 0.0), 1, 1)
        + corner_at(corners_in.at[3], 3, 1)
        + corner_at(corners_in.at[1], 1, rows)
    )
    east_in = unpack_column(cols_in[0])
    east_in = (
        pltpu.roll(jnp.where((lane >= 1) & (lane <= rows), east_in, 0.0), LANES - 1, 1)
        + corner_at(corners_in.at[2], 2, 0)
        + corner_at(corners_in.at[0], 0, rows - 1)
    )
    rim = (lane == 0) | (lane == LANES - 1)
    part[0] += rows_in[1]
    part[rows - 1] += rows_in[0]

    def add_columns(i, _):
        for u in range(4):
            r = 4 * i + u
            mix = pltpu.roll(
                jnp.where(lane == r + 1, west_in, east_in), LANES - 1 - r, 1
            )
            write_row(natural.at[r // 8], lax.rem(r, 8), part[r] + jnp.where(rim, mix, 0.0))

    lax.fori_loop(0, rows // 4, add_columns, None)

    def latent_grads(i, _):
        at = blocks(i)
        grad = natural[at]
        mean_v[at] = grad + mean_v[at]
        logstd_v[at] = grad * noise_v[at] + logstd_v[at]

    lax.fori_loop(0, rows, latent_grads, None)
    results = ((natural, nodes_out), (mean_v, mean_out), (logstd_v, logstd_out))
    for g, span in enumerate(groups):
        for source, target in results:
            pltpu.make_async_copy(source.at[g], target.at[:, span, :], out_sem).start()
    waits(gathered.at[others], ag_recv)
    pltpu.make_async_copy(gathered, total_out, out_sem).start()
    waits(scattered.at[others], rs_send)
    waits(gathered.at[others], ag_send)
    for ref in (natural, mean_v, logstd_v, gathered):
        waits(ref, out_sem)


def sum_call(n_blk, n_lon, *operands):
    recv = operands[3]
    rows = recv.shape[0]
    size = min(32, n_blk * n_lon)
    n_groups = n_blk * n_lon // size
    chunk = (4 * D // size, LANES)
    tile = (D, LANES)
    shape = lambda *dims: jax.ShapeDtypeStruct(dims, F32)
    vmem = lambda *dims: pltpu.VMEM(dims, F32)
    dma = pltpu.SemaphoreType.DMA
    return pl.pallas_call(
        functools.partial(sum_kernel, n_blk, n_lon),
        name="sums",
        out_shape=(shape(D, rows, LANES),) * 3 + (shape(size, *chunk),),
        in_specs=[HBM] * 12,
        out_specs=[HBM] * 4,
        scratch_shapes=[
            vmem(4, *tile),
            vmem(rows + 2, *tile),
            vmem(2, *tile),
            vmem(rows, *tile),
            vmem(rows, *tile),
            vmem(rows // 8, D, 8, LANES),
            vmem(rows // 8, D, 8, LANES),
            vmem(rows // 8, D, 8, LANES),
            vmem(rows // 8, D, 8, LANES),
            vmem(*tile),
            vmem(rows + 2, *tile),
            vmem(2, *tile),
            pltpu.VMEM((2 * D, P_LANES), BF16),
            vmem(2, *tile),
            vmem(2, D // 2, LANES),
            vmem(8, LANES),
            vmem(2, *tile),
            vmem(2, D // 2, LANES),
            vmem(4, 8, LANES),
            vmem(2 * D, 2 * D),
            vmem(2 * D, 2 * D + 16),
            vmem(size, *chunk),
            vmem(size, *chunk),
            vmem(n_groups, *chunk),
            vmem(size, *chunk),
            dma((6,)),
            dma((2,)),
            dma,
            dma,
            dma,
            dma,
            dma,
            dma,
            dma((8,)),
            dma((8,)),
            dma,
            dma,
        ],
        compiler_params=pltpu.CompilerParams(
            collective_id=1, has_side_effects=True, vmem_limit_bytes=ROOM
        ),
    )(*operands)


def final_kernel(*refs):
    large_in, (total_in, columns_in), refs = refs[:3], refs[3:5], refs[5:]
    large_outs, small_outs, refs = refs[:3], refs[3:16], refs[16:]
    large, (total, columns), smalls, refs = refs[:3], refs[3:5], refs[5:18], refs[18:]
    in_sem, small_sem, out_sem = refs
    n_chunks = in_sem.shape[0]
    depth = D // n_chunks
    for i, (source, target) in enumerate(((columns_in, columns), (total_in, total))):
        pltpu.make_async_copy(source, target, small_sem.at[i]).start()
    spans = [pl.ds(i * depth, depth) for i in range(n_chunks)]
    for i, span in enumerate(spans):
        for source, target in zip(large_in, large):
            pltpu.make_async_copy(source.at[span], target.at[span], in_sem.at[i]).start()

    def forward_block(i):
        for ref in large:
            waits(ref.at[spans[i]], in_sem.at[i])
        for source, target in zip(large, large_outs):
            pltpu.make_async_copy(source.at[spans[i]], target.at[spans[i]], out_sem).start()

    for i in range(n_chunks):
        forward_block(i)

    waits(columns, small_sem.at[0])
    waits(total, small_sem.at[1])
    kl_value, g_w_ei, g_w_eo, g_w_ni, g_w_no = smalls[:5]
    chunk = total.shape[1]
    per_block = D // chunk
    blocks = [
        jnp.concatenate([total[i * per_block + j] for j in range(per_block)], axis=0)
        for i in range(4)
    ]
    g_w_ei[:, : 2 * D] = blocks[0]
    g_w_ei[:, 2 * D :] = blocks[1][:, :D]
    g_w_ni[...] = blocks[2]
    g_w_eo[...] = blocks[3][:, :D]
    g_w_no[...] = pltpu.roll(blocks[3], D, 1)[:, :D]
    vector_rows = pltpu.roll(blocks[1][:16], D, 1)
    for i in range(8):
        smalls[5 + i][...] = vector_rows[i : i + 1, :D]
    diverged = jnp.sum(vector_rows[8:9, :D], axis=1, keepdims=True)
    kl_value[...] = diverged / columns[C_COUNT, 0:1, 0:1]
    for source, target in zip(smalls, small_outs):
        pltpu.make_async_copy(source, target, out_sem).start()
    for ref in (*large, *smalls):
        waits(ref, out_sem)


def final_call(*operands):
    shape = lambda *dims: jax.ShapeDtypeStruct(dims, F32)
    vmem = lambda *dims: pltpu.VMEM(dims, F32)
    whole, total = operands[0].shape, operands[3].shape
    small = ((1, 1), (D, 3 * D), (D, D), (D, 2 * D), (D, D)) + ((1, D),) * 8
    return pl.pallas_call(
        final_kernel,
        name="final",
        out_shape=[shape(*dims) for dims in (whole,) * 3 + small],
        in_specs=[HBM] * 5,
        out_specs=[HBM] * 16,
        scratch_shapes=[vmem(*whole) for _ in range(3)]
        + [vmem(*total), vmem(C_TILES, D, LANES)]
        + [vmem(*dims) for dims in small]
        + [
            pltpu.SemaphoreType.DMA((4,)),
            pltpu.SemaphoreType.DMA((2,)),
            pltpu.SemaphoreType.DMA,
        ],
        compiler_params=pltpu.CompilerParams(vmem_limit_bytes=ROOM),
    )(*operands)


def shards(
    nodes,
    edges,
    latent_mean,
    latent_logstd,
    latent_noise,
    kl_weight,
    band_counts,
    neighbors,
    edge_mask,
    w_edge_in,
    b_edge_in,
    w_edge_out,
    b_edge_out,
    edge_gain,
    edge_shift,
    w_node_in,
    b_node_in,
    w_node_out,
    b_node_out,
    node_gain,
    node_shift,
    cotangent,
):
    n_blk = lax.axis_size("blk")
    n_lon = lax.axis_size("lon")
    vectors = (
        b_edge_in,
        b_edge_out,
        edge_gain,
        edge_shift,
        b_node_in,
        b_node_out,
        node_gain,
        node_shift,
    )
    weights = (w_edge_in, w_edge_out, w_node_in, w_node_out)
    weights += tuple(vector.reshape(1, D) for vector in vectors)
    state, cols, projected, receiver, sides, codes, valid, pack, columns = start_call(
        n_blk,
        n_lon,
        band_counts,
        kl_weight,
        nodes,
        latent_mean,
        latent_logstd,
        latent_noise,
        neighbors,
        edge_mask,
        weights,
    )
    new_states, grad_edges, part, recv, own, cells, acc = layer_call(
        edges, cotangent, projected, receiver, sides, codes, valid, pack, columns, state
    )
    grads = sum_call(
        n_blk,
        n_lon,
        acc,
        own,
        cells,
        recv,
        part,
        state,
        cols,
        pack,
        columns,
        latent_mean,
        latent_logstd,
        latent_noise,
    )
    grad_nodes, grad_mean, grad_logstd, kl_value, g_w_ei, g_w_eo, g_w_ni, g_w_no, *g_vec = (
        final_call(*grads, columns)
    )
    g_vec = [vector.reshape(D) for vector in g_vec]
    return (
        new_states,
        kl_value.reshape(1),
        grad_nodes,
        grad_edges,
        grad_mean,
        grad_logstd,
        g_w_ei,
        g_vec[0],
        g_w_eo,
        g_vec[1],
        g_vec[2],
        g_vec[3],
        g_w_ni,
        g_vec[4],
        g_w_no,
        g_vec[5],
        g_vec[6],
        g_vec[7],
    )


def solution(mesh):
    node = P(None, "blk", "lon")
    slot = P(None, None, "blk", "lon")
    return jax.shard_map(
        shards,
        mesh=mesh,
        in_specs=(
            (node, slot, node, node, node, P(), P(), node, node) + (P(),) * 12 + (node,)
        ),
        out_specs=(node, P(), node, slot, node, node) + (P(),) * 12,
        check_vma=False,
    )
```

```python
import functools

import jax
import jax.numpy as jnp
from jax import lax
from jax.experimental import pallas as pl
from jax.experimental.pallas import tpu as pltpu
from jax.sharding import PartitionSpec as P

F32 = jnp.float32
BF16 = jnp.bfloat16
MESH = pl.DeviceIdType.MESH
D = 64
LANES = 128
NBR = 6
EPS = 1e-05
HBM = pl.BlockSpec(memory_space=pltpu.HBM)
VMEM = pl.BlockSpec(memory_space=pltpu.VMEM)
ROOM = 62 * 2**20
SMEM = pl.BlockSpec(memory_space=pltpu.SMEM)

WINDOWS = ((-1, -1), (-1, 0), (-1, 1), (0, -1), (0, 1), (1, -1), (1, 0), (1, 1))


def halves(value):
    high = value.astype(BF16)
    return high, (value - high.astype(F32)).astype(BF16)


def weight_pack(weight, *biases):
    high, low = halves(weight)
    if not biases:
        return jnp.concatenate([high, high, low], axis=1)
    place = lax.broadcasted_iota(jnp.int32, (weight.shape[0], 16), 1)
    wide = jnp.zeros((weight.shape[0], 16), F32)
    for i, bias in enumerate(biases):
        for j, part in enumerate(halves(bias)):
            wide = jnp.where(place == 2 * i + j, part.astype(F32), wide)
    return jnp.concatenate([high, high, wide.astype(BF16), low], axis=1)


def mxu(left, right):
    return jnp.dot(left, right, preferred_element_type=F32)


def outer(left, right):
    return lax.dot_general(
        left, right, (((1,), (1,)), ((), ())), preferred_element_type=F32
    )


def exact(left, right, dims):
    return lax.dot_general(
        left,
        right,
        (dims, ((), ())),
        precision=lax.Precision.HIGHEST,
        preferred_element_type=F32,
    )


def eye():
    return lax.broadcasted_iota(jnp.int32, (D, D), 0) == lax.broadcasted_iota(
        jnp.int32, (D, D), 1
    )


def to_column(row):
    return jnp.sum(jnp.where(eye(), row, 0.0), axis=1, keepdims=True)


def to_row(column):
    return jnp.sum(jnp.where(eye(), column, 0.0), axis=0, keepdims=True)


def waits(ref, sem):
    pltpu.make_async_copy(ref, ref, sem).wait()


def in_turn(*routines):
    waiting = list(routines)
    while waiting:
        for routine in list(waiting):
            if next(routine, routine) is routine:
                waiting.remove(routine)


def lane_ids(rows=D):
    return lax.broadcasted_iota(jnp.int32, (rows, LANES), 1)


P_HIDDEN, P_EDGE, P_EDGE_T, P_NODE_OUT = (0, 128), (128, 192), (192, 256), (256, 320)
P_NODE_OUT_T, P_NODE_IN_T, P_SEND_T, P_RECV_T = (320, 384), (384, 576), (576, 640), (640, 704)
P_NODE_IN, P_NODE_IN_END = (704, 768), (768, 832)
P_ROWS, P_LANES = 832, 256
C_GAIN_N, C_SHIFT_N, C_VALID, C_DIVERGED, C_COUNT, C_WEIGHT_N, C_ROWS = range(7)
C_TILES = 7


def packed_rows(ref, rows, lanes=3 * D):
    return ref[rows[0] : rows[1], :lanes]


def row_of(ref, row, step, count=D):
    flat = ref.reshape(count * step, LANES)
    return flat, pl.ds(row, count, stride=step)


def read_row(ref, row, step=8):
    flat, place = row_of(ref, row, step)
    return flat[place, :]


def write_row(ref, row, value, step=8):
    flat, place = row_of(ref, row, step)
    flat[place, :] = value


def pack_column(tile):
    return jnp.where(lane_ids(D // 2) < D, tile[: D // 2], pltpu.roll(tile[D // 2 :], D, 1))


def unpack_column(tile):
    return jnp.concatenate([tile, pltpu.roll(tile, D, 1)], axis=0)


def corner_rows(columns):
    rows = [to_row(column) for column in columns]
    wide = jnp.concatenate(rows + [jnp.zeros((4, D), F32)], axis=0)
    return jnp.concatenate([wide, jnp.zeros((8, D), F32)], axis=1)


def corner_at(ref, row, lane):
    return jnp.where(lane_ids() == lane, to_column(ref[row : row + 1, :D]), 0.0)


def rim_copies(around, rows, columns, corners, rows_in, columns_in, corners_in, send, recv):
    pairs = [(rows.at[0], rows_in.at[0]), (rows.at[1], rows_in.at[1])]
    pairs += [(columns.at[0], columns_in.at[0]), (columns.at[1], columns_in.at[1])]
    pairs += [(corners, corners_in.at[i]) for i in range(4)]
    return [
        pltpu.make_async_remote_copy(
            src_ref=source,
            dst_ref=target,
            send_sem=send.at[slot],
            recv_sem=recv.at[slot],
            device_id=place,
            device_id_type=MESH,
        )
        for slot, (place, (source, target)) in enumerate(zip(around, pairs))
    ]


def neighbours(n_blk, n_lon):
    blk = lax.axis_index("blk")
    lon = lax.axis_index("lon")
    up = lax.rem(blk + n_blk - 1, n_blk)
    down = lax.rem(blk + 1, n_blk)
    west = lax.rem(lon + n_lon - 1, n_lon)
    east = lax.rem(lon + 1, n_lon)
    around = (
        (up, lon),
        (down, lon),
        (blk, west),
        (blk, east),
        (up, west),
        (up, east),
        (down, west),
        (down, east),
    )
    return blk, lon, around


def start_kernel(
    n_blk,
    n_lon,
    counts,
    kl_weight,
    nodes,
    mean,
    logstd,
    noise,
    neighbors,
    edge_mask,
    w_ei,
    w_eo,
    w_ni,
    w_no,
    *rest,
):
    vectors = rest[:8]
    (
        state_out,
        cols_out,
        project_out,
        receive_out,
        sides_out,
        codes_out,
        valid_out,
        pack_out,
        columns_out,
        buf,
        state,
        projected,
        receiver,
        sides,
        nb,
        mk,
        codes,
        valid,
        v_ei,
        v_eo,
        v_ni,
        v_no,
        v_vec,
        pack,
        columns,
        cols,
        edge_rows,
        edge_cols,
        edge_corners,
        rows_in,
        cols_in,
        corners_in,
        in_sem,
        slot_sem,
        weight_sem,
        send_sem,
        recv_sem,
        out_sem,
    ) = rest[8:]
    rows = nodes.shape[1]
    blk, lon, around = neighbours(n_blk, n_lon)
    barrier = pltpu.get_barrier_semaphore()
    for place in around:
        pl.semaphore_signal(barrier, inc=1, device_id=place, device_id_type=MESH)

    n_groups = in_sem.shape[0]
    group = rows // n_groups
    for g in range(n_groups):
        for which, source in enumerate((nodes, mean, logstd, noise)):
            pltpu.make_async_copy(
                source.at[:, pl.ds(g * group, group), :], buf.at[g, which], in_sem.at[g]
            ).start()
    weights = [(w_ei, v_ei), (w_eo, v_eo), (w_ni, v_ni), (w_no, v_no)]
    weights += [(vectors[i], v_vec.at[i]) for i in range(8)]
    lane = lane_ids()
    count = counts[blk]
    inside = lane < count

    def state_row(g, j, carry):
        total, west_tile, east_tile = carry
        r = g * group + j
        node_r, mean_r, logstd_r, noise_r = [
            read_row(buf.at[g, which], j, group) for which in range(4)
        ]
        spread = jnp.exp(logstd_r)
        value = node_r + mean_r + spread * noise_r
        state[r + 1] = value
        total += jnp.where(inside, mean_r * mean_r + spread * spread - 2.0 * logstd_r, 0.0)
        moved = pltpu.roll(value, r + 1, 1)
        west_tile = jnp.where(lane == r + 1, moved, west_tile)
        east_tile = jnp.where(lane == r, moved, east_tile)
        return total, west_tile, east_tile

    carry = (jnp.zeros((D, LANES), F32),) * 3
    for source, target in weights:
        pltpu.make_async_copy(source, target, weight_sem).start()

    def state_group(g, carry):
        waits(buf.at[g], in_sem.at[g])
        for j in range(0, group, 2):
            carry = state_row(g, j + 1, state_row(g, j, carry))
        return carry

    carry = lax.fori_loop(0, n_groups, state_group, carry)
    total, west_tile, east_tile = carry
    edge_rows[0] = state[1]
    edge_rows[1] = state[rows]
    edge_cols[0] = pack_column(west_tile)
    edge_cols[1] = pack_column(east_tile)
    edge_corners[...] = corner_rows(
        [
            state[row][:, lane0 : lane0 + 1]
            for row in (1, rows)
            for lane0 in (0, LANES - 1)
        ]
    )

    pl.semaphore_wait(barrier, 8)
    copies = rim_copies(
        around,
        edge_rows,
        edge_cols,
        edge_corners,
        rows_in,
        cols_in,
        corners_in,
        send_sem,
        recv_sem,
    )
    for copy in copies:
        copy.start()
    pltpu.make_async_copy(neighbors, nb, slot_sem).start()
    pltpu.make_async_copy(edge_mask, mk, slot_sem).start()
    inner = pl.ds(1, rows)
    pltpu.make_async_copy(state.at[inner], state_out.at[inner], out_sem).start()

    for _, target in weights:
        waits(target, weight_sem)
    b_ei, b_eo, gain_e, shift_e, b_ni, b_no, gain_n, shift_n = [
        to_column(v_vec[i]) for i in range(8)
    ]
    n_valid = counts[0]
    for i in range(1, counts.shape[0]):
        n_valid += counts[i]
    for i, column in (
        (C_GAIN_N, gain_n),
        (C_SHIFT_N, shift_n),
        (C_VALID, jnp.where(inside, kl_weight[0], 0.0)),
        (C_COUNT, jnp.full((D, LANES), (D * rows * n_lon * n_valid).astype(F32))),
        (
            C_DIVERGED,
            0.5 * jnp.sum(total - rows * jnp.where(inside, 1.0, 0.0), axis=1, keepdims=True),
        ),
    ):
        columns[i] = jnp.broadcast_to(column, (D, LANES))
    w_in = v_ei[...]
    w_e, w_s, w_r = w_in[:, :D], w_in[:, D : 2 * D], w_in[:, 2 * D :]
    a_state = jnp.concatenate([weight_pack(0.5 * w_s), weight_pack(0.5 * w_r)], axis=0)
    w_o = v_eo[...]
    w_oc = w_o - jnp.mean(w_o, axis=0, keepdims=True)
    b_oc = b_eo - jnp.mean(b_eo, axis=0, keepdims=True)
    back = 0.5 * exact(w_o, w_oc, ((0,), (0,)))
    b_back = 0.5 * exact(w_o, b_oc, ((0,), (0,)))
    w_n = v_ni[...]
    w_nt = w_n.T
    gain_row, shift_row = v_vec[2], v_vec[3]
    one_row = jnp.ones_like(gain_row)
    scale_row = jnp.concatenate([one_row, gain_row], axis=1)
    add_row = jnp.concatenate([0.0 * one_row, shift_row], axis=1)
    columns[C_WEIGHT_N] = w_n
    row_id = lax.broadcasted_iota(jnp.int32, (D, LANES), 0)
    columns[C_ROWS] = jnp.where(row_id == 0, scale_row, jnp.where(row_id == 1, add_row, 0.0))
    w_shift = jnp.sum(w_n * add_row, axis=1, keepdims=True)
    w_out = v_no[...]
    scaled = gain_e * w_nt[D:]
    scaled = scaled - jnp.mean(scaled, axis=0, keepdims=True)

    def put(place, *parts):
        value = jnp.concatenate(parts, axis=0) if len(parts) > 1 else parts[0]
        pack[place[0] : place[1], : value.shape[1]] = value

    put(P_EDGE, weight_pack(0.5 * w_e))
    put(P_HIDDEN, weight_pack(w_oc, b_oc), weight_pack(back, b_back))
    put(P_EDGE_T, weight_pack(w_e.T))
    put(P_SEND_T, weight_pack(w_s.T))
    put(P_RECV_T, weight_pack(w_r.T))
    node_in = weight_pack(0.5 * w_n * scale_row, 0.5 * b_ni, 0.5 * w_shift)
    put(P_NODE_IN, node_in[:, :P_LANES])
    put(P_NODE_IN_END, node_in[:, P_LANES:])
    put(
        P_NODE_OUT,
        weight_pack(
            w_out - jnp.mean(w_out, axis=0, keepdims=True),
            b_no - jnp.mean(b_no, axis=0, keepdims=True),
        ),
    )
    put(P_NODE_OUT_T, weight_pack(0.5 * w_out.T))
    put(
        P_NODE_IN_T,
        weight_pack(w_nt[:D]),
        weight_pack(scaled),
        weight_pack(0.5 * exact(w_o, scaled, ((0,), (0,)))),
    )
    pltpu.make_async_copy(pack, pack_out, out_sem).start()
    pltpu.make_async_copy(columns, columns_out, out_sem).start()

    waits(nb, slot_sem)
    waits(mk, slot_sem)
    before = counts[lax.rem(blk + n_blk - 1, n_blk)]
    after = counts[lax.rem(blk + 1, n_blk)]
    row_id = lax.broadcasted_iota(jnp.int32, (rows, LANES), 0)
    col_id = lax.broadcasted_iota(jnp.int32, (rows, LANES), 1)
    above = jnp.where(row_id == 0, before, count)
    below = jnp.where(row_id == rows - 1, after, count)
    for k in range(NBR):
        delta = nb[k] - (row_id * (LANES + 2) + col_id)
        first = delta < LANES + 2
        middle = delta < 2 * (LANES + 2)
        step = jnp.where(
            first, delta, jnp.where(middle, delta - (LANES + 2), delta - 2 * (LANES + 2))
        )
        codes[k] = jnp.where(first, step, jnp.where(middle, 3 + (step >> 1), 5 + step))
        owner = col_id + step - 1
        owner = jnp.where(owner < 0, LANES - 1, jnp.where(owner >= LANES, 0, owner))
        limit = jnp.where(first, above, jnp.where(middle, count, below))
        valid[k] = jnp.where((col_id < count) & (owner < limit), mk[k].astype(F32), 0.0)
    for k in range(NBR, 8):
        codes[k] = jnp.zeros((rows, LANES), jnp.int32)
        valid[k] = jnp.zeros((rows, LANES), F32)
    for k in range(8):
        pltpu.make_async_copy(codes.at[k], codes_out.at[:, k, :], out_sem).start()
        pltpu.make_async_copy(valid.at[k], valid_out.at[:, k, :], out_sem).start()

    half_bias = 0.5 * b_ei

    def project(i, _):
        high, low = halves(
            jnp.concatenate([state[1 + 4 * i + u] for u in range(4)], axis=1)
        )
        both = mxu(a_state, jnp.concatenate([high, low, high], axis=0))
        for u in range(4):
            s = slice(u * LANES, (u + 1) * LANES)
            projected[1 + 4 * i + u] = both[:D, s]
            receiver[4 * i + u] = both[D:, s] + half_bias

    lax.fori_loop(0, rows // 4, project, None)
    pltpu.make_async_copy(projected.at[inner], project_out.at[inner], out_sem).start()
    pltpu.make_async_copy(receiver, receive_out, out_sem).start()

    for copy in copies:
        copy.wait()
    state[rows + 1] = rows_in[0]
    state[0] = rows_in[1]
    from_east = unpack_column(cols_in[0])
    from_west = unpack_column(cols_in[1])
    cols[1] = (
        pltpu.roll(jnp.where((lane >= 1) & (lane <= rows), from_east, 0.0), LANES - 1, 1)
        + corner_at(corners_in.at[0], 0, rows)
        + corner_at(corners_in.at[2], 2, LANES - 1)
    )
    cols[0] = (
        pltpu.roll(jnp.where(lane < rows, from_west, 0.0), 1, 1)
        + corner_at(corners_in.at[1], 1, rows + 1)
        + corner_at(corners_in.at[3], 3, 0)
    )
    high, low = halves(
        jnp.concatenate([rows_in[1], rows_in[0], cols[0], cols[1]], axis=1)
    )
    rim = mxu(a_state[:D], jnp.concatenate([high, low, high], axis=0))
    projected[0] = rim[:, :LANES]
    projected[rows + 1] = rim[:, LANES : 2 * LANES]
    sides[0] = rim[:, 2 * LANES : 3 * LANES]
    sides[1] = rim[:, 3 * LANES :]
    for t in (0, rows + 1):
        pltpu.make_async_copy(projected.at[t], project_out.at[t], out_sem).start()
        pltpu.make_async_copy(state.at[t], state_out.at[t], out_sem).start()
    pltpu.make_async_copy(sides, sides_out, out_sem).start()
    pltpu.make_async_copy(cols, cols_out, out_sem).start()
    for ref in (pack, columns, codes, valid, receiver, state, projected, cols, sides):
        waits(ref, out_sem)


def start_call(n_blk, n_lon, counts, kl_weight, nodes, mean, logstd, noise, neighbors, mask, weights):
    rows = nodes.shape[1]
    tile = (D, LANES)
    shapes = (
        ((rows + 2, *tile), F32),
        ((2, *tile), F32),
        ((rows + 2, *tile), F32),
        ((rows, *tile), F32),
        ((2, *tile), F32),
        ((rows, 8, LANES), jnp.int32),
        ((rows, 8, LANES), F32),
        ((P_ROWS, P_LANES), BF16),
        ((C_TILES, *tile), F32),
    )
    vmem = lambda *dims: pltpu.VMEM(dims, F32)
    ints = lambda *dims: pltpu.VMEM(dims, jnp.int32)
    dma = pltpu.SemaphoreType.DMA
    return pl.pallas_call(
        functools.partial(start_kernel, n_blk, n_lon),
        name="start",
        out_shape=[jax.ShapeDtypeStruct(*shape) for shape in shapes],
        in_specs=[SMEM, SMEM] + [HBM] * (6 + len(weights)),
        out_specs=[HBM] * len(shapes),
        scratch_shapes=[
            vmem(rows // 8, 4, D, 8, LANES),
            vmem(rows + 2, *tile),
            vmem(rows + 2, *tile),
            vmem(rows, *tile),
            vmem(2, *tile),
            ints(NBR, rows, LANES),
            ints(NBR, rows, LANES),
            ints(8, rows, LANES),
            vmem(8, rows, LANES),
            vmem(D, 3 * D),
            vmem(D, D),
            vmem(D, 2 * D),
            vmem(D, D),
            vmem(8, 1, D),
            pltpu.VMEM((P_ROWS, P_LANES), BF16),
            vmem(C_TILES, *tile),
            vmem(2, *tile),
            vmem(2, *tile),
            vmem(2, D // 2, LANES),
            vmem(8, LANES),
            vmem(2, *tile),
            vmem(2, D // 2, LANES),
            vmem(4, 8, LANES),
            dma((rows // 8,)),
            dma,
            dma,
            dma((8,)),
            dma((8,)),
            dma,
        ],
        compiler_params=pltpu.CompilerParams(
            collective_id=0, has_side_effects=True, vmem_limit_bytes=ROOM
        ),
    )(counts, kl_weight, nodes, mean, logstd, noise, neighbors, mask, *weights)


def layer_kernel(
    edges,
    cotangent,
    project_in,
    receive_in,
    sides_in,
    codes_in,
    valid_in,
    pack_in,
    columns_in,
    state_in,
    new_states,
    grad_edges,
    part_out,
    recv_out,
    own_out,
    cells_out,
    acc_out,
    slope,
    xs,
    hs,
    cb,
    db,
    staged,
    windows,
    projected,
    receiver,
    sides,
    codes,
    valid,
    pack,
    columns,
    state,
    inverse,
    summed,
    qc_ref,
    qo_ref,
    cot,
    fresh,
    placed,
    cells,
    gather_grads,
    acc_edge,
    acc_hidden,
    acc_nin,
    acc_nout,
    acc_vec,
    acc,
    row_sem,
    edge_sem,
    in_sem,
    out_sem,
):
    rows = cotangent.shape[1]
    wide = NBR * LANES
    two = 2 * LANES
    part, grad_recv, own = receiver, summed, projected
    lane = lane_ids()

    halfway = 10

    def load_edges(r):
        for k in range(NBR):
            pltpu.make_async_copy(
                edges.at[:, k, r, :],
                staged.at[r, :, pl.ds(k * LANES, LANES)],
                edge_sem.at[r],
            ).start()

    first_weights = pl.ds(P_HIDDEN[0], P_EDGE[1])
    first_small = (
        (sides_in, sides),
        (pack_in.at[first_weights], pack.at[first_weights]),
        (codes_in, codes),
        (valid_in, valid),
    )
    parts = []
    for g, (first, last) in enumerate(((0, halfway), (halfway, rows + 2))):
        send, receive = pl.ds(first, last - first), pl.ds(first, min(last, rows) - first)
        part_g = ((project_in, projected, send), (receive_in, receiver, receive))
        for source, target, span in part_g:
            pltpu.make_async_copy(source.at[span], target.at[span], row_sem.at[g]).start()
        parts.append([target.at[span] for _, target, span in part_g])
        if g == 0:
            for source, target in first_small[:2]:
                pltpu.make_async_copy(source, target, in_sem.at[0]).start()
            for r in range(4):
                load_edges(r)
            for source, target in first_small[2:]:
                pltpu.make_async_copy(source, target, in_sem.at[0]).start()
    lax.fori_loop(4, 12, lambda r, _: load_edges(r), None)

    def load_rest():
        rest = pl.ds(P_EDGE[1], P_ROWS - P_EDGE[1])
        pltpu.make_async_copy(pack_in.at[rest], pack.at[rest], in_sem.at[1]).start()
        pltpu.make_async_copy(columns_in, columns, in_sem.at[1]).start()
        pltpu.make_async_copy(state_in, state, in_sem.at[1]).start()

        for g in range(rows // 8):
            pltpu.make_async_copy(
                cotangent.at[:, pl.ds(8 * g, 8), :], cot.at[g], in_sem.at[1]
            ).start()
        lax.fori_loop(12, rows, lambda r, _: load_edges(r), None)
        return (cot, state, columns, pack.at[rest])

    ones16 = jnp.where(
        lax.broadcasted_iota(jnp.int32, (16, wide), 0) < 2, 1.0, 0.0
    ).astype(BF16)
    ones_two = ones16[:, :two]
    for _, target in first_small:
        waits(target, in_sem.at[0])

    def shift(t):
        centre = projected[t]
        mix = pltpu.roll(
            jnp.where(lane == t, sides[0], sides[1]), lax.rem(LANES - t, LANES), 1
        )
        windows[t, 1] = centre
        windows[t, 0] = jnp.where(lane == 0, mix, pltpu.roll(centre, 1, 1))
        windows[t, 2] = jnp.where(lane == LANES - 1, mix, pltpu.roll(centre, LANES - 1, 1))

    def edge_product(r, pair):
        own = receiver[r]
        s = pl.ds(pair * two, two)
        high, low = halves(staged[r, :, s])
        xs[r, :D, s] = high
        xs[r, D:, s] = low
        out = mxu(packed_rows(pack, P_EDGE), jnp.concatenate([high, low, high], axis=0))
        slope[r, :, s] = out + jnp.concatenate([own, own], axis=1)

    def hidden_values(r, pair):
        slots = (2 * pair, 2 * pair + 1)
        hidden = {k: [None] * 8 for k in slots}
        masks = {}
        for k in slots:
            code = jnp.broadcast_to(codes[r, pl.ds(k, 1), :], (8, LANES))
            masks[k] = ((code & 1) != 0, (code & 2) != 0, (code & 4) != 0)
        for f in range(8):
            rows_f = pl.ds(8 * f, 8)
            w = [windows[r + 1 + dr, 1 + dc, rows_f, :] for dr, dc in WINDOWS]
            for k in slots:
                s = pl.ds(k * LANES, LANES)
                b0, b1, b2 = masks[k]
                low = jnp.where(b1, jnp.where(b0, w[3], w[2]), jnp.where(b0, w[1], w[0]))
                top = jnp.where(b1, jnp.where(b0, w[7], w[6]), jnp.where(b0, w[5], w[4]))
                pre = slope[r, rows_f, s] + jnp.where(b2, top, low)
                t = jnp.tanh(pre)
                u = 1.0 + t
                h = pre * u
                slope[r, rows_f, s] = u + h * (1.0 - t)
                hidden[k][f] = h
        s = pl.ds(pair * two, two)
        high, low = halves(
            jnp.concatenate([jnp.concatenate(hidden[k], axis=0) for k in slots], axis=1)
        )
        hs[r, :D, s] = high
        hs[r, D : 2 * D, s] = low
        hs[r, 2 * D :, s] = ones_two

    def hidden_product(r, pair):
        s = pl.ds(pair * two, two)
        both = mxu(
            packed_rows(pack, P_HIDDEN, 3 * D + 16),
            jnp.concatenate([hs[r, :, s], hs[r, :D, s]], axis=0),
        )
        cb[r, :, s] = both[:D]
        db[r, :, s] = both[D:]
        return r, pair, both[:D]

    def norm(r, pair, pair_c, total):
        for j in range(2):
            k = 2 * pair + j
            c = pair_c[:, j * LANES : (j + 1) * LANES]
            variance = jnp.sum(c * c, axis=0, keepdims=True) * (1.0 / D)
            inv = lax.rsqrt(variance + EPS)
            inverse[r, pl.ds(k, 1), :] = inv
            term = (inv * valid[r, pl.ds(k, 1), :]) * c
            total = term if total is None else total + term
        if pair == NBR // 2 - 1:
            summed[r] = total
            total = None
        return total

    def forward(i, _, first=0, last=2):
        turn = [4 * i + u for u in range(4)]
        if first == 0:
            for r in turn:
                waits(staged.at[r + 4], edge_sem.at[r + 4])
            for r in turn:
                shift(r + 6)
        units = [(r, pair) for r in turn for pair in range(NBR // 2)]
        products = []
        total = None
        if last >= 2:
            products.append(hidden_product(units[0][0] - 4, units[0][1]))
        for i_unit, (r, pair) in enumerate(units):
            if last >= 2 and i_unit + 1 < len(units):
                ahead_r, ahead_pair = units[i_unit + 1]
                products.append(hidden_product(ahead_r - 4, ahead_pair))
            if first <= 1 <= last:
                if pair == 0:
                    placed[r + 2] = jnp.zeros((3, D, LANES), F32)
                hidden_values(r, pair)
            if last >= 2:
                total = norm(*products[i_unit], total)
            if first == 0:
                edge_product(r + 4, pair)

    for ref in parts[0]:
        waits(ref, row_sem.at[0])
    for t in range(6):
        shift(t)
    for r in range(2):
        placed[r] = jnp.zeros((3, D, LANES), F32)
    for r in range(4):
        waits(staged.at[r], edge_sem.at[r])
        for pair in range(NBR // 2):
            edge_product(r, pair)
    node_inputs = load_rest()
    forward(0, None, last=1)
    for ref in parts[1]:
        waits(ref, row_sem.at[1])
    turns = rows // 4
    lax.fori_loop(1, turns - 1, forward, None)
    forward(turns - 1, None, first=1)
    forward(turns, None, first=2)

    for ref in (acc_edge, acc_hidden, acc_nin, acc_nout, acc_vec):
        ref[...] = jnp.zeros_like(ref)
    for ref in node_inputs:
        waits(ref, in_sem.at[1])
    chunk = 4
    span = chunk * LANES

    def node_chunk(first):
        tile_cols = lambda i: jnp.concatenate([columns[i]] * chunk, axis=1)
        spread = lambda ref, offset: jnp.concatenate(
            [ref[first + offset + j] for j in range(chunk)], axis=1
        )
        degree = jnp.concatenate(
            [jnp.sum(valid[first + j], axis=0, keepdims=True) for j in range(chunk)], axis=1
        )
        st_high, st_low = halves(spread(state, 1))
        sum_high, sum_low = halves(spread(summed, 0))
        place = lax.broadcasted_iota(jnp.int32, (16, span), 0)
        extra = jnp.where(place < 2, 1.0, jnp.where(place < 4, degree, 0.0)).astype(BF16)
        tops = jnp.concatenate([st_high, sum_high], axis=0)
        ends = jnp.concatenate([st_low, sum_low], axis=0)
        pre = mxu(
            jnp.concatenate(
                [
                    packed_rows(pack, P_NODE_IN, P_LANES),
                    packed_rows(pack, P_NODE_IN_END, 6 * D + 16 - P_LANES),
                ],
                axis=1,
            ),
            jnp.concatenate([tops, ends, extra, tops], axis=0),
        )
        yield
        t = jnp.tanh(pre)
        u = 1.0 + t
        h = pre * u
        slope_n = u + h * (1.0 - t)
        h_high, h_low = halves(h)
        h_all = jnp.concatenate([h_high, h_low, ones16[:, :span]], axis=0)
        c = mxu(
            packed_rows(pack, P_NODE_OUT, 3 * D + 16),
            jnp.concatenate([h_all, h_high], axis=0),
        )
        yield
        cot_c = jnp.concatenate(
            [read_row(cot.at[(first + j) // 8], (first + j) % 8) for j in range(chunk)], axis=1
        )
        inv = lax.rsqrt(jnp.sum(c * c, axis=0, keepdims=True) * (1.0 / D) + EPS)
        n = c * inv
        new = spread(state, 1) + (tile_cols(C_GAIN_N) * n + tile_cols(C_SHIFT_N))
        q = cot_c * tile_cols(C_GAIN_N)
        q = q - jnp.sum(q, axis=0, keepdims=True) * (1.0 / D)
        grad = inv * (q - n * (jnp.sum(q * n, axis=0, keepdims=True) * (1.0 / D)))
        g_high, g_low = halves(grad)
        pre_grad = mxu(
            packed_rows(pack, P_NODE_OUT_T), jnp.concatenate([g_high, g_low, g_high], axis=0)
        )
        for j in range(chunk):
            s = slice(j * LANES, (j + 1) * LANES)
            write_row(fresh.at[(first + j) // 8], (first + j) % 8, new[:, s])
            acc_vec[0] += cot_c[:, s] * n[:, s]
            acc_vec[1] += cot_c[:, s]
        yield
        acc_nout[...] += outer(jnp.concatenate([g_high, g_low], axis=0), h_all)
        pre_grad = pre_grad * slope_n
        p_high, p_low = halves(pre_grad)
        back = mxu(
            packed_rows(pack, P_NODE_IN_T), jnp.concatenate([p_high, p_low, p_high], axis=0)
        )
        for j in range(chunk):
            s = slice(j * LANES, (j + 1) * LANES)
            acc_vec[2] += pre_grad[:, s]
            acc_vec[3] += pre_grad[:, s] * degree[:, s]
        yield
        acc_nin[...] += outer(
            jnp.concatenate([p_high, p_low], axis=0), jnp.concatenate([tops, ends], axis=0)
        )
        for j in range(chunk):
            s = slice(j * LANES, (j + 1) * LANES)
            part[first + j] = cot_c[:, s] + back[:D, s]
            qc_ref[first + j] = back[D : 2 * D, s]
            qo_ref[first + j] = back[2 * D :, s]

    in_flight = []
    for first in range(0, rows + 4 * chunk, chunk):
        if first < rows:
            in_flight.append(node_chunk(first))
        for routine in list(in_flight):
            if next(routine, routine) is routine:
                in_flight.remove(routine)

    for g in range(rows // 8):
        pltpu.make_async_copy(
            fresh.at[g], new_states.at[:, pl.ds(8 * g, 8), :], out_sem
        ).start()
    pltpu.make_async_copy(part, part_out, out_sem).start()

    def grad_unit(r, pair, u, received):
        qc = qc_ref[r]
        qo = qo_ref[r]
        hidden_grads, grads = [], []
        for k in (2 * pair, 2 * pair + 1):
            s = pl.ds(k * LANES, LANES)
            c = cb[r, :, s]
            inv = inverse[r, pl.ds(k, 1), :]
            alpha = inv * valid[r, pl.ds(k, 1), :]
            moment = jnp.sum(qc * c, axis=0, keepdims=True) * (1.0 / D)
            beta = alpha * inv * inv * moment
            hidden_grads.append(alpha * qc - beta * c)
            grad = (alpha * qo - beta * db[r, :, s]) * slope[r, :, s]
            grads.append(grad)
            received = grad if received is None else received + grad
        high, low = halves(jnp.concatenate(hidden_grads, axis=1))
        s = pl.ds(pair * two, two)
        gather_grads[u, :D, s] = high
        gather_grads[u, D : 2 * D, s] = low
        high, low = halves(jnp.concatenate(grads, axis=1))
        gather_grads[u, 2 * D : 3 * D, s] = high
        gather_grads[u, 3 * D :, s] = low
        ge = mxu(
            packed_rows(pack, P_EDGE_T), jnp.concatenate([high, low, high], axis=0)
        )
        return grads, received, ge

    def place_unit(r, pair, grads):
        code = [
            jnp.broadcast_to(codes[r, pl.ds(k, 1), :], (8, LANES))
            for k in (2 * pair, 2 * pair + 1)
        ]
        for which, (dr, dc) in enumerate(WINDOWS):
            masks = [c == which for c in code]
            for f in range(8):
                rows_f = pl.ds(8 * f, 8)
                value = placed[r + 1 + dr, 1 + dc, rows_f, :]
                for j in range(2):
                    value += jnp.where(masks[j], grads[j][8 * f : 8 * f + 8], 0.0)
                placed[r + 1 + dr, 1 + dc, rows_f, :] = value

    def store_unit(r, pair, ge):
        staged[r, :, pl.ds(pair * two, two)] = ge

    def products(r, u):
        r = jnp.maximum(r, 0)
        acc_hidden[...] += outer(gather_grads[u, : 2 * D], hs[r])
        acc_edge[...] += outer(gather_grads[u, 2 * D :], xs[r])

    def settle(t):
        to_west = placed[t, 0]
        to_east = placed[t, 2]
        own[t] = (
            placed[t, 1]
            + jnp.where(lane == 0, 0.0, pltpu.roll(to_east, 1, 1))
            + jnp.where(lane == LANES - 1, 0.0, pltpu.roll(to_west, LANES - 1, 1))
        )
        mix = pltpu.roll(jnp.where(lane == 0, to_west, to_east), t, 1)
        cells[0] = jnp.where(lane == t, mix, cells[0])
        cells[1] = jnp.where(lane == lax.rem(t + LANES - 1, LANES), mix, cells[1])

    def send_rows(i, unroll=4):
        span = pl.ds(unroll * i, unroll)
        pltpu.make_async_copy(grad_recv.at[span], recv_out.at[span], out_sem).start()
        for u in range(unroll):
            r = unroll * i + u
            for k in range(NBR):
                pltpu.make_async_copy(
                    staged.at[r, :, pl.ds(k * LANES, LANES)],
                    grad_edges.at[:, k, r, :],
                    out_sem,
                ).start()

    def backward(i, _, unroll=4):
        if not isinstance(i, int):
            send_rows(i - 1)
            for u in range(unroll):
                settle(unroll * (i - 1) + u)
        pending = None
        for u in range(unroll):
            r = unroll * i + u
            products(r - unroll, u)
            received = None
            for pair in range(NBR // 2):
                grads, received, ge = grad_unit(r, pair, u, received)
                place_unit(r, pair, grads)
                if pending is not None:
                    store_unit(*pending)
                pending = (r, pair, ge)
            grad_recv[r] = received
        store_unit(*pending)
        if not isinstance(i, int):
            span = pl.ds(unroll * (i - 1), unroll)
            pltpu.make_async_copy(own.at[span], own_out.at[span], out_sem).start()

    cells[...] = jnp.zeros_like(cells)
    gather_grads[...] = jnp.zeros_like(gather_grads)
    backward(0, None)
    lax.fori_loop(1, rows // 4, backward, None)
    send_rows(rows // 4 - 1)
    for u in range(4):
        products(rows - 4 + u, u)
    for t in range(rows - 4, rows + 2):
        settle(t)
    tail = pl.ds(rows - 4, 6)
    pltpu.make_async_copy(own.at[tail], own_out.at[tail], out_sem).start()
    pltpu.make_async_copy(cells, cells_out, out_sem).start()

    def folded(ref):
        half = ref[:D, : 2 * D] + ref[D:, : 2 * D]
        return half + pltpu.roll(half, D, 1)

    left = lane < D
    acc[0] = folded(acc_edge)
    plain = (
        acc_nin[:D, : 2 * D]
        + acc_nin[D:, : 2 * D]
        + acc_nin[:D, 2 * D :]
        + acc_nin[D:, 2 * D :]
    )
    pick = lambda ref, start, i: jnp.sum(
        jnp.where(lane[:, :16] == i, ref[:D, start:] + ref[D:, start:], 0.0),
        axis=1,
        keepdims=True,
    )
    lane_sum = lambda i: jnp.sum(acc_vec[i], axis=1, keepdims=True)
    by_degree = lane_sum(3)
    acc[2] = plain * columns[C_ROWS, 0:1, :] + by_degree * columns[C_ROWS, 1:2, :]
    acc[3] = jnp.where(left, folded(acc_hidden), folded(acc_nout))
    weight_n = columns[C_WEIGHT_N]
    gain_row = jnp.sum(weight_n * plain, axis=0, keepdims=True)[:, D:]
    shift_row = jnp.sum(weight_n * by_degree, axis=0, keepdims=True)[:, D:]
    block = jnp.zeros((D, LANES), F32)
    for i, vector in (
        (1, pick(acc_hidden, 2 * D, 0)),
        (2, to_column(gain_row)),
        (3, to_column(shift_row)),
        (4, lane_sum(2)),
        (5, pick(acc_nout, 2 * D, 0)),
        (6, lane_sum(0)),
        (7, lane_sum(1)),
        (8, columns[C_DIVERGED]),
    ):
        block = jnp.where(lane == D + i, vector, block)
    acc[1] = block
    pltpu.make_async_copy(acc, acc_out, out_sem).start()
    for ref in (fresh, part, grad_recv, own.at[pl.ds(0, rows + 2)], cells, staged, acc):
        waits(ref, out_sem)


def layer_call(edges, cotangent, projected, receiver, sides, codes, valid, pack, columns, state):
    rows = cotangent.shape[1]
    wide = NBR * LANES
    tile = (D, LANES)
    shape = lambda *dims: jax.ShapeDtypeStruct(dims, F32)
    vmem = lambda *dims: pltpu.VMEM(dims, F32)
    return pl.pallas_call(
        layer_kernel,
        name="layer",
        out_shape=(
            shape(D, rows, LANES),
            shape(D, NBR, rows, LANES),
            shape(rows, *tile),
            shape(rows, *tile),
            shape(rows + 2, *tile),
            shape(2, *tile),
            shape(4, *tile),
        ),
        in_specs=[HBM] * 10,
        out_specs=[HBM] * 7,
        scratch_shapes=[
            vmem(rows, D, wide),
            pltpu.VMEM((rows, 2 * D, wide), BF16),
            pltpu.VMEM((rows, 2 * D + 16, wide), BF16),
            vmem(rows, D, wide),
            vmem(rows, D, wide),
            vmem(rows, D, wide),
            vmem(rows + 6, 3, *tile),
            vmem(rows + 6, *tile),
            vmem(rows, *tile),
            vmem(2, *tile),
            pltpu.VMEM((rows, 8, LANES), jnp.int32),
            vmem(rows, 8, LANES),
            pltpu.VMEM((P_ROWS, P_LANES), BF16),
            vmem(C_TILES, *tile),
            vmem(rows + 2, *tile),
            vmem(rows, 8, LANES),
            vmem(rows, *tile),
            vmem(rows, *tile),
            vmem(rows, *tile),
            vmem(rows // 8, D, 8, LANES),
            vmem(rows // 8, D, 8, LANES),
            vmem(rows + 2, 3, *tile),
            vmem(2, *tile),
            pltpu.VMEM((4, 4 * D, wide), BF16),
            vmem(2 * D, 2 * D),
            vmem(2 * D, 2 * D + 16),
            vmem(2 * D, 4 * D),
            vmem(2 * D, 2 * D + 16),
            vmem(4, *tile),
            vmem(4, *tile),
            pltpu.SemaphoreType.DMA((2,)),
            pltpu.SemaphoreType.DMA((rows,)),
            pltpu.SemaphoreType.DMA((2,)),
            pltpu.SemaphoreType.DMA,
        ],
        compiler_params=pltpu.CompilerParams(vmem_limit_bytes=ROOM),
    )(edges, cotangent, projected, receiver, sides, codes, valid, pack, columns, state)


def sum_kernel(
    n_blk,
    n_lon,
    acc_in,
    own_in,
    cells_in,
    recv_in,
    part_in,
    state_in,
    cols_all,
    pack_in,
    columns_in,
    mean,
    logstd,
    noise,
    nodes_out,
    mean_out,
    logstd_out,
    total_out,
    acc,
    own,
    cells,
    grad_recv,
    part,
    natural,
    mean_v,
    logstd_v,
    noise_v,
    inside,
    state,
    cols,
    pack,
    edge_rows,
    edge_cols,
    edge_corners,
    rows_in,
    cols_in,
    corners_in,
    acc_send,
    acc_recv,
    packed,
    scattered,
    across,
    gathered,
    in_sem,
    row_sem,
    rs_send,
    rs_recv,
    x_send,
    x_recv,
    ag_send,
    ag_recv,
    halo_send,
    halo_recv,
    latent_sem,
    out_sem,
):
    rows = recv_in.shape[0]
    blk, lon, around = neighbours(n_blk, n_lon)
    size = scattered.shape[0]
    n_groups = across.shape[0]
    per = size // n_lon
    me = lax.rem(blk, per) * n_lon + lon
    own_group = blk // per
    lane = lane_ids()

    def member(index):
        if n_lon & (n_lon - 1):
            return (own_group * per + index // n_lon, lax.rem(index, n_lon))
        return (own_group * per + (index >> (n_lon.bit_length() - 1)), index & (n_lon - 1))

    def other(step):
        if size & (size - 1):
            return lax.rem(me + step, size)
        return (me + step) & (size - 1)

    def peer(step):
        return (lax.rem(own_group + step, n_groups) * per + lax.rem(blk, per), lon)

    half = rows // 2
    for h in range(2):
        span = pl.ds(h * half, half)
        span3 = pl.ds(0, half + 1) if h == 0 else pl.ds(half + 1, half + 1)
        for source, target in (
            (own_in.at[span3], own.at[span3]),
            (state_in.at[span3], state.at[span3]),
            (recv_in.at[span], grad_recv.at[span]),
        ):
            pltpu.make_async_copy(source, target, row_sem.at[h]).start()
    small = (
        (pack_in.at[pl.ds(P_SEND_T[0], 2 * D)], pack),
        (cols_all, cols),
        (acc_in, acc),
        (part_in, part),
        (cells_in, cells),
        (columns_in.at[C_VALID], inside),
    )
    for i, (source, target) in enumerate(small):
        pltpu.make_async_copy(source, target, in_sem.at[i]).start()

    groups = [pl.ds(8 * g, 8) for g in range(rows // 8)]
    latent = ((mean, mean_v), (logstd, logstd_v), (noise, noise_v))
    barrier = pltpu.get_barrier_semaphore()

    def greet(step, _):
        pl.semaphore_signal(
            barrier, inc=1, device_id=member(other(step)), device_id_type=MESH
        )

    lax.fori_loop(1, size, greet, None)
    expected = size - 1
    if n_groups > 1:
        for place in around:
            pl.semaphore_signal(barrier, inc=1, device_id=place, device_id_type=MESH)

        def greet_group(step, _):
            pl.semaphore_signal(barrier, inc=1, device_id=peer(step), device_id_type=MESH)

        lax.fori_loop(1, n_groups, greet_group, None)
        expected += 8 + n_groups - 1

    acc_send[...] = jnp.zeros_like(acc_send)
    acc_recv[...] = jnp.zeros_like(acc_recv)

    def both_halves(value):
        return jnp.concatenate(halves(value), axis=0)

    ones_row = jnp.where(
        lax.broadcasted_iota(jnp.int32, (16, 4 * LANES), 0) < 1, 1.0, 0.0
    ).astype(BF16)

    def collect(i, _):
        wide = lambda ref, first: both_halves(
            jnp.concatenate([ref[first + u] for u in range(4)], axis=1)
        )
        there = wide(state, 1 + 4 * i)
        acc_send[...] += outer(wide(own, 1 + 4 * i), there)
        acc_recv[...] += outer(
            wide(grad_recv, 4 * i), jnp.concatenate([there, ones_row], axis=0)
        )

    for h in range(2):
        waits(own.at[pl.ds(h * (half + 1), half + 1)], row_sem.at[h])
        waits(state.at[pl.ds(h * (half + 1), half + 1)], row_sem.at[h])
        waits(grad_recv.at[pl.ds(h * half, half)], row_sem.at[h])
        lax.fori_loop(h * half // 4, (h + 1) * half // 4, collect, None)
    waits(cells, in_sem.at[4])
    waits(cols, in_sem.at[1])
    edge_values = jnp.concatenate([own[0], own[rows + 1], cells[0], cells[1]], axis=1)
    edge_states = jnp.concatenate([state[0], state[rows + 1], cols[0], cols[1]], axis=1)
    acc_send[...] += outer(both_halves(edge_values), both_halves(edge_states))

    def folded(ref):
        part_sum = ref[:D, : 2 * D] + ref[D:, : 2 * D]
        return part_sum + pltpu.roll(part_sum, D, 1)

    left = lane < D
    waits(acc, in_sem.at[2])
    ones_sum = jnp.sum(
        jnp.where(lane[:, :16] == 0, acc_recv[:D, 2 * D :] + acc_recv[D:, 2 * D :], 0.0),
        axis=1,
        keepdims=True,
    )
    columns_t = jnp.where(lane == D, ones_sum, acc[1]).T[D:]
    vector_rows = jnp.concatenate([jnp.zeros((D, D), F32), columns_t], axis=1)
    chunk = packed.shape[1]
    blocks = (
        jnp.where(left, acc[0], folded(acc_send)),
        jnp.where(left, folded(acc_recv), vector_rows),
        acc[2],
        acc[3],
    )
    per_block = D // chunk
    for i, block in enumerate(blocks):
        for j in range(per_block):
            packed[i * per_block + j] = block[j * chunk : (j + 1) * chunk]
    for g, span in enumerate(groups):
        for source, target in latent:
            pltpu.make_async_copy(source.at[:, span, :], target.at[g], latent_sem).start()

    pl.semaphore_wait(barrier, expected)

    def scatter(step, _):
        target = other(step)
        pltpu.make_async_remote_copy(
            src_ref=packed.at[target],
            dst_ref=scattered.at[me],
            send_sem=rs_send,
            recv_sem=rs_recv,
            device_id=member(target),
            device_id_type=MESH,
        ).start()

    lax.fori_loop(1, size, scatter, None)
    scattered[me] = packed[me]

    waits(pack, in_sem.at[0])
    a_send = pack[:D, : 3 * D]
    a_recv = pack[D : 2 * D, : 3 * D]
    high, low = halves(edge_values)
    edge_grads = mxu(a_send, jnp.concatenate([high, low, high], axis=0))
    edge_grad = [edge_grads[:, i * LANES : (i + 1) * LANES] for i in range(4)]
    edge_rows[0], edge_rows[1] = edge_grad[0], edge_grad[1]
    west_cells, east_cells = edge_grad[2], edge_grad[3]
    edge_cols[0], edge_cols[1] = pack_column(west_cells), pack_column(east_cells)
    edge_corners[...] = corner_rows(
        [
            west_cells[:, :1],
            east_cells[:, LANES - 1 :],
            west_cells[:, rows + 1 : rows + 2],
            east_cells[:, rows : rows + 1],
        ]
    )
    copies = rim_copies(
        around,
        edge_rows,
        edge_cols,
        edge_corners,
        rows_in,
        cols_in,
        corners_in,
        halo_send,
        halo_recv,
    )
    for copy in copies:
        copy.start()
    waits(part, in_sem.at[3])

    def finish(i, _):
        for u in range(2):
            first = 4 * i + 2 * u
            grads = None
            for weights, ref, offset in ((a_send, own, 1), (a_recv, grad_recv, 0)):
                high, low = halves(
                    jnp.concatenate([ref[first + offset], ref[first + offset + 1]], axis=1)
                )
                product = mxu(weights, jnp.concatenate([high, low, high], axis=0))
                grads = product if grads is None else grads + product
            for j in range(2):
                part[first + j] += grads[:, j * LANES : (j + 1) * LANES]

    lax.fori_loop(0, rows // 4, finish, None)

    waits(inside, in_sem.at[5])
    for _, target in latent:
        waits(target, latent_sem)
    weight = inside[0:1, :].reshape(1, 1, LANES)

    def blocks(i):
        return i // 8, pl.ds(8 * (i % 8), 8)

    def latent_terms(i, _):
        at = blocks(i)
        spread = jnp.exp(logstd_v[at])
        mean_v[at] = weight * mean_v[at]
        noise_v[at] = spread * noise_v[at]
        logstd_v[at] = weight * (spread * spread - 1.0)

    lax.fori_loop(0, rows, latent_terms, None)

    others = pl.ds(0, size - 1)
    waits(scattered.at[others], rs_recv)
    mine = scattered[0]
    for i in range(1, size):
        mine = mine + scattered[i]
    if n_groups > 1:
        across[own_group] = mine

        def cross(step, _):
            pltpu.make_async_remote_copy(
                src_ref=across.at[own_group],
                dst_ref=across.at[own_group],
                send_sem=x_send,
                recv_sem=x_recv,
                device_id=peer(step),
                device_id_type=MESH,
            ).start()

        lax.fori_loop(1, n_groups, cross, None)
        rest = pl.ds(0, n_groups - 1)
        waits(across.at[rest], x_recv)
        waits(across.at[rest], x_send)
        mine = across[0]
        for i in range(1, n_groups):
            mine = mine + across[i]
    gathered[me] = mine

    def gather(step, _):
        pltpu.make_async_remote_copy(
            src_ref=gathered.at[me],
            dst_ref=gathered.at[me],
            send_sem=ag_send,
            recv_sem=ag_recv,
            device_id=member(other(step)),
            device_id_type=MESH,
        ).start()

    lax.fori_loop(1, size, gather, None)
    for copy in copies:
        copy.wait()
    west_in = (
        pltpu.roll(jnp.where(lane < rows, unpack_column(cols_in[1]), 0.0), 1, 1)
        + corner_at(corners_in.at[3], 3, 1)
        + corner_at(corners_in.at[1], 1, rows)
    )
    east_in = unpack_column(cols_in[0])
    east_in = (
        pltpu.roll(jnp.where((lane >= 1) & (lane <= rows), east_in, 0.0), LANES - 1, 1)
        + corner_at(corners_in.at[2], 2, 0)
        + corner_at(corners_in.at[0], 0, rows - 1)
    )
    rim = (lane == 0) | (lane == LANES - 1)
    part[0] += rows_in[1]
    part[rows - 1] += rows_in[0]

    def add_columns(i, _):
        for u in range(4):
            r = 4 * i + u
            mix = pltpu.roll(
                jnp.where(lane == r + 1, west_in, east_in), LANES - 1 - r, 1
            )
            write_row(natural.at[r // 8], lax.rem(r, 8), part[r] + jnp.where(rim, mix, 0.0))

    lax.fori_loop(0, rows // 4, add_columns, None)

    def latent_grads(i, _):
        at = blocks(i)
        grad = natural[at]
        mean_v[at] = grad + mean_v[at]
        logstd_v[at] = grad * noise_v[at] + logstd_v[at]

    lax.fori_loop(0, rows, latent_grads, None)
    results = ((natural, nodes_out), (mean_v, mean_out), (logstd_v, logstd_out))
    for g, span in enumerate(groups):
        for source, target in results:
            pltpu.make_async_copy(source.at[g], target.at[:, span, :], out_sem).start()
    waits(gathered.at[others], ag_recv)
    pltpu.make_async_copy(gathered, total_out, out_sem).start()
    waits(scattered.at[others], rs_send)
    waits(gathered.at[others], ag_send)
    for ref in (natural, mean_v, logstd_v, gathered):
        waits(ref, out_sem)


def sum_call(n_blk, n_lon, *operands):
    recv = operands[3]
    rows = recv.shape[0]
    size = min(32, n_blk * n_lon)
    n_groups = n_blk * n_lon // size
    chunk = (4 * D // size, LANES)
    tile = (D, LANES)
    shape = lambda *dims: jax.ShapeDtypeStruct(dims, F32)
    vmem = lambda *dims: pltpu.VMEM(dims, F32)
    dma = pltpu.SemaphoreType.DMA
    return pl.pallas_call(
        functools.partial(sum_kernel, n_blk, n_lon),
        name="sums",
        out_shape=(shape(D, rows, LANES),) * 3 + (shape(size, *chunk),),
        in_specs=[HBM] * 12,
        out_specs=[HBM] * 4,
        scratch_shapes=[
            vmem(4, *tile),
            vmem(rows + 2, *tile),
            vmem(2, *tile),
            vmem(rows, *tile),
            vmem(rows, *tile),
            vmem(rows // 8, D, 8, LANES),
            vmem(rows // 8, D, 8, LANES),
            vmem(rows // 8, D, 8, LANES),
            vmem(rows // 8, D, 8, LANES),
            vmem(*tile),
            vmem(rows + 2, *tile),
            vmem(2, *tile),
            pltpu.VMEM((2 * D, P_LANES), BF16),
            vmem(2, *tile),
            vmem(2, D // 2, LANES),
            vmem(8, LANES),
            vmem(2, *tile),
            vmem(2, D // 2, LANES),
            vmem(4, 8, LANES),
            vmem(2 * D, 2 * D),
            vmem(2 * D, 2 * D + 16),
            vmem(size, *chunk),
            vmem(size, *chunk),
            vmem(n_groups, *chunk),
            vmem(size, *chunk),
            dma((6,)),
            dma((2,)),
            dma,
            dma,
            dma,
            dma,
            dma,
            dma,
            dma((8,)),
            dma((8,)),
            dma,
            dma,
        ],
        compiler_params=pltpu.CompilerParams(
            collective_id=1, has_side_effects=True, vmem_limit_bytes=ROOM
        ),
    )(*operands)


def final_kernel(*refs):
    large_in, (total_in, columns_in), refs = refs[:3], refs[3:5], refs[5:]
    large_outs, small_outs, refs = refs[:3], refs[3:16], refs[16:]
    large, (total, columns), smalls, refs = refs[:3], refs[3:5], refs[5:18], refs[18:]
    in_sem, small_sem, out_sem = refs
    n_chunks = in_sem.shape[0]
    depth = D // n_chunks
    for i, (source, target) in enumerate(((columns_in.at[C_COUNT], columns), (total_in, total))):
        pltpu.make_async_copy(source, target, small_sem.at[i]).start()
    spans = [pl.ds(i * depth, depth) for i in range(n_chunks)]
    for i, span in enumerate(spans):
        for source, target in zip(large_in, large):
            pltpu.make_async_copy(source.at[span], target.at[span], in_sem.at[i]).start()

    def forward_block(i):
        for ref in large:
            waits(ref.at[spans[i]], in_sem.at[i])
        for source, target in zip(large, large_outs):
            pltpu.make_async_copy(source.at[spans[i]], target.at[spans[i]], out_sem).start()

    for i in range(n_chunks):
        forward_block(i)

    waits(columns, small_sem.at[0])
    waits(total, small_sem.at[1])
    kl_value, g_w_ei, g_w_eo, g_w_ni, g_w_no = smalls[:5]
    chunk = total.shape[1]
    per_block = D // chunk
    blocks = [
        jnp.concatenate([total[i * per_block + j] for j in range(per_block)], axis=0)
        for i in range(4)
    ]
    g_w_ei[:, : 2 * D] = blocks[0]
    g_w_ei[:, 2 * D :] = blocks[1][:, :D]
    g_w_ni[...] = blocks[2]
    g_w_eo[...] = blocks[3][:, :D]
    g_w_no[...] = pltpu.roll(blocks[3], D, 1)[:, :D]
    vector_rows = pltpu.roll(blocks[1][:16], D, 1)
    for i in range(8):
        smalls[5 + i][...] = vector_rows[i : i + 1, :D]
    diverged = jnp.sum(vector_rows[8:9, :D], axis=1, keepdims=True)
    kl_value[...] = diverged / columns[0:1, 0:1]
    for source, target in zip(smalls, small_outs):
        pltpu.make_async_copy(source, target, out_sem).start()
    for ref in (*large, *smalls):
        waits(ref, out_sem)


def final_call(*operands):
    shape = lambda *dims: jax.ShapeDtypeStruct(dims, F32)
    vmem = lambda *dims: pltpu.VMEM(dims, F32)
    whole, total = operands[0].shape, operands[3].shape
    small = ((1, 1), (D, 3 * D), (D, D), (D, 2 * D), (D, D)) + ((1, D),) * 8
    return pl.pallas_call(
        final_kernel,
        name="final",
        out_shape=[shape(*dims) for dims in (whole,) * 3 + small],
        in_specs=[HBM] * 5,
        out_specs=[HBM] * 16,
        scratch_shapes=[vmem(*whole) for _ in range(3)]
        + [vmem(*total), vmem(D, LANES)]
        + [vmem(*dims) for dims in small]
        + [
            pltpu.SemaphoreType.DMA((4,)),
            pltpu.SemaphoreType.DMA((2,)),
            pltpu.SemaphoreType.DMA,
        ],
        compiler_params=pltpu.CompilerParams(vmem_limit_bytes=ROOM),
    )(*operands)


def shards(
    nodes,
    edges,
    latent_mean,
    latent_logstd,
    latent_noise,
    kl_weight,
    band_counts,
    neighbors,
    edge_mask,
    w_edge_in,
    b_edge_in,
    w_edge_out,
    b_edge_out,
    edge_gain,
    edge_shift,
    w_node_in,
    b_node_in,
    w_node_out,
    b_node_out,
    node_gain,
    node_shift,
    cotangent,
):
    n_blk = lax.axis_size("blk")
    n_lon = lax.axis_size("lon")
    vectors = (
        b_edge_in,
        b_edge_out,
        edge_gain,
        edge_shift,
        b_node_in,
        b_node_out,
        node_gain,
        node_shift,
    )
    weights = (w_edge_in, w_edge_out, w_node_in, w_node_out)
    weights += tuple(vector.reshape(1, D) for vector in vectors)
    state, cols, projected, receiver, sides, codes, valid, pack, columns = start_call(
        n_blk,
        n_lon,
        band_counts,
        kl_weight,
        nodes,
        latent_mean,
        latent_logstd,
        latent_noise,
        neighbors,
        edge_mask,
        weights,
    )
    new_states, grad_edges, part, recv, own, cells, acc = layer_call(
        edges, cotangent, projected, receiver, sides, codes, valid, pack, columns, state
    )
    grads = sum_call(
        n_blk,
        n_lon,
        acc,
        own,
        cells,
        recv,
        part,
        state,
        cols,
        pack,
        columns,
        latent_mean,
        latent_logstd,
        latent_noise,
    )
    grad_nodes, grad_mean, grad_logstd, kl_value, g_w_ei, g_w_eo, g_w_ni, g_w_no, *g_vec = (
        final_call(*grads, columns)
    )
    g_vec = [vector.reshape(D) for vector in g_vec]
    return (
        new_states,
        kl_value.reshape(1),
        grad_nodes,
        grad_edges,
        grad_mean,
        grad_logstd,
        g_w_ei,
        g_vec[0],
        g_w_eo,
        g_vec[1],
        g_vec[2],
        g_vec[3],
        g_w_ni,
        g_vec[4],
        g_w_no,
        g_vec[5],
        g_vec[6],
        g_vec[7],
    )


def solution(mesh):
    node = P(None, "blk", "lon")
    slot = P(None, None, "blk", "lon")
    return jax.shard_map(
        shards,
        mesh=mesh,
        in_specs=(
            (node, slot, node, node, node, P(), P(), node, node) + (P(),) * 12 + (node,)
        ),
        out_specs=(node, P(), node, slot, node, node) + (P(),) * 12,
        check_vma=False,
    )
```
